32 devices in a mesh: shard: 4 (over z), ctx: 4 (over x, core), batch: 2 (over y).
Axes of the slice: x: 2, y: 2, z: 4, core: 2. Of those that a mesh axis runs over, the one named last changes fastest.
Arguments:
- tokens: bfloat16 [16, 2048, 1536], P(('shard', 'batch'), 'ctx'), may hold values from -6 to 6
- span_order: int32 [16, 16], P(('shard', 'batch')), may hold values from 0 to 15, as said below
- token_positions: int32 [16, 2048], P(('shard', 'batch'), 'ctx'), may hold values from 0 to 4094, as said below
- attn_gain: bfloat16 [1536], P('shard'), may hold values from 0.099609375 to 1.8984375
- w_query: bfloat16 [1536, 1536], P('shard'), may hold values from -0.15625 to 0.15625
- w_key: bfloat16 [1536, 768], P('shard'), may hold values from -0.15625 to 0.15625
- w_value: bfloat16 [1536, 768], P('shard'), may hold values from -0.15625 to 0.15625
- w_out: bfloat16 [1536, 1536], P('shard'), may hold values from -1.75 to 1.75
- mlp_gain: bfloat16 [1536], P('shard'), may hold values from 0.099609375 to 1.8984375
- w_gate: bfloat16 [1536, 4096], P('shard'), may hold values from -0.15625 to 0.15625
- w_up: bfloat16 [1536, 4096], P('shard'), may hold values from -0.15625 to 0.15625
- w_down: bfloat16 [4096, 1536], P('shard'), may hold values from -0.09375 to 0.09375
- cotangent: bfloat16 [16, 2048, 1536], P(('shard', 'batch'), 'ctx'), may hold values from -6 to 6
Outputs:
- layer_out: bfloat16 [16, 2048, 1536], P(('shard', 'batch'), 'ctx')
- grad_tokens: bfloat16 [16, 2048, 1536], P(('shard', 'batch'), 'ctx')
- grad_attn_gain: float32 [1536], P('shard')
- grad_w_query: float32 [1536, 1536], P('shard')
- grad_w_key: float32 [1536, 768], P('shard')
- grad_w_value: float32 [1536, 768], P('shard')
- grad_w_out: float32 [1536, 1536], P('shard')
- grad_mlp_gain: float32 [1536], P('shard')
- grad_w_gate: float32 [1536, 4096], P('shard')
- grad_w_up: float32 [1536, 4096], P('shard')
- grad_w_down: float32 [4096, 1536], P('shard')
The draws below stay inside these ranges and needn't reach their ends.
Inputs may be any that keep to these rules, and one draw needn't show every extreme that they name: span_order[s] names each of the 16 spans of sequence s once; slots 2 i and 2 i + 1 hold spans c and 15 - c for some c. Taken in true token order, token_positions[s] starts at 0, rises by 1 to 3 from each token to the next, and the last token of every sequence has position 4094.
All inputs are finite; a program needn't handle non-finite values.
Results may differ from the reference program's by a relative error of at most 0.023.
Values may be sent and summed in bfloat16 or wider, within the bound.
No kernel may reach another device: no remote copies, remote signals or barrier semaphores. Data moves between devices by JAX's collectives and lax.ppermute only.
A program may use at most 320 MiB of HBM per device.

```python
import jax
import jax.numpy as jnp
from jax import lax

D = 1536
HEADS = 16
KV_HEADS = 8
HEAD_DIM = 96
FF = 4096
LEN = 2048
SPAN = 128
NCH = 16
SEQS = 16


def permute_one(row_key):
    return jax.random.permutation(row_key, NCH // 2)


def make_order(key):
    row_keys = jax.random.split(jax.random.fold_in(key, 11), SEQS)
    pair_list = jax.vmap(permute_one)(row_keys).astype(jnp.int32)
    flip_bits = jax.random.randint(jax.random.fold_in(key, 12), (SEQS, NCH // 2), 0, 2)
    mirror = NCH - 1 - pair_list
    first_slot = jnp.where(flip_bits == 1, mirror, pair_list)
    second_slot = jnp.where(flip_bits == 1, pair_list, mirror)
    return jnp.stack([first_slot, second_slot], axis=-1).reshape(SEQS, NCH).astype(jnp.int32)


def draw_span_order(key, part):
    span_table = make_order(key)
    return span_table


def draw_token_positions(key, part):
    span_table = make_order(key)
    key = jax.random.fold_in(key, 5)
    base_steps = jax.random.randint(key, (SEQS, LEN // 2), 1, 4).astype(jnp.int32)
    column = jnp.arange(LEN, dtype=jnp.int32)
    pair_index = jnp.clip((column - 1) // 2, 0, LEN // 2 - 1).astype(jnp.int32)
    picked = base_steps[:, pair_index]
    strides = jnp.where(((column - 1) % 2 == 0)[None, :], picked, 4 - picked)
    strides = jnp.where((column == LEN - 1)[None, :], 2, strides)
    strides = jnp.where((column == 0)[None, :], 0, strides).astype(jnp.int32)
    true_positions = jnp.cumsum(strides, axis=1).astype(jnp.int32)
    source = span_table[:, column // SPAN] * SPAN + column[None, :] % SPAN
    return jnp.take_along_axis(true_positions, source.astype(jnp.int32), axis=1).astype(jnp.int32)


def steps_of(own_key, shape, cuts, smallest, high):
    def one(axis_at, blocks):
        steps = jax.random.uniform(jax.random.fold_in(jax.random.fold_in(own_key, 6), axis_at), (blocks,), jnp.float32, smallest / len(cuts), high / len(cuts))
        return jnp.repeat(jnp.exp(steps), shape[axis_at] // blocks).reshape((-1,) + (1,) * (len(shape) - axis_at - 1))

    loudness = one(*cuts[0])
    for cut in cuts[1:]:
        loudness = loudness * one(*cut)
    return loudness


def scatter_about(rng, shape, width, bound, cuts=(), held_as=jnp.bfloat16):
    gain = steps_of(rng, shape, cuts, -0.22, 0.18) if cuts else 1.0
    array = jax.random.normal(rng, shape, jnp.float32) * width * gain
    return jnp.minimum(jnp.maximum(array, -bound), bound).astype(held_as)


def setup_inputs(seed: int = 0) -> dict:
    keys = jax.random.split(jax.random.key(seed), 14)
    tokens = scatter_about(keys[0], (SEQS, LEN, D), 1.0, 6.0, ((0, 8), (1, 4)))
    span_order = draw_span_order(jax.random.fold_in(keys[13], 71), 0)
    token_positions = draw_token_positions(jax.random.fold_in(keys[13], 71), 0)
    attn_gain = jnp.clip(1.0 + 0.18 * jax.random.normal(keys[3], (D,), jnp.float32), 0.099609375, 1.8984375).astype(jnp.bfloat16)
    w_query = scatter_about(keys[4], (D, D), D ** -0.5, 0.15625, ((0, 4),))
    w_key = scatter_about(keys[5], (D, KV_HEADS * HEAD_DIM), D ** -0.5, 0.15625, ((0, 4),))
    w_value = scatter_about(keys[6], (D, KV_HEADS * HEAD_DIM), D ** -0.5, 0.15625, ((0, 4),))
    w_out = scatter_about(keys[7], (D, D), (max(D * 16 // LEN, 1)) ** -0.5, 1.75, ((0, 4),))
    mlp_gain = jnp.clip(1.0 + 0.18 * jax.random.normal(keys[8], (D,), jnp.float32), 0.099609375, 1.8984375).astype(jnp.bfloat16)
    w_gate = scatter_about(keys[9], (D, FF), D ** -0.5, 0.15625, ((0, 4),))
    w_up = scatter_about(keys[10], (D, FF), D ** -0.5, 0.15625, ((0, 4),))
    w_down = scatter_about(keys[11], (FF, D), FF ** -0.5, 0.09375, ((0, 4),))
    cotangent = scatter_about(keys[12], (SEQS, LEN, D), 1.0, 6.0, ((0, 8), (1, 4)))
    return {"tokens": tokens, "span_order": span_order, "token_positions": token_positions, "attn_gain": attn_gain, "w_query": w_query, "w_key": w_key, "w_value": w_value, "w_out": w_out, "mlp_gain": mlp_gain, "w_gate": w_gate, "w_up": w_up, "w_down": w_down, "cotangent": cotangent}


@jax.custom_vjp
def low(v):
    return lax.optimization_barrier(v.astype(jnp.bfloat16)).astype(jnp.float32)

@jax.custom_vjp
def low_back(v):
    return v

def low_keep(v):
    return (low(v), None)

def low_pass(kept, grad):
    return (grad,)

def back_keep(v):
    return (v, None)

def back_low(kept, grad):
    return (low(grad),)
low.defvjp(low_keep, low_pass)
low_back.defvjp(back_keep, back_low)
norm_eps = 1e-05
rope_base = 100000.0
masked_value = -1e+30
highest = lax.Precision.HIGHEST

def rms_scale(values):
    return lax.rsqrt(lax.optimization_barrier(jnp.mean(values * values, axis=-1, keepdims=True)) + norm_eps)

def rope_tables(positions):
    half_dim = HEAD_DIM // 2
    frequency = rope_base ** (-2.0 * jnp.arange(half_dim, dtype=jnp.float32) / HEAD_DIM)
    angles = positions.astype(jnp.float32)[..., None] * frequency
    return (jnp.cos(angles), jnp.sin(angles))

def rotate(values, cosine, sine_table):
    half_dim = values.shape[-1] // 2
    first_half = values[..., :half_dim]
    second_half = values[..., half_dim:]
    cosine = cosine[..., None, :]
    sine_table = sine_table[..., None, :]
    return jnp.concatenate([first_half * cosine - second_half * sine_table, second_half * cosine + first_half * sine_table], axis=-1)

def true_index(order_row):
    slot_index = jnp.arange(LEN, dtype=jnp.int32)
    return (order_row[slot_index // SPAN] * SPAN + slot_index % SPAN).astype(jnp.int32)

def layer(x_seq, params, cosine, sine_table, tindex):
    attn_gain, w_query, w_key, w_value, w_out, mlp_gain, w_gate, w_up, w_down = params
    groups = HEADS // KV_HEADS
    score_scale = HEAD_DIM ** (-0.5)
    normed = low(x_seq * rms_scale(x_seq) * attn_gain)
    queries = low_back(jnp.dot(normed, w_query, precision=highest)).reshape(LEN, HEADS, HEAD_DIM)
    queries = low(rotate(queries, cosine, sine_table))
    keys_all = low_back(jnp.dot(normed, w_key, precision=highest)).reshape(LEN, KV_HEADS, HEAD_DIM)
    keys_all = low(rotate(keys_all, cosine, sine_table))
    values_all = low(low_back(jnp.dot(normed, w_value, precision=highest))).reshape(LEN, KV_HEADS, HEAD_DIM)
    block_rows = min(512, LEN)
    query_blocks = queries.reshape(LEN // block_rows, block_rows, KV_HEADS, groups, HEAD_DIM)
    index_blocks = tindex.reshape(LEN // block_rows, block_rows)

    def attend(pieces):
        query_block, index_block = pieces
        raw_scores = jnp.einsum('qgjd,kgd->gjqk', query_block, keys_all, precision=highest)
        scores = low_back(score_scale * raw_scores)
        allowed = index_block[:, None] >= tindex[None, :]
        scores = jnp.where(allowed[None, None], scores, masked_value)
        row_max = lax.optimization_barrier(jnp.max(scores, axis=-1, keepdims=True))
        exponent = jnp.exp(scores - row_max)
        probabilities = low(exponent / lax.optimization_barrier(jnp.sum(exponent, axis=-1, keepdims=True)))
        return jnp.einsum('gjqk,kgd->qgjd', probabilities, values_all, precision=highest)
    mixed = lax.map(jax.checkpoint(attend), (query_blocks, index_blocks)).reshape(LEN, D)
    attended = low_back(jnp.dot(low(low_back(mixed)), w_out, precision=highest))
    hidden = x_seq + attended
    normed_two = low(hidden * rms_scale(hidden) * mlp_gain)
    gate_pre = low_back(jnp.dot(normed_two, w_gate, precision=highest))
    up_pre = low_back(jnp.dot(normed_two, w_up, precision=highest))
    product = low(jax.nn.silu(gate_pre) * up_pre)
    return hidden + jnp.dot(product, w_down, precision=highest)

def reference(tokens, span_order, token_positions, attn_gain, w_query, w_key, w_value, w_out, mlp_gain, w_gate, w_up, w_down, cotangent):
    params = (attn_gain.astype(jnp.float32), w_query.astype(jnp.float32), w_key.astype(jnp.float32), w_value.astype(jnp.float32), w_out.astype(jnp.float32), mlp_gain.astype(jnp.float32), w_gate.astype(jnp.float32), w_up.astype(jnp.float32), w_down.astype(jnp.float32))

    def one_sequence(totals, item):
        x_seq, cot_seq, order_row, position_row = item
        cosine, sine_table = rope_tables(position_row)
        tindex = true_index(order_row)

        def forward(x_value, param_values):
            return layer(x_value, param_values, cosine, sine_table, tindex)
        result, pullback = jax.vjp(forward, x_seq.astype(jnp.float32), params)
        grad_x, grad_params = pullback(cot_seq.astype(jnp.float32))
        totals = jax.tree.map(jnp.add, totals, grad_params)
        return (totals, (result.astype(jnp.bfloat16), grad_x.astype(jnp.bfloat16)))
    zeros_init = jax.tree.map(jnp.zeros_like, params)
    totals, outputs = lax.scan(one_sequence, zeros_init, (tokens, cotangent, span_order, token_positions))
    return (outputs[0], outputs[1], totals[0], totals[1], totals[2], totals[3], totals[4], totals[5], totals[6], totals[7], totals[8])
```

```python
import functools

import jax
import jax.numpy as jnp
import numpy as np
from jax import lax
from jax.experimental import pallas as pl
from jax.experimental.pallas import tpu as pltpu
from jax.sharding import PartitionSpec as P

HEADS = 16
KV_HEADS = 8
HEAD_DIM = 96
SPAN = 128
GROUPS = HEADS // KV_HEADS
HALF = HEAD_DIM // 2
LANES = 128
SLOT = LANES // 2
GROUP_COLS = (GROUPS + 2) * HEAD_DIM
Q_COLS = GROUPS * HEAD_DIM
Q_LANES = GROUPS * LANES
PAD_ROWS = 16

norm_eps = 1e-05
rope_base = 100000.0
masked_value = -1e30
score_scale = HEAD_DIM ** (-0.5)
exp2_scale = score_scale * 1.4426950408889634

bf16 = jnp.bfloat16
f32 = jnp.float32
MIB = 1 << 20
NT = (((1,), (1,)), ((), ()))
TN = (((0,), (0,)), ((), ()))


def rms_scale(values):
    return lax.rsqrt(jnp.mean(values * values, axis=-1, keepdims=True) + norm_eps)


def matmul(left, right):
    return jnp.dot(left, right, preferred_element_type=f32)


def dot_nt(left, right):
    return lax.dot_general(left, right, NT, preferred_element_type=f32)


def dot_tn(left, right):
    return lax.dot_general(left, right, TN, preferred_element_type=f32)


def params(limit=60):
    return pltpu.CompilerParams(vmem_limit_bytes=limit * MIB)


def short():
    return pl.CostEstimate(flops=1000, bytes_accessed=1000, transcendentals=0)


def whole(shape):
    return pl.BlockSpec(shape, lambda *_: (0,) * len(shape))


def part(block, index):
    return pl.BlockSpec(block, lambda *_: index)


def call(kernel, grid, in_specs, out_specs, out_shape, operands, name, prefetch=(), scratch=()):
    return pl.pallas_call(
        kernel,
        grid_spec=pltpu.PrefetchScalarGridSpec(
            num_scalar_prefetch=len(prefetch), grid=grid, in_specs=in_specs, out_specs=out_specs, scratch_shapes=list(scratch)
        ),
        out_shape=[jax.ShapeDtypeStruct(shape, dtype) for shape, dtype in out_shape],
        compiler_params=params(),
        cost_estimate=short(),
        name=name,
    )(*prefetch, *operands)


def spread_matrix():
    spread = np.zeros((GROUP_COLS, (GROUPS + 2) * LANES), np.float32)
    for row in range(spread.shape[0]):
        head, feature = divmod(row, HEAD_DIM)
        half, place = divmod(feature, HALF)
        spread[row, head * LANES + half * SLOT + place] = 1.0
    return spread


def front_kernel(near_ref, far_ref, flag_ref, *refs):
    spans = 4
    near, far, refs = refs[:spans], refs[spans : 2 * spans], refs[2 * spans :]
    cos_ref, sin_ref, gain_ref, spread_ref, w0, w1, w2, w3a, w3b, x_out, n_out, nt_out, q_out, k_out, v_out, w_out = refs
    q_width, k_width = q_out.shape[1], k_out.shape[1]
    step_at = pl.program_id(0)

    @pl.when(step_at == 0)
    def _():
        depth = w0.shape[1]
        halves = w3a.shape[0]
        for at, piece in enumerate((w0, w1, w2, None)):
            for z in range(w0.shape[0]):
                block = piece[z] if piece is not None else (w3a[z] if z < halves else w3b[z - halves])
                spread = matmul(block, spread_ref[...]).astype(bf16)
                rows = slice(z * depth, (z + 1) * depth)
                w_out[rows, Q_LANES * at : Q_LANES * (at + 1)] = spread[:, :Q_LANES]
                w_out[rows, q_width + LANES * at : q_width + LANES * (at + 1)] = spread[:, Q_LANES : Q_LANES + LANES]
                at_v = q_width + k_width + LANES * at
                w_out[rows, at_v : at_v + LANES] = spread[:, Q_LANES + LANES :]

    for k in range(spans):
        rows = slice(k * SPAN, (k + 1) * SPAN)

        @pl.when(flag_ref[spans * step_at + k] == 0)
        def _():
            x_out[rows, :] = near[k][0]

        @pl.when(flag_ref[spans * step_at + k] != 0)
        def _():
            x_out[rows, :] = far[k][0]

    x = x_out[...].astype(f32)
    normed = (x * rms_scale(x) * gain_ref[...]).astype(bf16)
    n_out[...] = normed
    nt_out[...] = normed.T
    cosine, sine = cos_ref[...], sin_ref[...]
    lane = lax.broadcasted_iota(jnp.int32, (1, LANES), 1)
    ones = jnp.where((lane >= HALF) & (lane < HALF + 3), 1.0, 0.0)
    step = 4 * LANES
    for start in range(0, w_out.shape[1], step):
        raw = matmul(normed, w_out[:, start : start + step])
        for piece in range(0, step, LANES):
            at = start + piece
            head = raw[:, piece : piece + LANES]
            if at < q_width + k_width:
                head = head * cosine + pltpu.roll(head, SLOT, 1) * sine
            if at < q_width:
                q_out[:, at : at + LANES] = head.astype(bf16)
            elif at < q_width + k_width:
                k_out[:, at - q_width : at - q_width + LANES] = (head + ones).astype(bf16)
            else:
                v_out[:, at - q_width - k_width : at - q_width - k_width + LANES] = (head + ones).astype(bf16)


def span_specs(width, count):
    def near(k):
        return pl.BlockSpec((1, SPAN, width), lambda i, near, far, flag: (near[count * i + k], 0, 0))

    def far(k):
        return pl.BlockSpec((1, SPAN, width), lambda i, near, far, flag: (far[count * i + k], 0, 0))

    return [near(k) for k in range(count)] + [far(k) for k in range(count)]


def as_spans(array):
    return array.reshape(array.shape[0] // SPAN, SPAN, array.shape[1])


def front(places, near, far, cosine, sine, gain, pieces):
    rows, width = 2 * near.shape[0], near.shape[1]
    groups = len(pieces) - 1
    n_shard = pieces[0].shape[0]
    depth = width // n_shard
    spread = jnp.asarray(spread_matrix(), bf16)
    spans = 4
    tile = spans * SPAN
    q_width, k_width = groups * Q_LANES, groups * LANES
    total = q_width + 2 * k_width

    def rows_spec(cols):
        return pl.BlockSpec((tile, cols), lambda i, *_: (i, 0))

    near, far = as_spans(near), as_spans(far)
    return call(
        front_kernel,
        (rows // tile,),
        span_specs(width, spans)
        + [rows_spec(LANES), rows_spec(LANES), whole(gain.shape), whole(spread.shape)]
        + [part((p.shape[0], depth, p.shape[2]), (0, 0, 0)) for p in pieces],
        [rows_spec(width), rows_spec(width), pl.BlockSpec((width, tile), lambda i, *_: (0, i))]
        + [rows_spec(q_width), rows_spec(k_width), rows_spec(k_width), whole((n_shard * depth, total))],
        [
            ((rows, width), bf16),
            ((rows, width), bf16),
            ((width, rows), bf16),
            ((rows, q_width), bf16),
            ((rows, k_width), bf16),
            ((rows, k_width), bf16),
            ((n_shard * depth, total), bf16),
        ],
        [near] * spans + [far] * spans + [cosine, sine, gain, spread, *pieces],
        "front",
        places,
    )


def span_copy(places, source):
    width = source.shape[1]
    count = places.shape[0]

    def kernel(place_ref, x_ref, o_ref):
        o_ref[...] = x_ref[...]

    (out,) = call(
        kernel,
        (count,),
        [pl.BlockSpec((1, SPAN, width), lambda i, place: (place[i], 0, 0))],
        [pl.BlockSpec((1, SPAN, width), lambda i, place: (i, 0, 0))],
        [((count, SPAN, width), source.dtype)],
        [as_spans(source)],
        "span_copy",
        [places],
    )
    return out.reshape(count * SPAN, width)


def span_join(places, near, far):
    width = near.shape[1]
    count = 2 * near.shape[0] // SPAN

    def kernel(near_ref, far_ref, flag_ref, a_ref, b_ref, o_ref):
        @pl.when(flag_ref[pl.program_id(0)] == 0)
        def _():
            o_ref[...] = a_ref[...]

        @pl.when(flag_ref[pl.program_id(0)] != 0)
        def _():
            o_ref[...] = b_ref[...]

    (out,) = call(
        kernel,
        (count,),
        span_specs(width, 1),
        [pl.BlockSpec((1, SPAN, width), lambda i, *_: (i, 0, 0))],
        [((count, SPAN, width), near.dtype)],
        [as_spans(near), as_spans(far)],
        "span_join",
        places,
    )
    return out.reshape(count * SPAN, width)


def three_parts(values):
    first = values.astype(bf16).astype(f32)
    second = (values - first).astype(bf16).astype(f32)
    third = values - first - second
    return first, second, third


def with_lanes(block, column):
    lane = lax.broadcasted_iota(jnp.int32, block.shape, 1)
    first, second, third = three_parts(column)
    wide = block.astype(f32)
    wide = jnp.where(lane == HALF, first, wide)
    wide = jnp.where(lane == HALF + 1, second, wide)
    wide = jnp.where(lane == HALF + 2, third, wide)
    return wide.astype(bf16)


Q_TILE = 256
K_CHUNK = 512


def heads_down(block):
    return jnp.concatenate([block[:, LANES * h : LANES * (h + 1)] for h in range(GROUPS)], axis=0)


def attend_kernel(q_ref, k_ref, v_ref, mixed_ref, q_aug_ref):
    rows = q_ref.shape[0]
    for tile in range(rows // Q_TILE):
        first_row = tile * Q_TILE
        query = heads_down(q_ref[first_row : first_row + Q_TILE, :])
        end = first_row + Q_TILE
        top = acc = None
        for start in range(0, end, K_CHUNK):
            size = min(K_CHUNK, end - start)
            key = k_ref[start : start + size, :]
            value = v_ref[start : start + size, :]
            scores = dot_nt(query, key)
            if start + size > first_row:
                row = lax.broadcasted_iota(jnp.int32, (Q_TILE, size), 0) + first_row
                column = lax.broadcasted_iota(jnp.int32, (Q_TILE, size), 1) + start
                allowed = row >= column
                scores = jnp.where(jnp.concatenate([allowed] * GROUPS, axis=0), scores, masked_value)
            chunk_top = jnp.max(scores, axis=-1, keepdims=True)
            new_top = chunk_top if top is None else jnp.maximum(top, chunk_top)
            weights = jnp.exp2((scores - new_top) * exp2_scale).astype(bf16)
            part = matmul(weights, value)
            acc = part if top is None else acc * jnp.exp2((top - new_top) * exp2_scale) + part
            top = new_top
        total = acc[:, HALF : HALF + 1]
        mixed = (acc * (1.0 / total)).astype(bf16)
        log_total = top + jnp.log2(total) * (1.0 / exp2_scale)
        marked = with_lanes(query, -log_total)
        for h in range(GROUPS):
            mixed_ref[first_row : first_row + Q_TILE, LANES * h : LANES * (h + 1)] = mixed[Q_TILE * h : Q_TILE * (h + 1)]
            q_aug_ref[first_row : first_row + Q_TILE, LANES * h : LANES * (h + 1)] = marked[Q_TILE * h : Q_TILE * (h + 1)]


def attend(queries, keys, values):
    rows, k_width = keys.shape
    groups = k_width // LANES
    pair = pl.BlockSpec((rows, Q_LANES), lambda g: (0, g))
    single = pl.BlockSpec((rows, LANES), lambda g: (0, g))
    return call(
        attend_kernel, (groups,), [pair, single, single], [pair, pair], [(queries.shape, bf16)] * 2, [queries, keys, values], "attend"
    )


def attend_back_kernel(q_ref, k_ref, v_ref, do_ref, o_ref, cos_ref, sin_ref, dq_ref, dk_ref, dv_ref, q_s, do_s, dq_s, dk_s, dv_s):
    rows = q_ref.shape[0]
    tiles = rows // Q_TILE
    for tile in range(tiles):
        at = slice(tile * Q_TILE, (tile + 1) * Q_TILE)
        q_s[tile] = heads_down(q_ref[at, :])
        grad = heads_down(do_ref[at, :])
        inner = jnp.sum(grad.astype(f32) * heads_down(o_ref[at, :]).astype(f32), axis=-1, keepdims=True)
        do_s[tile] = with_lanes(grad, -inner)
        dq_s[tile] = jnp.zeros(dq_s.shape[1:], f32)

    def unit(tile, key_start, size, mask_from):
        key = k_ref[key_start : key_start + size, :]
        value = v_ref[key_start : key_start + size, :]
        query, grad = q_s[tile], do_s[tile]
        probs = jnp.exp2(dot_nt(key, query) * exp2_scale)
        if mask_from is not None:
            row = lax.broadcasted_iota(jnp.int32, (size, Q_TILE), 0)
            column = lax.broadcasted_iota(jnp.int32, (size, Q_TILE), 1) + mask_from
            allowed = jnp.concatenate([row <= column] * GROUPS, axis=1)
            probs = jnp.where(allowed, probs, 0.0)
        d_scores = (probs * dot_nt(value, grad)).astype(bf16)
        dv_s[:size] += matmul(probs.astype(bf16), grad)
        dk_s[:size] += matmul(d_scores, query)
        dq_s[tile] += dot_tn(d_scores, key)

    for key_start in range(0, rows, K_CHUNK):
        dk_s[...] = jnp.zeros(dk_s.shape, f32)
        dv_s[...] = jnp.zeros(dv_s.shape, f32)
        tile = key_start // Q_TILE
        unit(tile, key_start, Q_TILE, 0)
        unit(tile + 1, key_start, K_CHUNK, Q_TILE)
        if tile + 2 < tiles:

            @pl.loop(tile + 2, tiles)
            def _(later):
                unit(later, key_start, K_CHUNK, None)

        at = slice(key_start, key_start + K_CHUNK)
        turned = dk_s[...] * score_scale
        turned = turned * cos_ref[at, :] - pltpu.roll(turned, SLOT, 1) * sin_ref[at, :]
        dk_ref[at, :] = turned.astype(bf16)
        dv_ref[at, :] = dv_s[...].astype(bf16)
    for tile in range(tiles):
        at = slice(tile * Q_TILE, (tile + 1) * Q_TILE)
        cosine, sine = cos_ref[at, :], sin_ref[at, :]
        for h in range(GROUPS):
            turned = dq_s[tile, Q_TILE * h : Q_TILE * (h + 1), :] * score_scale
            turned = turned * cosine - pltpu.roll(turned, SLOT, 1) * sine
            dq_ref[at, LANES * h : LANES * (h + 1)] = turned.astype(bf16)


def attend_back(first, groups, q_aug, keys, values, grad, mixed, cosine, sine):
    rows = keys.shape[0]
    tiles = rows // Q_TILE
    pair = pl.BlockSpec((rows, Q_LANES), lambda g: (0, g + first))
    single = pl.BlockSpec((rows, LANES), lambda g: (0, g + first))
    pair_out = pl.BlockSpec((rows, Q_LANES), lambda g: (0, g))
    single_out = pl.BlockSpec((rows, LANES), lambda g: (0, g))
    stacked = (tiles, GROUPS * Q_TILE, LANES)
    table = whole((rows, LANES))
    return call(
        attend_back_kernel,
        (groups,),
        [pair, single, single, pair, pair, table, table],
        [pair_out, single_out, single_out],
        [((rows, groups * Q_LANES), bf16), ((rows, groups * LANES), bf16), ((rows, groups * LANES), bf16)],
        [q_aug, keys, values, grad, mixed, cosine, sine],
        "attend_back",
        scratch=[
            pltpu.VMEM(stacked, bf16),
            pltpu.VMEM(stacked, bf16),
            pltpu.VMEM(stacked, f32),
            pltpu.VMEM((K_CHUNK, LANES), f32),
            pltpu.VMEM((K_CHUNK, LANES), f32),
        ],
    )


def flat(block):
    return block.reshape(block.shape[0] * block.shape[1], block.shape[2])


def down_columns(down_ref, j, zs):
    rows = down_ref.shape[1] // 3
    return jnp.concatenate([down_ref[z, rows * j : rows * (j + 1), :] for z in zs], axis=0)


def hidden_kernel(n_ref, cot_ref, gate_ref, up_ref, down_ref, product_ref, dboth_ref):
    n_shard, units = gate_ref.shape[0], gate_ref.shape[2]
    third = cot_ref.shape[1] // 3
    step = 256
    for start in range(0, units, step):
        at = slice(start, start + step)
        zs = range(start * n_shard // units, (start + step) * n_shard // units)
        gate = matmul(n_ref[...], flat(gate_ref[:, :, at]))
        up = matmul(n_ref[...], flat(up_ref[:, :, at]))
        d_product = sum(dot_nt(cot_ref[:, third * j : third * (j + 1)], down_columns(down_ref, j, zs)) for j in range(3))
        sigmoid = 1.0 / (1.0 + jnp.exp(-gate))
        silu = gate * sigmoid
        product_ref[:, at] = (silu * up).astype(bf16)
        dboth_ref[:, at] = (d_product * up * sigmoid * (1.0 + gate * (1.0 - sigmoid))).astype(bf16)
        dboth_ref[:, units + start : units + start + step] = (d_product * silu).astype(bf16)


def feed_grads(normed_t, cot, product, d_both):
    width, rows = normed_t.shape
    units = product.shape[1]
    steps = width // units

    def kernel(n_ref, cot_ref, product_ref, both_ref, gate_ref, up_ref, down_ref, turned_ref):
        step = pl.program_id(0)

        @pl.when(step < steps)
        def _():
            gate_ref[...] = matmul(n_ref[...], both_ref[:, :units]).astype(bf16)
            up_ref[...] = matmul(n_ref[...], both_ref[:, units:]).astype(bf16)

        @pl.when(step == steps)
        def _():
            turned_ref[...] = product_ref[...].T

        @pl.when(step >= steps)
        def _():
            down_ref[...] = matmul(turned_ref[...], cot_ref[...]).astype(bf16)

    early = lambda i: (jnp.minimum(i, steps - 1), 0)
    late = lambda i: (0, jnp.maximum(i - steps, 0))
    return call(
        kernel,
        (2 * steps,),
        [pl.BlockSpec((units, rows), early), pl.BlockSpec((rows, units), late), whole(product.shape), whole(d_both.shape)],
        [pl.BlockSpec((units, units), early), pl.BlockSpec((units, units), early), pl.BlockSpec((units, units), late)],
        [((width, units), bf16), ((width, units), bf16), ((units, width), bf16)],
        [normed_t, cot, product, d_both],
        "feed_grads",
        scratch=[pltpu.VMEM((units, rows), bf16)],
    )


def whole_of(array):
    return array, array.shape, (0,) * array.ndim


def third_of(array, index):
    rows = 384
    return array, (array.shape[0], rows, array.shape[2]), (0, index, 0)


def hidden_units(normed, cot, weights):
    rows, width = normed.shape
    units = weights[0][0].shape[2]
    tile = 512
    wide = pl.BlockSpec((tile, width), lambda i: (i, 0))
    thin = pl.BlockSpec((tile, units), lambda i: (i, 0))
    return call(
        hidden_kernel,
        (rows // tile,),
        [wide, wide] + [part(block, index) for _, block, index in weights],
        [thin, pl.BlockSpec((tile, 2 * units), lambda i: (i, 0))],
        [((rows, units), bf16), ((rows, 2 * units), bf16)],
        [normed, cot] + [a for a, _, _ in weights],
        "hidden_units",
    )


def sum_rows_call(body, base, lhs, rhs, others, outs, tile, name):
    rows = outs[0][0][0]

    def shifted(cols):
        return pl.BlockSpec((tile, cols), lambda i, base: (base[0] + i, 0))

    def plain(cols):
        return pl.BlockSpec((tile, cols), lambda i, base: (i, 0))

    in_specs = [shifted(a.shape[1]) for a in lhs] + [part(block, index) for _, block, index in rhs]
    for a, kind in others:
        in_specs.append(whole(a.shape) if kind == "whole" else {"shifted": shifted, "plain": plain}[kind](a.shape[1]))
    out_specs = [plain(shape[1]) if shape[0] == rows else whole(shape) for shape, _ in outs]
    n_lhs, n_rhs, n_other = len(lhs), len(rhs), len(others)

    def kernel(base_ref, *refs):
        left, refs = refs[:n_lhs], refs[n_lhs:]
        right, refs = refs[:n_rhs], refs[n_rhs:]
        body(left, right, refs[:n_other], refs[n_other:])

    return call(
        kernel,
        (rows // tile,),
        in_specs,
        out_specs,
        outs,
        [*lhs, *[a for a, _, _ in rhs], *[a for a, _ in others]],
        name,
        [base],
    )


def norm_back(grad_normed, values, scale_rows, gain):
    scaled = grad_normed * gain
    return scale_rows * scaled - values * (scale_rows * scale_rows * scale_rows) * jnp.mean(scaled * values, axis=-1, keepdims=True)


def column_sums(values):
    return jnp.sum(values.reshape(-1, 8, values.shape[-1]), axis=0)


def half_specs(tile, tiles, width):
    own = pl.BlockSpec((tile, width), lambda i, core: (jnp.clip(i - tiles * core[0], 0, tiles - 1), 0))
    far = pl.BlockSpec((tile, width), lambda i, core: (jnp.clip(i - tiles * (1 - core[0]), 0, tiles - 1), 0))
    return [own, far]


def place_half(core_ref, tiles, own_ref, far_ref, out_ref):
    is_own = pl.program_id(0) // tiles == core_ref[0]

    @pl.when(is_own)
    def _():
        out_ref[...] = own_ref[...]

    @pl.when(jnp.logical_not(is_own))
    def _():
        out_ref[...] = far_ref[...]


def join_halves(core, own, far):
    rows, width = own.shape
    tile = 256
    tiles = rows // tile

    def kernel(core_ref, own_ref, far_ref, out_ref, turned_ref):
        place_half(core_ref, tiles, own_ref, far_ref, out_ref)
        turned_ref[...] = out_ref[...].T

    return call(
        kernel,
        (2 * tiles,),
        half_specs(tile, tiles, width),
        [pl.BlockSpec((tile, width), lambda i, _: (i, 0)), pl.BlockSpec((width, tile), lambda i, _: (0, i))],
        [((2 * rows, width), bf16), ((width, 2 * rows), bf16)],
        [own, far],
        "join_halves",
        [core],
    )


def mixed_back(core, own, far, w_out_rows):
    rows, width = own.shape
    heads = w_out_rows.shape[0]
    tile = 512
    tiles = rows // tile

    def kernel(core_ref, own_ref, far_ref, w_ref, out_ref, grad_ref):
        place_half(core_ref, tiles, own_ref, far_ref, out_ref)
        grad_ref[...] = dot_nt(out_ref[...], w_ref[...]).astype(bf16)

    return call(
        kernel,
        (2 * tiles,),
        half_specs(tile, tiles, width) + [whole(w_out_rows.shape)],
        [pl.BlockSpec((tile, width), lambda i, _: (i, 0)), pl.BlockSpec((tile, heads), lambda i, _: (i, 0))],
        [((2 * rows, width), bf16), ((2 * rows, heads), bf16)],
        [own, far, w_out_rows],
        "mixed_back",
        [core],
    )


def out_rows(place, blocks):
    n_shard, rows_in, cols = blocks[0].shape
    chunks = rows_in // HALF
    quarters = len(blocks)
    shape = (quarters * quarters * SLOT, chunks * cols)

    def kernel(place_ref, *refs):
        out_ref = refs[-1]
        out_ref[...] = jnp.zeros(shape, bf16)
        for group in range(quarters):
            for at in range(quarters):
                row = pl.multiple_of(Q_LANES * group + SLOT * (at ^ place_ref[0]), SLOT)
                for j in range(chunks):
                    out_ref[pl.ds(row, HALF), cols * j : cols * (j + 1)] = refs[at][group ^ place_ref[0], HALF * j : HALF * (j + 1), :]

    (out,) = call(
        kernel,
        (1,),
        [whole((n_shard, rows_in, cols))] * quarters,
        [whole(shape)],
        [(shape, bf16)],
        blocks,
        "out_rows",
        [place],
    )
    return out


def out_grad_blocks(place, mixed, grad):
    rows, heads = mixed.shape
    width = grad.shape[1]
    quarters = heads // Q_LANES
    tile = 512

    def kernel(place_ref, mixed_ref, grad_ref, *refs):
        outs = refs[:quarters]
        group = pl.program_id(0)
        sums = dot_tn(mixed_ref[...], grad_ref[...]).astype(bf16)
        refs[quarters][...] = sums
        shard = group ^ place_ref[0]
        for at in range(quarters):
            row = pl.multiple_of(SLOT * (at ^ place_ref[0]), SLOT)
            outs[at][shard] = refs[quarters][pl.ds(row, HALF), :]

    return call(
        kernel,
        (quarters,),
        [pl.BlockSpec((rows, Q_LANES), lambda g, _: (0, g)), whole((rows, width))],
        [whole((quarters, HALF, width))] * quarters,
        [((quarters, HALF, width), bf16)] * quarters,
        [mixed, grad],
        "out_grads",
        [place],
        [pltpu.VMEM((Q_LANES, width), bf16)],
    )


def qkv_grad(normed_t, d_query, d_key, d_value):
    width, rows = normed_t.shape
    spread = jnp.asarray(spread_matrix(), bf16)
    tile = 512

    def kernel(n_ref, q_ref, k_ref, v_ref, spread_ref, out_ref):
        query = matmul(n_ref[...], q_ref[...]).astype(bf16)
        both = matmul(n_ref[...], jnp.concatenate([k_ref[...], v_ref[...]], axis=1)).astype(bf16)
        out_ref[...] = dot_nt(jnp.concatenate([query, both], axis=1), spread_ref[...]).astype(bf16)

    (out,) = call(
        kernel,
        (width // tile,),
        [
            pl.BlockSpec((tile, rows), lambda i: (i, 0)),
            whole(d_query.shape),
            whole(d_key.shape),
            whole(d_value.shape),
            whole(spread.shape),
        ],
        [pl.BlockSpec((tile, GROUP_COLS), lambda i: (i, 0))],
        [((width, GROUP_COLS), bf16)],
        [normed_t, d_query, d_key, d_value, spread],
        "qkv_grad",
    )
    return out


def unit_columns(where, pieces, n_shard, index):
    depth, cols = pieces[0].shape[0] // 2, pieces[0].shape[1]
    tile = 96
    count = len(pieces)
    quarters = count // 2
    unit_cols = cols // n_shard

    def kernel(where_ref, *refs):
        out_ref = refs[-1]
        for k in range(count):
            unit = quarters * (where_ref[1] ^ (k // quarters)) + (where_ref[0] ^ (k % quarters))
            for z in range(n_shard):
                at = pl.multiple_of((count * z + unit) * unit_cols, unit_cols)
                out_ref[:, pl.ds(at, unit_cols)] = refs[k][:, unit_cols * z : unit_cols * (z + 1)].astype(f32)

    steps = depth // tile
    (out,) = call(
        kernel,
        (depth // tile,),
        [pl.BlockSpec((tile, cols), lambda i, _: (index * steps + i, 0))] * count,
        [pl.BlockSpec((tile, cols * count), lambda i, _: (i, 0))],
        [((depth, cols * count), f32)],
        pieces,
        "unit_columns",
        [where],
    )
    return out


def unit_rows(where, pieces, down_depth):
    depth, width = pieces[0].shape
    count = len(pieces)
    quarters = count // 2
    out_depth = depth - down_depth

    def unit_at(i, where_ref):
        return quarters * (where_ref[1] ^ (i // quarters)) + (where_ref[0] ^ (i % quarters))

    def kernel(where_ref, *refs):
        for k in range(count):

            @pl.when(pl.program_id(0) == k)
            def _():
                refs[count][...] = refs[k][:down_depth, :].astype(f32)
                refs[count + 1][...] = refs[k][down_depth:, :].astype(f32)

    return call(
        kernel,
        (count,),
        [whole((depth, width))] * count,
        [
            pl.BlockSpec((down_depth, width), lambda i, where: (unit_at(i, where), 0)),
            pl.BlockSpec((out_depth, width), lambda i, where: (unit_at(i, where), 0)),
        ],
        [((down_depth * count, width), f32), ((out_depth * count, width), f32)],
        pieces,
        "unit_rows",
        [where],
    )


def head_columns(where, pieces):
    depth, cols = pieces[0].shape
    count = len(pieces)
    quarters = count // 2
    split = 2

    def kernel(where_ref, *refs):
        q_out, k_out, v_out = refs[count:]
        place, core = where_ref[0], where_ref[1]
        row = lax.broadcasted_iota(jnp.int32, (cols, cols), 0)
        column = lax.broadcasted_iota(jnp.int32, (cols, cols), 1)

        def moved(piece, start, size, to):
            chosen = (row >= start) & (row < start + size) & (row - start == column - to)
            return matmul(piece, jnp.where(chosen, 1.0, 0.0).astype(bf16))

        for at in range(quarters):
            total = 0.0
            for other in range(split):
                total += moved(refs[quarters * other + at][...], 0, Q_COLS, Q_COLS * (core ^ other))
            q_out[:, pl.ds(pl.multiple_of(cols * (place ^ at), LANES), cols)] = total
        for pair in range(quarters // 2):
            keys = values = 0.0
            for low in range(2):
                for other in range(split):
                    piece = refs[quarters * other + 2 * pair + low][...]
                    to = HEAD_DIM * (2 * ((place & 1) ^ low) + (core ^ other))
                    keys += moved(piece, Q_COLS, HEAD_DIM, to)
                    values += moved(piece, Q_COLS + HEAD_DIM, HEAD_DIM, to)
            start = pl.multiple_of(cols * ((place >> 1) ^ pair), LANES)
            k_out[:, pl.ds(start, cols)] = keys
            v_out[:, pl.ds(start, cols)] = values

    shapes = [(depth, quarters * split * w) for w in (Q_COLS, HEAD_DIM, HEAD_DIM)]
    return call(
        kernel, (1,), [whole((depth, cols))] * count, [whole(s) for s in shapes], [(s, f32) for s in shapes], pieces, "head_columns", [where]
    )


def chip_layer(
    tokens, span_order, token_positions, attn_gain, w_query, w_key, w_value, w_out, mlp_gain, w_gate, w_up, w_down, cotangent
):
    seq_dev, local_len, width = tokens.shape
    n_ctx, n_shard = lax.axis_size("ctx"), lax.axis_size("shard")
    split = n_ctx // seq_dev
    full_len = local_len * n_ctx
    half_rows = full_len // split
    spans_dev = local_len // SPAN
    quarters = 4
    units = w_gate.shape[1] // (split * quarters)
    unit_cols = units // n_shard
    gain_width = attn_gain.shape[0]
    ctx, batch, shard = lax.axis_index("ctx"), lax.axis_index("batch"), lax.axis_index("shard")
    seq, core = ctx // split, ctx % split
    place = 2 * seq + batch

    perm_x = [(c, c ^ split) for c in range(n_ctx)]
    perm_core = [(c, c ^ 1) for c in range(n_ctx)]
    perm_both = [(c, c ^ (split | 1)) for c in range(n_ctx)]
    perm_diagonal = [(2 * c + b, 2 * (c ^ split) + (b ^ 1)) for c in range(n_ctx) for b in range(2)]
    over_x = lambda a: lax.ppermute(a, "ctx", perm_x)
    over_core = lambda a: lax.ppermute(a, "ctx", perm_core)
    over_both = lambda a: lax.ppermute(a, "ctx", perm_both)
    over_y = lambda a: lax.ppermute(a, "batch", [(0, 1), (1, 0)])
    over_diagonal = lambda a: lax.ppermute(a, ("ctx", "batch"), perm_diagonal)

    def over_z(piece):
        gathered = lax.all_gather(piece, "shard", axis=0, tiled=True)
        return gathered.reshape(n_shard, piece.shape[0], piece.shape[1])

    def pick(array, index, axis):
        return lax.dynamic_index_in_dim(array, index, axis, keepdims=False)

    def scatter(block):
        return lax.psum_scatter(block, "shard", scatter_dimension=0, tiled=True)

    def add(*terms):
        return functools.reduce(lambda a, b: a + b, [t.astype(f32) for t in terms]).astype(bf16)

    def fence(*arrays):
        return lax.optimization_barrier(arrays)

    column = split * place + core
    unit_at = quarters * core + place

    def columns_of(array, width_of):
        return lax.dynamic_slice_in_dim(array, column * width_of, width_of, 1)

    def units_of(array, at):
        blocks = [lax.dynamic_slice_in_dim(array, (split * quarters * z + at) * unit_cols, unit_cols, 1) for z in range(n_shard)]
        return jnp.concatenate(blocks, axis=1)

    def stacked(rows, cols):
        return jnp.concatenate([rows[:, cols * j : cols * (j + 1)] for j in range(rows.shape[1] // cols)], axis=0)

    head_piece = jnp.concatenate(
        [columns_of(w_query, Q_COLS), columns_of(w_key, HEAD_DIM), columns_of(w_value, HEAD_DIM)], axis=1
    )
    gains = jnp.pad(jnp.stack([attn_gain, mlp_gain]), ((0, PAD_ROWS - 2), (0, 0)))
    out_piece = stacked(lax.dynamic_slice_in_dim(w_out, unit_at * HALF, HALF, 0), GROUP_COLS)
    head_piece = jnp.concatenate([head_piece, gains, out_piece], axis=0)

    def second_piece(at):
        return jnp.concatenate([units_of(w_up, at), stacked(lax.dynamic_slice_in_dim(w_down, at * unit_cols, unit_cols, 0), units)], axis=0)

    own_tokens, sent_tokens = pick(tokens, seq, 0), pick(tokens, 1 - seq, 0)
    positions = pick(token_positions, seq, 0)
    sent_positions = pick(token_positions, 1 - seq, 0)
    head_piece, own_tokens, sent_tokens, positions, sent_positions, w_gate, w_up, w_down = fence(
        head_piece, own_tokens, sent_tokens, positions, sent_positions, w_gate, w_up, w_down
    )
    head_own = over_z(head_piece)
    positions = jnp.stack([positions, over_x(sent_positions)])
    x_near = jnp.concatenate([own_tokens, over_x(sent_tokens)], axis=0)
    head_rows = gain_width + PAD_ROWS
    head_sent, out_own = head_own[:, :head_rows], head_own[:, head_rows:]
    gate_piece, second_own, second_last = units_of(w_gate, unit_at), second_piece(unit_at), second_piece(unit_at ^ 3)
    head_own, head_sent, out_own, x_near, positions, gate_piece, second_own, second_last, cotangent = fence(
        head_own, head_sent, out_own, x_near, positions, gate_piece, second_own, second_last, cotangent
    )

    gate_own = over_z(gate_piece)
    head_x, head_y, x_far = over_x(head_sent), over_y(head_sent), over_core(x_near)
    positions = jnp.concatenate([positions, over_core(positions)], axis=0).reshape(-1, SPAN)
    cot_own, cot_sent = pick(cotangent, seq, 0), pick(cotangent, 1 - seq, 0)
    order = pick(span_order, seq, 0)
    n_spans = order.shape[0]
    span_ids = jnp.arange(n_spans, dtype=jnp.int32)
    slot_of = jnp.sum(jnp.where(order[None, :] == span_ids[:, None], span_ids[None, :], 0), axis=1)
    owner = slot_of // spans_dev
    from_far = (owner % split) ^ core
    side_place = ((owner // split) ^ seq) * spans_dev + slot_of % spans_dev
    places = [
        jnp.where(from_far == 0, side_place, 0).astype(jnp.int32),
        jnp.where(from_far == 0, 0, side_place).astype(jnp.int32),
        from_far.astype(jnp.int32),
    ]
    head_x, head_y, x_far, positions, cot_own, cot_sent, out_own = fence(
        head_x, head_y, x_far, positions, cot_own, cot_sent, out_own
    )

    middle = n_shard // 2
    head_last = [over_x(head_y[:middle]), over_y(head_x[middle:])]
    choice = (from_far * seq_dev * spans_dev + side_place)[:, None] == span_ids[None, :]
    positions = jnp.sum(jnp.where(choice[:, :, None], positions[None], 0), axis=1).reshape(full_len)
    frequency = rope_base ** (-2.0 * jnp.arange(HALF, dtype=f32) / HEAD_DIM)
    angles = positions.astype(f32)[:, None] * frequency
    blank = jnp.zeros((full_len, SLOT - HALF), f32)
    cos_half, sin_half = jnp.cos(angles), jnp.sin(angles)
    cosine = jnp.concatenate([cos_half, blank, cos_half, blank], axis=1)
    sine = jnp.concatenate([-sin_half, blank, sin_half, blank], axis=1)
    gain_one = head_own[:, gain_width, :].reshape(1, width).astype(f32)
    gain_two = head_own[:, gain_width + 1, :].reshape(1, width).astype(f32)
    *head_last, cosine, sine, cot_sent, gate_own, second_own, out_own = fence(
        *head_last, cosine, sine, cot_sent, gate_own, second_own, out_own
    )

    out_blocks = [out_own, over_y(out_own), over_x(out_own), over_diagonal(out_own)]
    head_blocks = [head_own, head_y, head_x, *head_last]
    x, normed, normed_t, queries, keys, values, w_qkv = front(places, x_near, x_far, cosine, sine, gain_one, head_blocks)
    x, normed_t, queries, keys, values, w_qkv = fence(x, normed_t, queries, keys, values, w_qkv)

    second_own = over_z(second_own)
    cot_received, gate_y = over_x(cot_sent), over_y(gate_own)
    mixed, q_aug = attend(queries, keys, values)
    cot_near = jnp.concatenate([cot_own, cot_received], axis=0)
    mixed, q_aug, cot_near, gate_y, second_own, second_last, gate_sent, *out_blocks = fence(
        mixed, q_aug, cot_near, gate_y, second_own, second_last, gate_own, *out_blocks
    )

    second_last = over_z(second_last)
    gate_x, cot_far = over_x(gate_sent), over_core(cot_near)
    second_y = over_y(second_own)
    place_at = place.astype(jnp.int32)[None]
    w_out_rows = out_rows(place_at, out_blocks)
    mine = core.astype(jnp.int32)[None]
    other = 1 - mine
    row_tile = 256
    tiles_half = half_rows // row_tile
    full_out = (w_out_rows, w_out_rows.shape, (0, 0))

    def partial_rows(lhs, rhs, dots, name):
        def body(left, right, _, outs):
            dots(left, right, lambda at, total: outs[0].__setitem__((slice(None), at), total.astype(bf16)))

        tile = 512
        return sum_rows_call(body, other * (half_rows // tile), lhs, rhs, [], [((half_rows, width), bf16)], tile, name)[0]

    def out_dot(left, right, store):
        store(slice(None), matmul(left[0][...], right[0][...]))

    def back_dot(left, right, store):
        total = 0.0
        for k, both in enumerate(left):
            for which in range(2):
                total += dot_nt(both[:, units * which : units * (which + 1)], flat(right[2 * k + which][...]))
        store(slice(None), total)

    def down_dot(left, right, store):
        for j in range(width // units):
            total = sum(matmul(a[...], down_columns(b, j, range(n_shard))) for a, b in zip(left, right))
            store(slice(units * j, units * (j + 1)), total)

    def in_dot(left, right, store):
        total = 0.0
        for which, weights in enumerate(right):
            total += dot_nt(jnp.concatenate([a[...] for a in left[which::3]], axis=1), weights[...])
        store(slice(None), total)

    def kept(dots, left, right):
        found = []
        dots(left, right, lambda at, total: found.append(total))
        return found[0]

    received = over_core(partial_rows([mixed], [full_out], out_dot, "out_other"))

    def hidden_body(left, right, others, outs):
        x_ref, received_ref, gain_ref = others
        hidden = x_ref[...].astype(f32) + kept(out_dot, left, right) + received_ref[...].astype(f32)
        outs[0][...] = hidden
        outs[1][...] = (hidden * rms_scale(hidden) * gain_ref[...]).astype(bf16)

    hidden, normed_two_own = sum_rows_call(
        hidden_body,
        mine * tiles_half,
        [mixed],
        [full_out],
        [(x, "shifted"), (received, "plain"), (gain_two, "whole")],
        [((half_rows, width), f32), ((half_rows, width), bf16)],
        row_tile,
        "out_own",
    )
    normed_two_own, cot_far, gate_x, second_own = fence(normed_two_own, cot_far, gate_x, second_own)
    second_x = over_x(second_own)
    cot = span_join(places, cot_near, cot_far)
    normed_two, normed_two_t = join_halves(mine, normed_two_own, over_core(normed_two_own))
    normed_two, normed_two_t, cot, second_y, second_last = fence(normed_two, normed_two_t, cot, second_y, second_last)

    def feed(normed_two, cot, gate, second, with_grads=True):
        weights = [whole_of(gate), third_of(second, 0), third_of(second, 1)]
        product, d_both = hidden_units(normed_two, cot, weights)
        if not with_grads:
            return weights, product, d_both
        return weights, product, d_both, feed_grads(normed_two_t, cot, product, d_both)

    gate_last = over_y(gate_x)
    fed = [feed(normed_two, cot, gate_own, second_own)]
    own_grads, normed_two, second_x, gate_last = fence(fed[0][3], normed_two, second_x, gate_last)
    fed.append(feed(normed_two, cot, gate_y, second_y))
    (gate_gy, up_gy, down_gy), normed_two = fence(fed[1][3], normed_two)
    down_gy = over_y(down_gy)
    fed.append(feed(normed_two, cot, gate_x, second_x))
    (gate_gx, up_gx, down_gx), normed_two, gate_gy, up_gy, down_gy = fence(fed[2][3], normed_two, gate_gy, up_gy, down_gy)
    gate_gy, down_gx = over_y(gate_gy), over_x(down_gx)
    weights_last, product_last, d_both_last = feed(normed_two, cot, gate_last, second_last, False)
    fed.append((weights_last, product_last, d_both_last))
    products, d_boths = [f[1] for f in fed], [f[2] for f in fed]

    back_rhs = [f[0][k] for f in fed for k in range(2)]
    downs = [f[0][2] for f in fed]
    back_sent = partial_rows(d_boths, back_rhs, back_dot, "back_other")
    back_sent, d_boths, products, gate_gy, up_gy, down_gx, gate_gx, up_gx = fence(
        back_sent, d_boths, products, gate_gy, up_gy, down_gx, gate_gx, up_gx
    )
    received_two = over_core(back_sent)
    up_gy, gate_gx = over_y(up_gy), over_x(gate_gx)
    gate_gl, up_gl, down_gl = feed_grads(normed_two_t, cot, products[3], d_boths[3])
    out_sent = partial_rows(products, downs, down_dot, "down_other")
    received_two, out_sent, up_gy, gate_gx, gate_gl, up_gl, up_gx, down_gl = fence(
        received_two, out_sent, up_gy, gate_gx, gate_gl, up_gl, up_gx, down_gl
    )

    def back_body(left, right, others, outs):
        received_ref, hidden_ref, cot_ref, gain_ref = others
        grad_normed = kept(back_dot, left, right) + received_ref[...].astype(f32)
        values_ = hidden_ref[...]
        scale_rows = rms_scale(values_)
        grad_hidden = cot_ref[...].astype(f32) + norm_back(grad_normed, values_, scale_rows, gain_ref[...])
        outs[0][...] = grad_hidden
        outs[1][...] = grad_hidden.astype(bf16)

        @pl.when(pl.program_id(0) == 0)
        def _():
            outs[2][...] = jnp.zeros(outs[2].shape, f32)

        outs[2][...] += column_sums(grad_normed * values_ * scale_rows)

    up_gx, gate_gl = over_x(up_gx), scatter(gate_gl)
    received_out = over_core(out_sent)
    grad_hidden, grad_attended_own, gain_two_sums = sum_rows_call(
        back_body,
        mine * tiles_half,
        d_boths,
        back_rhs,
        [(received_two, "plain"), (hidden, "plain"), (cot, "shifted"), (gain_two, "whole")],
        [((half_rows, width), f32), ((half_rows, width), bf16), ((8, width), f32)],
        row_tile,
        "back_own",
    )
    grad_attended_own, received_out, up_gx, gate_gl, up_gl, gate_gx = fence(grad_attended_own, received_out, up_gx, gate_gl, up_gl, gate_gx)
    grad_attended_far = over_core(grad_attended_own)
    up_gl = scatter(up_gl)
    gate_sum = add(own_grads[0], gate_gy, gate_gx)

    def down_body(left, right, others, outs):
        hidden_ref, received_ref = others

        def store(at, total):
            outs[0][:, at] = (hidden_ref[:, at] + total + received_ref[:, at].astype(f32)).astype(bf16)

        down_dot(left, right, store)

    (layer_rows,) = sum_rows_call(
        down_body,
        mine * tiles_half,
        products,
        downs,
        [(hidden, "plain"), (received_out, "plain")],
        [((half_rows, width), bf16)],
        row_tile,
        "down_own",
    )
    grad_attended_own, grad_attended_far, layer_rows, down_gl, gate_sum = fence(
        grad_attended_own, grad_attended_far, layer_rows, down_gl, gate_sum
    )

    pair_order = order.reshape(n_ctx, spans_dev // 2, 2)
    in_half = jnp.where(pair_order[..., 0] // (n_spans // 2) == core, pair_order[..., 0], pair_order[..., 1]) - core * (n_spans // 2)
    steps = jnp.arange(n_ctx, dtype=jnp.int32) ^ ctx
    send_places = in_half[steps].reshape(-1).astype(jnp.int32)
    my_order = lax.dynamic_slice_in_dim(span_order, ctx * spans_dev, spans_dev, 1)
    from_mine = (my_order // (n_spans // 2) == core).reshape(seq_dev, spans_dev // 2, 2, 1, 1)

    def to_slots(arranged):
        return [arranged[0], over_core(arranged[1]), over_x(arranged[2]), over_both(arranged[3])]

    def arrange(rows):
        arranged = span_copy(send_places, rows).reshape(n_ctx, -1, width)
        return [arranged[k] for k in range(n_ctx)]

    def from_slots(parts):
        parts = [p.reshape(spans_dev // 2, 1, SPAN, width) for p in parts]
        near = jnp.where(from_mine[seq], parts[0], parts[1])
        far = jnp.where(from_mine[1 - seq], parts[2], parts[3])
        near, far = near.reshape(local_len, width), far.reshape(local_len, width)
        return jnp.where(seq == 0, jnp.stack([near, far]), jnp.stack([far, near]))

    def sides(piece):
        return [piece, over_y(piece), over_x(piece), over_diagonal(piece)]

    def both_cores(side):
        return side + [over_core(a) for a in side]

    gate_sum = scatter(gate_sum)
    down_gl = over_diagonal(down_gl)
    grad_attended, grad_mixed = mixed_back(mine, grad_attended_own, grad_attended_far, w_out_rows)
    out_grads = [b.reshape(-1, width) for b in out_grad_blocks(place_at, mixed, grad_attended)]
    layer_parts = arrange(layer_rows)
    up_sum = add(own_grads[1], up_gy, up_gx)
    grad_mixed, out_grads, down_gl, layer_parts, up_sum, gate_gl, up_gl = fence(
        grad_mixed, out_grads, down_gl, layer_parts, up_sum, gate_gl, up_gl
    )

    def back_of(group, q_aug):
        return attend_back(group, 1, q_aug, keys, values, grad_mixed, mixed, cosine, sine)

    up_sum = scatter(up_sum)
    layer_parts = to_slots(layer_parts)
    both_gl = over_diagonal(jnp.concatenate([gate_gl, up_gl], axis=0))
    back_last = back_of(3, q_aug)
    down_sum = add(own_grads[2], down_gy, down_gx, down_gl)
    back_last, q_aug, layer_parts, gate_sum, both_gl, down_sum, out_grads = fence(
        back_last, q_aug, layer_parts, gate_sum, both_gl, down_sum, out_grads
    )
    qkv_last = qkv_grad(normed_t, *back_last)
    qkv_last, q_aug, down_sum = fence(qkv_last, q_aug, down_sum)

    qkv_last = over_diagonal(qkv_last)
    down_sum = scatter(down_sum)
    out_grads = [out_grads[0], over_y(out_grads[1]), over_x(out_grads[2]), over_diagonal(out_grads[3])]
    back_x = back_of(2, q_aug)
    back_x, q_aug, qkv_last, out_grads, up_sum = fence(back_x, q_aug, qkv_last, out_grads, up_sum)
    qkv_x = qkv_grad(normed_t, *back_x)
    out_sum = add(*out_grads)
    both_sum = add(jnp.concatenate([gate_sum, up_sum], axis=0), both_gl)
    qkv_x, out_sum, both_sum, q_aug = fence(qkv_x, out_sum, both_sum, q_aug)

    qkv_x = over_x(qkv_x)
    out_sum = scatter(out_sum)
    both_sides = sides(both_sum)
    back_y = back_of(1, q_aug)
    back_y, q_aug, qkv_x, both_sides, down_sum = fence(back_y, q_aug, qkv_x, both_sides, down_sum)
    qkv_y = qkv_grad(normed_t, *back_y)
    qkv_y, q_aug = fence(qkv_y, q_aug)

    qkv_y = over_y(qkv_y)
    both_pieces = both_cores(both_sides)
    back_own = back_of(0, q_aug)
    back_own, qkv_y, both_pieces, out_sum = fence(back_own, qkv_y, both_pieces, out_sum)

    in_lhs = [*back_own, *back_y, *back_x, *back_last]
    depth = w_qkv.shape[0]
    q_width, k_width = queries.shape[1], keys.shape[1]
    in_rhs = [(w_qkv, (depth, q_width), (0, 0))]
    in_rhs += [(w_qkv, (depth, k_width), (0, q_width // k_width + which)) for which in range(2)]
    received_in = over_core(partial_rows(in_lhs, in_rhs, in_dot, "in_other"))
    row_sides = sides(jnp.concatenate([down_sum, out_sum], axis=0))
    qkv_sum = add(qkv_grad(normed_t, *back_own), qkv_y, qkv_x, qkv_last)
    qkv_sum, received_in, row_sides = fence(qkv_sum, received_in, row_sides)
    qkv_sum = scatter(qkv_sum)

    def in_body(left, right, others, outs):
        received_ref, x_ref, grad_ref, gain_ref = others
        grad_normed = kept(in_dot, left, right) + received_ref[...].astype(f32)
        values_ = x_ref[...].astype(f32)
        scale_rows = rms_scale(values_)
        outs[0][...] = (grad_ref[...] + norm_back(grad_normed, values_, scale_rows, gain_ref[...])).astype(bf16)

        @pl.when(pl.program_id(0) == 0)
        def _():
            outs[1][...] = jnp.zeros(outs[1].shape, f32)

        outs[1][...] += column_sums(grad_normed * values_ * scale_rows)

    grad_rows, gain_one_sums = sum_rows_call(
        in_body,
        mine * tiles_half,
        in_lhs,
        in_rhs,
        [(received_in, "plain"), (x, "shifted"), (grad_hidden, "plain"), (gain_one, "whole")],
        [((half_rows, width), bf16), ((8, width), f32)],
        row_tile,
        "in_own",
    )
    sums = jnp.stack([gain_one_sums.sum(0), gain_two_sums.sum(0)])
    token_parts, sums, qkv_sum, row_sides = fence(arrange(grad_rows), sums, qkv_sum, row_sides)
    for step in (over_core, over_x, over_y):
        sums = sums + step(sums)
    total = lax.dynamic_slice_in_dim(sums, shard * gain_width, gain_width, 1)
    for step in range(1, n_shard):
        to = lax.dynamic_slice_in_dim(sums, (shard + step) % n_shard * gain_width, gain_width, 1)
        total = total + lax.ppermute(to, "shard", [(z, (z + step) % n_shard) for z in range(n_shard)])
    token_parts = to_slots(token_parts)
    where = jnp.stack([place, core]).astype(jnp.int32)
    qkv_pieces = both_cores(sides(qkv_sum))
    grad_w_gate = unit_columns(where, both_pieces, n_shard, 0)
    grad_w_up = unit_columns(where, both_pieces, n_shard, 1)
    grad_w_down, grad_w_out = unit_rows(where, both_cores(row_sides), unit_cols)
    layer_out = from_slots(layer_parts)
    grad_w_query, grad_w_key, grad_w_value = head_columns(where, qkv_pieces)
    grad_tokens = from_slots(token_parts)

    return (
        layer_out,
        grad_tokens,
        total[0],
        grad_w_query,
        grad_w_key,
        grad_w_value,
        grad_w_out,
        total[1],
        grad_w_gate,
        grad_w_up,
        grad_w_down,
    )


def rope_tables(positions):
    half_dim = HEAD_DIM // 2
    frequency = rope_base ** (-2.0 * jnp.arange(half_dim, dtype=jnp.float32) / HEAD_DIM)
    angles = positions.astype(jnp.float32)[..., None] * frequency
    return (jnp.cos(angles), jnp.sin(angles))


def rotate(values, cosine, sine_table):
    half_dim = values.shape[-1] // 2
    first_half = values[..., :half_dim]
    second_half = values[..., half_dim:]
    cosine = cosine[..., None, :]
    sine_table = sine_table[..., None, :]
    return jnp.concatenate(
        [
            first_half * cosine - second_half * sine_table,
            second_half * cosine + first_half * sine_table,
        ],
        axis=-1,
    )


def general_layer(
    tokens,
    span_order,
    token_positions,
    attn_gain,
    w_query,
    w_key,
    w_value,
    w_out,
    mlp_gain,
    w_gate,
    w_up,
    w_down,
    cotangent,
):
    seq_dev, local_len, model_width = tokens.shape
    row_count = seq_dev * local_len
    groups = HEADS // KV_HEADS
    kv_width = KV_HEADS * HEAD_DIM
    score_scale = HEAD_DIM ** (-0.5)
    full_len = local_len * lax.axis_size("ctx")
    ctx_index = lax.axis_index("ctx")
    slot_index = jnp.arange(full_len, dtype=jnp.int32)
    key_index = span_order[:, slot_index // SPAN] * SPAN + slot_index[None, :] % SPAN
    query_index = lax.dynamic_slice_in_dim(key_index, ctx_index * local_len, local_len, 1)
    allowed = query_index[:, :, None] >= key_index[:, None, :]
    cosine, sine_table = rope_tables(token_positions)
    gain_one, wq_full, wk_full, wv_full, wo_full = (
        lax.all_gather(attn_gain, "shard", axis=0, tiled=True),
        lax.all_gather(w_query, "shard", axis=0, tiled=True),
        lax.all_gather(w_key, "shard", axis=0, tiled=True),
        lax.all_gather(w_value, "shard", axis=0, tiled=True),
        lax.all_gather(w_out, "shard", axis=0, tiled=True),
    )
    x_rows = tokens.reshape(row_count, model_width).astype(jnp.float32)
    scale_one = rms_scale(x_rows)
    normed = (x_rows * scale_one * gain_one).astype(jnp.bfloat16)
    queries = rotate(
        matmul(normed, wq_full).reshape(seq_dev, local_len, HEADS, HEAD_DIM), cosine, sine_table
    ).astype(jnp.bfloat16)
    keys_local = rotate(
        matmul(normed, wk_full).reshape(seq_dev, local_len, KV_HEADS, HEAD_DIM), cosine, sine_table
    ).astype(jnp.bfloat16)
    values_local = matmul(normed, wv_full).astype(jnp.bfloat16)
    keys_all, values_all = (
        lax.all_gather(keys_local.reshape(seq_dev, local_len, kv_width), "ctx", axis=1, tiled=True),
        lax.all_gather(
            values_local.reshape(seq_dev, local_len, kv_width), "ctx", axis=1, tiled=True
        ),
    )
    query_heads = queries.reshape(seq_dev, local_len, KV_HEADS, groups, HEAD_DIM).transpose(
        2, 0, 1, 3, 4
    )
    key_heads = keys_all.reshape(seq_dev, full_len, KV_HEADS, HEAD_DIM).transpose(2, 0, 1, 3)
    value_heads = values_all.reshape(seq_dev, full_len, KV_HEADS, HEAD_DIM).transpose(2, 0, 1, 3)

    def scores_of(query_head, key_head):
        raw_scores = (
            jnp.einsum("sqjd,skd->sjqk", query_head, key_head, preferred_element_type=jnp.float32)
            * score_scale
        )
        return jnp.where(allowed[:, None], raw_scores, masked_value)

    def attend_head(pieces):
        query_head, key_head, value_head = pieces
        scores = scores_of(query_head, key_head)
        row_max = jnp.max(scores, axis=-1, keepdims=True)
        exponent = jnp.exp(scores - row_max)
        row_total = jnp.sum(exponent, axis=-1, keepdims=True)
        probabilities = (exponent / row_total).astype(jnp.bfloat16)
        mixed_head = jnp.einsum(
            "sjqk,skd->sqjd", probabilities, value_head, preferred_element_type=jnp.float32
        )
        return (mixed_head, row_max[..., 0] + jnp.log(row_total[..., 0]))

    mixed_heads, log_totals = lax.map(attend_head, (query_heads, key_heads, value_heads))
    mixed_low = (
        mixed_heads.transpose(1, 2, 0, 3, 4).reshape(row_count, model_width).astype(jnp.bfloat16)
    )
    hidden = x_rows + matmul(mixed_low, wo_full)
    scale_two = rms_scale(hidden)
    gain_two, wg_full, wu_full, wd_full = (
        lax.all_gather(mlp_gain, "shard", axis=0, tiled=True),
        lax.all_gather(w_gate, "shard", axis=0, tiled=True),
        lax.all_gather(w_up, "shard", axis=0, tiled=True),
        lax.all_gather(w_down, "shard", axis=0, tiled=True),
    )
    normed_two = (hidden * scale_two * gain_two).astype(jnp.bfloat16)
    gate_pre = matmul(normed_two, wg_full)
    up_pre = matmul(normed_two, wu_full)
    sigmoid_gate = jax.nn.sigmoid(gate_pre)
    activated = gate_pre * sigmoid_gate
    product = (activated * up_pre).astype(jnp.bfloat16)
    layer_out = (hidden + matmul(product, wd_full)).astype(jnp.bfloat16).reshape(tokens.shape)
    grad_out = cotangent.reshape(row_count, model_width)
    gain_two_back, wg_back, wu_back, wd_back = (
        lax.all_gather(mlp_gain, "shard", axis=0, tiled=True),
        lax.all_gather(w_gate, "shard", axis=0, tiled=True),
        lax.all_gather(w_up, "shard", axis=0, tiled=True),
        lax.all_gather(w_down, "shard", axis=0, tiled=True),
    )
    grad_product = matmul(grad_out, wd_back.T)
    grad_w_down = matmul(product.T, grad_out)
    grad_gate = (
        grad_product * up_pre * sigmoid_gate * (1.0 + gate_pre * (1.0 - sigmoid_gate))
    ).astype(jnp.bfloat16)
    grad_up = (grad_product * activated).astype(jnp.bfloat16)
    grad_w_gate = matmul(normed_two.T, grad_gate)
    grad_w_up = matmul(normed_two.T, grad_up)
    grad_normed_two = matmul(grad_gate, wg_back.T) + matmul(grad_up, wu_back.T)
    gain_two_f = gain_two_back.astype(jnp.float32)
    grad_mlp_gain = jnp.sum(grad_normed_two * hidden * scale_two, axis=0)
    grad_hidden = grad_out.astype(jnp.float32) + norm_back(
        grad_normed_two, hidden, scale_two, gain_two_f
    )
    gain_one_back, wq_back, wk_back, wv_back, wo_back = (
        lax.all_gather(attn_gain, "shard", axis=0, tiled=True),
        lax.all_gather(w_query, "shard", axis=0, tiled=True),
        lax.all_gather(w_key, "shard", axis=0, tiled=True),
        lax.all_gather(w_value, "shard", axis=0, tiled=True),
        lax.all_gather(w_out, "shard", axis=0, tiled=True),
    )
    grad_attended = grad_hidden.astype(jnp.bfloat16)
    grad_w_out = matmul(mixed_low.T, grad_attended)
    grad_mixed = matmul(grad_attended, wo_back.T).astype(jnp.bfloat16)
    grad_heads = grad_mixed.reshape(seq_dev, local_len, KV_HEADS, groups, HEAD_DIM).transpose(
        2, 0, 1, 3, 4
    )

    def attend_back(pieces):
        query_head, key_head, value_head, grad_head, log_total = pieces
        scores = scores_of(query_head, key_head)
        probabilities = jnp.exp(scores - log_total[..., None])
        grad_probs = jnp.einsum(
            "sqjd,skd->sjqk", grad_head, value_head, preferred_element_type=jnp.float32
        )
        inner_sum = jnp.sum(probabilities * grad_probs, axis=-1, keepdims=True)
        grad_scores = (probabilities * (grad_probs - inner_sum)).astype(jnp.bfloat16)
        grad_query = (
            jnp.einsum("sjqk,skd->sqjd", grad_scores, key_head, preferred_element_type=jnp.float32)
            * score_scale
        )
        grad_key = (
            jnp.einsum(
                "sjqk,sqjd->skd", grad_scores, query_head, preferred_element_type=jnp.float32
            )
            * score_scale
        )
        grad_value = jnp.einsum(
            "sjqk,sqjd->skd",
            probabilities.astype(jnp.bfloat16),
            grad_head,
            preferred_element_type=jnp.float32,
        )
        return (grad_query, grad_key, grad_value)

    grad_queries, key_terms, value_terms = lax.map(
        attend_back, (query_heads, key_heads, value_heads, grad_heads, log_totals)
    )
    key_terms = key_terms.transpose(1, 2, 0, 3).reshape(seq_dev, full_len, kv_width)
    value_terms = value_terms.transpose(1, 2, 0, 3).reshape(seq_dev, full_len, kv_width)
    grad_keys, grad_values = (
        lax.psum_scatter(
            key_terms.astype(jnp.bfloat16), "ctx", scatter_dimension=1, tiled=True
        ).astype(jnp.float32),
        lax.psum_scatter(
            value_terms.astype(jnp.bfloat16), "ctx", scatter_dimension=1, tiled=True
        ).astype(jnp.float32),
    )
    grad_queries = grad_queries.transpose(1, 2, 0, 3, 4).reshape(
        seq_dev, local_len, HEADS, HEAD_DIM
    )
    grad_q_low = (
        rotate(grad_queries, cosine, -sine_table)
        .reshape(row_count, model_width)
        .astype(jnp.bfloat16)
    )
    grad_k_low = (
        rotate(grad_keys.reshape(seq_dev, local_len, KV_HEADS, HEAD_DIM), cosine, -sine_table)
        .reshape(row_count, kv_width)
        .astype(jnp.bfloat16)
    )
    grad_v_low = grad_values.reshape(row_count, kv_width).astype(jnp.bfloat16)
    grad_w_query = matmul(normed.T, grad_q_low)
    grad_w_key = matmul(normed.T, grad_k_low)
    grad_w_value = matmul(normed.T, grad_v_low)
    grad_normed = (
        matmul(grad_q_low, wq_back.T)
        + matmul(grad_k_low, wk_back.T)
        + matmul(grad_v_low, wv_back.T)
    )
    gain_one_f = gain_one_back.astype(jnp.float32)
    grad_attn_gain = jnp.sum(grad_normed * x_rows * scale_one, axis=0)
    grad_tokens = (grad_hidden + norm_back(grad_normed, x_rows, scale_one, gain_one_f)).astype(
        jnp.bfloat16
    )
    grad_tokens = grad_tokens.reshape(tokens.shape)
    part_gain_two, part_gate, part_up, part_down = (
        lax.psum_scatter(
            grad_mlp_gain.astype(jnp.bfloat16), "shard", scatter_dimension=0, tiled=True
        ).astype(jnp.float32),
        lax.psum_scatter(
            grad_w_gate.astype(jnp.bfloat16), "shard", scatter_dimension=0, tiled=True
        ).astype(jnp.float32),
        lax.psum_scatter(
            grad_w_up.astype(jnp.bfloat16), "shard", scatter_dimension=0, tiled=True
        ).astype(jnp.float32),
        lax.psum_scatter(
            grad_w_down.astype(jnp.bfloat16), "shard", scatter_dimension=0, tiled=True
        ).astype(jnp.float32),
    )
    part_gain_one, part_query, part_key, part_value, part_out = (
        lax.psum_scatter(
            grad_attn_gain.astype(jnp.bfloat16), "shard", scatter_dimension=0, tiled=True
        ).astype(jnp.float32),
        lax.psum_scatter(
            grad_w_query.astype(jnp.bfloat16), "shard", scatter_dimension=0, tiled=True
        ).astype(jnp.float32),
        lax.psum_scatter(
            grad_w_key.astype(jnp.bfloat16), "shard", scatter_dimension=0, tiled=True
        ).astype(jnp.float32),
        lax.psum_scatter(
            grad_w_value.astype(jnp.bfloat16), "shard", scatter_dimension=0, tiled=True
        ).astype(jnp.float32),
        lax.psum_scatter(
            grad_w_out.astype(jnp.bfloat16), "shard", scatter_dimension=0, tiled=True
        ).astype(jnp.float32),
    )
    summed = (
        lax.psum(part_gain_one.astype(jnp.bfloat16), ("ctx", "batch")).astype(jnp.float32),
        lax.psum(part_query.astype(jnp.bfloat16), ("ctx", "batch")).astype(jnp.float32),
        lax.psum(part_key.astype(jnp.bfloat16), ("ctx", "batch")).astype(jnp.float32),
        lax.psum(part_value.astype(jnp.bfloat16), ("ctx", "batch")).astype(jnp.float32),
        lax.psum(part_out.astype(jnp.bfloat16), ("ctx", "batch")).astype(jnp.float32),
        lax.psum(part_gain_two.astype(jnp.bfloat16), ("ctx", "batch")).astype(jnp.float32),
        lax.psum(part_gate.astype(jnp.bfloat16), ("ctx", "batch")).astype(jnp.float32),
        lax.psum(part_up.astype(jnp.bfloat16), ("ctx", "batch")).astype(jnp.float32),
        lax.psum(part_down.astype(jnp.bfloat16), ("ctx", "batch")).astype(jnp.float32),
    )
    return (
        layer_out,
        grad_tokens,
        summed[0],
        summed[1],
        summed[2],
        summed[3],
        summed[4],
        summed[5],
        summed[6],
        summed[7],
        summed[8],
    )


def fits(mesh):
    split = mesh.shape["ctx"] // 2
    return split == 2 and mesh.shape["batch"] == 2 and mesh.shape["shard"] * split == KV_HEADS and mesh.shape["shard"] == 4


def solution(mesh):
    in_specs = (
        P(("shard", "batch"), "ctx", None),
        P(("shard", "batch"), None),
        P(("shard", "batch"), "ctx"),
        P("shard"),
        P("shard", None),
        P("shard", None),
        P("shard", None),
        P("shard", None),
        P("shard"),
        P("shard", None),
        P("shard", None),
        P("shard", None),
        P(("shard", "batch"), "ctx", None),
    )
    out_specs = (
        P(("shard", "batch"), "ctx", None),
        P(("shard", "batch"), "ctx", None),
        P("shard"),
        P("shard", None),
        P("shard", None),
        P("shard", None),
        P("shard", None),
        P("shard"),
        P("shard", None),
        P("shard", None),
        P("shard", None),
    )
    layer = chip_layer if fits(mesh) else general_layer
    return jax.shard_map(layer, mesh=mesh, in_specs=in_specs, out_specs=out_specs, check_vma=False)
```

```python
import functools

import jax
import jax.numpy as jnp
import numpy as np
from jax import lax
from jax.experimental import pallas as pl
from jax.experimental.pallas import tpu as pltpu
from jax.sharding import PartitionSpec as P

HEADS = 16
KV_HEADS = 8
HEAD_DIM = 96
SPAN = 128
GROUPS = HEADS // KV_HEADS
HALF = HEAD_DIM // 2
LANES = 128
SLOT = LANES // 2
GROUP_COLS = (GROUPS + 2) * HEAD_DIM
Q_COLS = GROUPS * HEAD_DIM
Q_LANES = GROUPS * LANES
PAD_ROWS = 16

norm_eps = 1e-05
rope_base = 100000.0
masked_value = -1e30
score_scale = HEAD_DIM ** (-0.5)
exp2_scale = score_scale * 1.4426950408889634

bf16 = jnp.bfloat16
f32 = jnp.float32
MIB = 1 << 20
NT = (((1,), (1,)), ((), ()))
TN = (((0,), (0,)), ((), ()))


def rms_scale(values):
    return lax.rsqrt(jnp.mean(values * values, axis=-1, keepdims=True) + norm_eps)


def matmul(left, right):
    return jnp.dot(left, right, preferred_element_type=f32)


def dot_nt(left, right):
    return lax.dot_general(left, right, NT, preferred_element_type=f32)


def dot_tn(left, right):
    return lax.dot_general(left, right, TN, preferred_element_type=f32)


def params(limit):
    return pltpu.CompilerParams(vmem_limit_bytes=limit * MIB)


def short():
    return pl.CostEstimate(flops=1000, bytes_accessed=1000, transcendentals=0)


def whole(shape):
    return pl.BlockSpec(shape, lambda *_: (0,) * len(shape))


def part(block, index):
    return pl.BlockSpec(block, lambda *_: index, pipeline_mode=pl.Buffered(1))


def fixed(shape):
    return part(shape, (0,) * len(shape))


def call(kernel, grid, in_specs, out_specs, out_shape, operands, name, prefetch=(), scratch=(), limit=60):
    return pl.pallas_call(
        kernel,
        grid_spec=pltpu.PrefetchScalarGridSpec(
            num_scalar_prefetch=len(prefetch), grid=grid, in_specs=in_specs, out_specs=out_specs, scratch_shapes=list(scratch)
        ),
        out_shape=[jax.ShapeDtypeStruct(shape, dtype) for shape, dtype in out_shape],
        compiler_params=params(limit),
        cost_estimate=short(),
        name=name,
    )(*prefetch, *operands)


def spread_matrix():
    spread = np.zeros((GROUP_COLS, (GROUPS + 2) * LANES), np.float32)
    for row in range(spread.shape[0]):
        head, feature = divmod(row, HEAD_DIM)
        half, place = divmod(feature, HALF)
        spread[row, head * LANES + half * SLOT + place] = 1.0
    return spread


def front_kernel(near_ref, far_ref, flag_ref, *refs):
    spans = 4
    near, far, refs = refs[:spans], refs[spans : 2 * spans], refs[2 * spans :]
    cos_ref, sin_ref, gain_ref, spread_ref, w0, w1, w2, w3a, w3b, x_out, n_out, nt_out, q_out, k_out, v_out, w_out = refs
    q_width, k_width = q_out.shape[1], k_out.shape[1]
    step_at = pl.program_id(0)

    @pl.when(step_at == 0)
    def _():
        depth = w0.shape[1]
        halves = w3a.shape[0]
        for at, piece in enumerate((w0, w1, w2, None)):
            for z in range(w0.shape[0]):
                block = piece[z] if piece is not None else (w3a[z] if z < halves else w3b[z - halves])
                spread = matmul(block, spread_ref[...]).astype(bf16)
                rows = slice(z * depth, (z + 1) * depth)
                w_out[rows, Q_LANES * at : Q_LANES * (at + 1)] = spread[:, :Q_LANES]
                w_out[rows, q_width + LANES * at : q_width + LANES * (at + 1)] = spread[:, Q_LANES : Q_LANES + LANES]
                at_v = q_width + k_width + LANES * at
                w_out[rows, at_v : at_v + LANES] = spread[:, Q_LANES + LANES :]

    for k in range(spans):
        rows = slice(k * SPAN, (k + 1) * SPAN)

        @pl.when(flag_ref[spans * step_at + k] == 0)
        def _():
            x_out[rows, :] = near[k][0]

        @pl.when(flag_ref[spans * step_at + k] != 0)
        def _():
            x_out[rows, :] = far[k][0]

    x = x_out[...].astype(f32)
    normed = (x * rms_scale(x) * gain_ref[...]).astype(bf16)
    n_out[...] = normed
    nt_out[...] = normed.T
    cosine, sine = cos_ref[...], sin_ref[...]
    lane = lax.broadcasted_iota(jnp.int32, (1, LANES), 1)
    ones = jnp.where((lane >= HALF) & (lane < HALF + 3), 1.0, 0.0)
    step = 4 * LANES
    for start in range(0, w_out.shape[1], step):
        raw = matmul(normed, w_out[:, start : start + step])
        for piece in range(0, step, LANES):
            at = start + piece
            head = raw[:, piece : piece + LANES]
            if at < q_width + k_width:
                head = head * cosine + pltpu.roll(head, SLOT, 1) * sine
            if at < q_width:
                q_out[:, at : at + LANES] = head.astype(bf16)
            elif at < q_width + k_width:
                k_out[:, at - q_width : at - q_width + LANES] = (head + ones).astype(bf16)
            else:
                v_out[:, at - q_width - k_width : at - q_width - k_width + LANES] = (head + ones).astype(bf16)


def span_specs(width, count):
    def near(k):
        return pl.BlockSpec((1, SPAN, width), lambda i, near, far, flag: (near[count * i + k], 0, 0))

    def far(k):
        return pl.BlockSpec((1, SPAN, width), lambda i, near, far, flag: (far[count * i + k], 0, 0))

    return [near(k) for k in range(count)] + [far(k) for k in range(count)]


def as_spans(array):
    return array.reshape(array.shape[0] // SPAN, SPAN, array.shape[1])


def front(places, near, far, cosine, sine, gain, pieces):
    rows, width = 2 * near.shape[0], near.shape[1]
    groups = len(pieces) - 1
    n_shard = pieces[0].shape[0]
    depth = width // n_shard
    spread = jnp.asarray(spread_matrix(), bf16)
    spans = 4
    tile = spans * SPAN
    q_width, k_width = groups * Q_LANES, groups * LANES
    total = q_width + 2 * k_width

    def rows_spec(cols):
        return pl.BlockSpec((tile, cols), lambda i, *_: (i, 0))

    near, far = as_spans(near), as_spans(far)
    return call(
        front_kernel,
        (rows // tile,),
        span_specs(width, spans)
        + [rows_spec(LANES), rows_spec(LANES), fixed(gain.shape), fixed(spread.shape)]
        + [part((p.shape[0], depth, p.shape[2]), (0, 0, 0)) for p in pieces],
        [rows_spec(width), rows_spec(width), pl.BlockSpec((width, tile), lambda i, *_: (0, i))]
        + [rows_spec(q_width), rows_spec(k_width), rows_spec(k_width), whole((n_shard * depth, total))],
        [
            ((rows, width), bf16),
            ((rows, width), bf16),
            ((width, rows), bf16),
            ((rows, q_width), bf16),
            ((rows, k_width), bf16),
            ((rows, k_width), bf16),
            ((n_shard * depth, total), bf16),
        ],
        [near] * spans + [far] * spans + [cosine, sine, gain, spread, *pieces],
        "front",
        places,
    )


def span_copy(places, source):
    width = source.shape[1]
    count = places.shape[0]

    def kernel(place_ref, x_ref, o_ref):
        o_ref[...] = x_ref[...]

    (out,) = call(
        kernel,
        (count,),
        [pl.BlockSpec((1, SPAN, width), lambda i, place: (place[i], 0, 0))],
        [pl.BlockSpec((1, SPAN, width), lambda i, place: (i, 0, 0))],
        [((count, SPAN, width), source.dtype)],
        [as_spans(source)],
        "span_copy",
        [places],
    )
    return out.reshape(count * SPAN, width)


def span_join(places, near, far):
    width = near.shape[1]
    count = 2 * near.shape[0] // SPAN

    def kernel(near_ref, far_ref, flag_ref, a_ref, b_ref, o_ref):
        @pl.when(flag_ref[pl.program_id(0)] == 0)
        def _():
            o_ref[...] = a_ref[...]

        @pl.when(flag_ref[pl.program_id(0)] != 0)
        def _():
            o_ref[...] = b_ref[...]

    (out,) = call(
        kernel,
        (count,),
        span_specs(width, 1),
        [pl.BlockSpec((1, SPAN, width), lambda i, *_: (i, 0, 0))],
        [((count, SPAN, width), near.dtype)],
        [as_spans(near), as_spans(far)],
        "span_join",
        places,
    )
    return out.reshape(count * SPAN, width)


def three_parts(values):
    first = values.astype(bf16).astype(f32)
    second = (values - first).astype(bf16).astype(f32)
    third = values - first - second
    return first, second, third


def with_lanes(block, column):
    lane = lax.broadcasted_iota(jnp.int32, block.shape, 1)
    first, second, third = three_parts(column)
    wide = block.astype(f32)
    wide = jnp.where(lane == HALF, first, wide)
    wide = jnp.where(lane == HALF + 1, second, wide)
    wide = jnp.where(lane == HALF + 2, third, wide)
    return wide.astype(bf16)


Q_TILE = 256
K_CHUNK = 512


def heads_down(block):
    return jnp.concatenate([block[:, LANES * h : LANES * (h + 1)] for h in range(GROUPS)], axis=0)


def attend_kernel(q_ref, k_ref, v_ref, mixed_ref, q_aug_ref):
    rows = q_ref.shape[0]
    for tile in range(rows // Q_TILE):
        first_row = tile * Q_TILE
        query = heads_down(q_ref[first_row : first_row + Q_TILE, :])
        end = first_row + Q_TILE
        top = acc = None
        for start in range(0, end, K_CHUNK):
            size = min(K_CHUNK, end - start)
            key = k_ref[start : start + size, :]
            value = v_ref[start : start + size, :]
            scores = dot_nt(query, key)
            if start + size > first_row:
                row = lax.broadcasted_iota(jnp.int32, (Q_TILE, size), 0) + first_row
                column = lax.broadcasted_iota(jnp.int32, (Q_TILE, size), 1) + start
                allowed = row >= column
                scores = jnp.where(jnp.concatenate([allowed] * GROUPS, axis=0), scores, masked_value)
            chunk_top = jnp.max(scores, axis=-1, keepdims=True)
            new_top = chunk_top if top is None else jnp.maximum(top, chunk_top)
            weights = jnp.exp2((scores - new_top) * exp2_scale).astype(bf16)
            part = matmul(weights, value)
            acc = part if top is None else acc * jnp.exp2((top - new_top) * exp2_scale) + part
            top = new_top
        total = acc[:, HALF : HALF + 1]
        mixed = (acc * (1.0 / total)).astype(bf16)
        log_total = top + jnp.log2(total) * (1.0 / exp2_scale)
        marked = with_lanes(query, -log_total)
        for h in range(GROUPS):
            mixed_ref[first_row : first_row + Q_TILE, LANES * h : LANES * (h + 1)] = mixed[Q_TILE * h : Q_TILE * (h + 1)]
            q_aug_ref[first_row : first_row + Q_TILE, LANES * h : LANES * (h + 1)] = marked[Q_TILE * h : Q_TILE * (h + 1)]


def attend(queries, keys, values):
    rows, k_width = keys.shape
    groups = k_width // LANES
    pair = pl.BlockSpec((rows, Q_LANES), lambda g: (0, g))
    single = pl.BlockSpec((rows, LANES), lambda g: (0, g))
    return call(
        attend_kernel, (groups,), [pair, single, single], [pair, pair], [(queries.shape, bf16)] * 2, [queries, keys, values], "attend"
    )


def attend_back_kernel(q_ref, k_ref, v_ref, do_ref, o_ref, cos_ref, sin_ref, dq_ref, dk_ref, dv_ref, q_s, do_s, dq_s, dk_s, dv_s):
    rows = q_ref.shape[0]
    tiles = rows // Q_TILE
    for tile in range(tiles):
        at = slice(tile * Q_TILE, (tile + 1) * Q_TILE)
        q_s[tile] = heads_down(q_ref[at, :])
        grad = heads_down(do_ref[at, :])
        inner = jnp.sum(grad.astype(f32) * heads_down(o_ref[at, :]).astype(f32), axis=-1, keepdims=True)
        do_s[tile] = with_lanes(grad, -inner)
        dq_s[tile] = jnp.zeros(dq_s.shape[1:], f32)

    def unit(tile, key_start, size, mask_from):
        key = k_ref[key_start : key_start + size, :]
        value = v_ref[key_start : key_start + size, :]
        query, grad = q_s[tile], do_s[tile]
        probs = jnp.exp2(dot_nt(key, query) * exp2_scale)
        if mask_from is not None:
            row = lax.broadcasted_iota(jnp.int32, (size, Q_TILE), 0)
            column = lax.broadcasted_iota(jnp.int32, (size, Q_TILE), 1) + mask_from
            allowed = jnp.concatenate([row <= column] * GROUPS, axis=1)
            probs = jnp.where(allowed, probs, 0.0)
        d_scores = (probs * dot_nt(value, grad)).astype(bf16)
        dv_s[:size] += matmul(probs.astype(bf16), grad)
        dk_s[:size] += matmul(d_scores, query)
        dq_s[tile] += dot_tn(d_scores, key)

    for key_start in range(0, rows, K_CHUNK):
        dk_s[...] = jnp.zeros(dk_s.shape, f32)
        dv_s[...] = jnp.zeros(dv_s.shape, f32)
        tile = key_start // Q_TILE
        unit(tile, key_start, Q_TILE, 0)
        unit(tile + 1, key_start, K_CHUNK, Q_TILE)
        if tile + 2 < tiles:

            @pl.loop(tile + 2, tiles)
            def _(later):
                unit(later, key_start, K_CHUNK, None)

        at = slice(key_start, key_start + K_CHUNK)
        turned = dk_s[...] * score_scale
        turned = turned * cos_ref[at, :] - pltpu.roll(turned, SLOT, 1) * sin_ref[at, :]
        dk_ref[at, :] = turned.astype(bf16)
        dv_ref[at, :] = dv_s[...].astype(bf16)
    for tile in range(tiles):
        at = slice(tile * Q_TILE, (tile + 1) * Q_TILE)
        cosine, sine = cos_ref[at, :], sin_ref[at, :]
        for h in range(GROUPS):
            turned = dq_s[tile, Q_TILE * h : Q_TILE * (h + 1), :] * score_scale
            turned = turned * cosine - pltpu.roll(turned, SLOT, 1) * sine
            dq_ref[at, LANES * h : LANES * (h + 1)] = turned.astype(bf16)


def attend_back(first, groups, q_aug, keys, values, grad, mixed, cosine, sine):
    rows = keys.shape[0]
    tiles = rows // Q_TILE
    pair = pl.BlockSpec((rows, Q_LANES), lambda g: (0, g + first))
    single = pl.BlockSpec((rows, LANES), lambda g: (0, g + first))
    pair_out = pl.BlockSpec((rows, Q_LANES), lambda g: (0, g))
    single_out = pl.BlockSpec((rows, LANES), lambda g: (0, g))
    stacked = (tiles, GROUPS * Q_TILE, LANES)
    table = fixed((rows, LANES))
    return call(
        attend_back_kernel,
        (groups,),
        [pair, single, single, pair, pair, table, table],
        [pair_out, single_out, single_out],
        [((rows, groups * Q_LANES), bf16), ((rows, groups * LANES), bf16), ((rows, groups * LANES), bf16)],
        [q_aug, keys, values, grad, mixed, cosine, sine],
        "attend_back",
        scratch=[
            pltpu.VMEM(stacked, bf16),
            pltpu.VMEM(stacked, bf16),
            pltpu.VMEM(stacked, f32),
            pltpu.VMEM((K_CHUNK, LANES), f32),
            pltpu.VMEM((K_CHUNK, LANES), f32),
        ],
    )


def flat(block):
    return block.reshape(block.shape[0] * block.shape[1], block.shape[2])


def down_columns(down_ref, j, zs):
    rows = down_ref.shape[1] // 3
    return jnp.concatenate([down_ref[z, rows * j : rows * (j + 1), :] for z in zs], axis=0)


def hidden_kernel(n_ref, cot_ref, gate_ref, up_ref, down_ref, product_ref, dboth_ref):
    n_shard, units = gate_ref.shape[0], gate_ref.shape[2]
    third = cot_ref.shape[1] // 3
    step = 256
    for start in range(0, units, step):
        at = slice(start, start + step)
        zs = range(start * n_shard // units, (start + step) * n_shard // units)
        gate = matmul(n_ref[...], flat(gate_ref[:, :, at]))
        up = matmul(n_ref[...], flat(up_ref[:, :, at]))
        d_product = sum(dot_nt(cot_ref[:, third * j : third * (j + 1)], down_columns(down_ref, j, zs)) for j in range(3))
        sigmoid = 1.0 / (1.0 + jnp.exp(-gate))
        silu = gate * sigmoid
        product_ref[:, at] = (silu * up).astype(bf16)
        dboth_ref[:, at] = (d_product * up * sigmoid * (1.0 + gate * (1.0 - sigmoid))).astype(bf16)
        dboth_ref[:, units + start : units + start + step] = (d_product * silu).astype(bf16)


def feed_grads(normed_t, cot, product, d_both):
    width, rows = normed_t.shape
    units = product.shape[1]
    steps = width // units

    def kernel(n_ref, cot_ref, product_ref, both_ref, gate_ref, up_ref, down_ref, turned_ref):
        step = pl.program_id(0)

        @pl.when(step < steps)
        def _():
            gate_ref[...] = matmul(n_ref[...], both_ref[:, :units]).astype(bf16)
            up_ref[...] = matmul(n_ref[...], both_ref[:, units:]).astype(bf16)

        @pl.when(step == steps)
        def _():
            turned_ref[...] = product_ref[...].T

        @pl.when(step >= steps)
        def _():
            down_ref[...] = matmul(turned_ref[...], cot_ref[...]).astype(bf16)

    early = lambda i: (jnp.minimum(i, steps - 1), 0)
    late = lambda i: (0, jnp.maximum(i - steps, 0))
    return call(
        kernel,
        (2 * steps,),
        [pl.BlockSpec((units, rows), early), pl.BlockSpec((rows, units), late), fixed(product.shape), fixed(d_both.shape)],
        [pl.BlockSpec((units, units), early), pl.BlockSpec((units, units), early), pl.BlockSpec((units, units), late)],
        [((width, units), bf16), ((width, units), bf16), ((units, width), bf16)],
        [normed_t, cot, product, d_both],
        "feed_grads",
        scratch=[pltpu.VMEM((units, rows), bf16)],
    )


def whole_of(array):
    return array, array.shape, (0,) * array.ndim


def third_of(array, index):
    rows = 384
    return array, (array.shape[0], rows, array.shape[2]), (0, index, 0)


def hidden_units(normed, cot, weights):
    rows, width = normed.shape
    units = weights[0][0].shape[2]
    tile = 512
    wide = pl.BlockSpec((tile, width), lambda i: (i, 0))
    thin = pl.BlockSpec((tile, units), lambda i: (i, 0))
    return call(
        hidden_kernel,
        (rows // tile,),
        [wide, wide] + [part(block, index) for _, block, index in weights],
        [thin, pl.BlockSpec((tile, 2 * units), lambda i: (i, 0))],
        [((rows, units), bf16), ((rows, 2 * units), bf16)],
        [normed, cot] + [a for a, _, _ in weights],
        "hidden_units",
    )


def sum_rows_call(body, base, lhs, rhs, others, outs, tile, name):
    rows = outs[0][0][0]

    def shifted(cols):
        return pl.BlockSpec((tile, cols), lambda i, base: (base[0] + i, 0))

    def plain(cols):
        return pl.BlockSpec((tile, cols), lambda i, base: (i, 0))

    in_specs = [shifted(a.shape[1]) for a in lhs] + [part(block, index) for _, block, index in rhs]
    for a, kind in others:
        in_specs.append(fixed(a.shape) if kind == "whole" else {"shifted": shifted, "plain": plain}[kind](a.shape[1]))
    out_specs = [plain(shape[1]) if shape[0] == rows else whole(shape) for shape, _ in outs]
    n_lhs, n_rhs, n_other = len(lhs), len(rhs), len(others)

    def kernel(base_ref, *refs):
        left, refs = refs[:n_lhs], refs[n_lhs:]
        right, refs = refs[:n_rhs], refs[n_rhs:]
        body(left, right, refs[:n_other], refs[n_other:])

    return call(
        kernel,
        (rows // tile,),
        in_specs,
        out_specs,
        outs,
        [*lhs, *[a for a, _, _ in rhs], *[a for a, _ in others]],
        name,
        [base],
    )


def norm_back(grad_normed, values, scale_rows, gain):
    scaled = grad_normed * gain
    return scale_rows * scaled - values * (scale_rows * scale_rows * scale_rows) * jnp.mean(scaled * values, axis=-1, keepdims=True)


def column_sums(values):
    return jnp.sum(values.reshape(-1, 8, values.shape[-1]), axis=0)


def half_specs(tile, tiles, width):
    own = pl.BlockSpec((tile, width), lambda i, core: (jnp.clip(i - tiles * core[0], 0, tiles - 1), 0))
    far = pl.BlockSpec((tile, width), lambda i, core: (jnp.clip(i - tiles * (1 - core[0]), 0, tiles - 1), 0))
    return [own, far]


def place_half(core_ref, tiles, own_refs, far_refs, out_ref):
    is_own = pl.program_id(0) // tiles == core_ref[0]

    def place(refs):
        start = 0
        for ref in refs:
            out_ref[:, start : start + ref.shape[1]] = ref[...]
            start += ref.shape[1]

    @pl.when(is_own)
    def _():
        place(own_refs)

    @pl.when(jnp.logical_not(is_own))
    def _():
        place(far_refs)


def join_halves(core, own, far):
    rows, cols = own[0].shape
    count = len(own)
    width = count * cols
    tile = 256
    tiles = rows // tile

    def kernel(core_ref, *refs):
        out_ref, turned_ref = refs[2 * count :]
        place_half(core_ref, tiles, refs[:count], refs[count : 2 * count], out_ref)
        turned_ref[...] = out_ref[...].T

    own_spec, far_spec = half_specs(tile, tiles, cols)
    return call(
        kernel,
        (2 * tiles,),
        [own_spec] * count + [far_spec] * count,
        [pl.BlockSpec((tile, width), lambda i, _: (i, 0)), pl.BlockSpec((width, tile), lambda i, _: (0, i))],
        [((2 * rows, width), bf16), ((width, 2 * rows), bf16)],
        [*own, *far],
        "join_halves",
        [core],
    )


def mixed_back(core, own, far, w_out_rows):
    rows, width = own.shape
    heads = w_out_rows.shape[0]
    tile = 512
    tiles = rows // tile

    def kernel(core_ref, own_ref, far_ref, w_ref, out_ref, grad_ref):
        place_half(core_ref, tiles, [own_ref], [far_ref], out_ref)
        grad_ref[...] = dot_nt(out_ref[...], w_ref[...]).astype(bf16)

    return call(
        kernel,
        (2 * tiles,),
        half_specs(tile, tiles, width) + [fixed(w_out_rows.shape)],
        [pl.BlockSpec((tile, width), lambda i, _: (i, 0)), pl.BlockSpec((tile, heads), lambda i, _: (i, 0))],
        [((2 * rows, width), bf16), ((2 * rows, heads), bf16)],
        [own, far, w_out_rows],
        "mixed_back",
        [core],
    )


def out_rows(place, blocks):
    n_shard, rows_in, cols = blocks[0].shape
    chunks = rows_in // HALF
    quarters = len(blocks)
    shape = (quarters * quarters * SLOT, chunks * cols)

    def kernel(place_ref, *refs):
        out_ref = refs[-1]
        out_ref[...] = jnp.zeros(shape, bf16)
        for group in range(quarters):
            for at in range(quarters):
                row = pl.multiple_of(Q_LANES * group + SLOT * (at ^ place_ref[0]), SLOT)
                for j in range(chunks):
                    out_ref[pl.ds(row, HALF), cols * j : cols * (j + 1)] = refs[at][group ^ place_ref[0], HALF * j : HALF * (j + 1), :]

    (out,) = call(
        kernel,
        (1,),
        [fixed((n_shard, rows_in, cols))] * quarters,
        [whole(shape)],
        [(shape, bf16)],
        blocks,
        "out_rows",
        [place],
    )
    return out


def out_grad_blocks(place, mixed, grad):
    rows, heads = mixed.shape
    width = grad.shape[1]
    quarters = heads // Q_LANES
    tile = 512

    def kernel(place_ref, mixed_ref, grad_ref, *refs):
        outs = refs[:quarters]
        group = pl.program_id(0)
        sums = dot_tn(mixed_ref[...], grad_ref[...]).astype(bf16)
        refs[quarters][...] = sums
        shard = group ^ place_ref[0]
        for at in range(quarters):
            row = pl.multiple_of(SLOT * (at ^ place_ref[0]), SLOT)
            outs[at][shard] = refs[quarters][pl.ds(row, HALF), :]

    return call(
        kernel,
        (quarters,),
        [pl.BlockSpec((rows, Q_LANES), lambda g, _: (0, g)), fixed((rows, width))],
        [whole((quarters, HALF, width))] * quarters,
        [((quarters, HALF, width), bf16)] * quarters,
        [mixed, grad],
        "out_grads",
        [place],
        [pltpu.VMEM((Q_LANES, width), bf16)],
    )


def qkv_grad(normed_t, d_query, d_key, d_value):
    width, rows = normed_t.shape
    spread = jnp.asarray(spread_matrix(), bf16)
    tile = 512

    def kernel(n_ref, q_ref, k_ref, v_ref, spread_ref, out_ref):
        query = matmul(n_ref[...], q_ref[...]).astype(bf16)
        both = matmul(n_ref[...], jnp.concatenate([k_ref[...], v_ref[...]], axis=1)).astype(bf16)
        out_ref[...] = dot_nt(jnp.concatenate([query, both], axis=1), spread_ref[...]).astype(bf16)

    (out,) = call(
        kernel,
        (width // tile,),
        [
            pl.BlockSpec((tile, rows), lambda i: (i, 0)),
            fixed(d_query.shape),
            fixed(d_key.shape),
            fixed(d_value.shape),
            fixed(spread.shape),
        ],
        [pl.BlockSpec((tile, GROUP_COLS), lambda i: (i, 0))],
        [((width, GROUP_COLS), bf16)],
        [normed_t, d_query, d_key, d_value, spread],
        "qkv_grad",
    )
    return out


def unit_columns(where, pieces, n_shard, index):
    depth, cols = pieces[0].shape[0] // 2, pieces[0].shape[1]
    tile = 96
    count = len(pieces)
    quarters = count // 2
    unit_cols = cols // n_shard

    def kernel(where_ref, *refs):
        out_ref = refs[-1]
        for k in range(count):
            unit = quarters * (where_ref[1] ^ (k // quarters)) + (where_ref[0] ^ (k % quarters))
            for z in range(n_shard):
                at = pl.multiple_of((count * z + unit) * unit_cols, unit_cols)
                out_ref[:, pl.ds(at, unit_cols)] = refs[k][:, unit_cols * z : unit_cols * (z + 1)].astype(f32)

    steps = depth // tile
    (out,) = call(
        kernel,
        (depth // tile,),
        [pl.BlockSpec((tile, cols), lambda i, _: (index * steps + i, 0))] * count,
        [pl.BlockSpec((tile, cols * count), lambda i, _: (i, 0))],
        [((depth, cols * count), f32)],
        pieces,
        "unit_columns",
        [where],
    )
    return out


def unit_rows(where, pieces, down_depth):
    depth, width = pieces[0].shape
    count = len(pieces)
    quarters = count // 2
    out_depth = depth - down_depth

    def unit_at(i, where_ref):
        return quarters * (where_ref[1] ^ (i // quarters)) + (where_ref[0] ^ (i % quarters))

    def kernel(where_ref, *refs):
        for k in range(count):

            @pl.when(pl.program_id(0) == k)
            def _():
                refs[count][...] = refs[k][:down_depth, :].astype(f32)
                refs[count + 1][...] = refs[k][down_depth:, :].astype(f32)

    return call(
        kernel,
        (count,),
        [fixed((depth, width))] * count,
        [
            pl.BlockSpec((down_depth, width), lambda i, where: (unit_at(i, where), 0)),
            pl.BlockSpec((out_depth, width), lambda i, where: (unit_at(i, where), 0)),
        ],
        [((down_depth * count, width), f32), ((out_depth * count, width), f32)],
        pieces,
        "unit_rows",
        [where],
    )


def head_columns(where, pieces):
    depth, cols = pieces[0].shape
    count = len(pieces)
    quarters = count // 2
    split = 2

    def kernel(where_ref, *refs):
        q_out, k_out, v_out = refs[count:]
        place, core = where_ref[0], where_ref[1]
        row = lax.broadcasted_iota(jnp.int32, (cols, cols), 0)
        column = lax.broadcasted_iota(jnp.int32, (cols, cols), 1)

        def moved(piece, start, size, to):
            chosen = (row >= start) & (row < start + size) & (row - start == column - to)
            return matmul(piece, jnp.where(chosen, 1.0, 0.0).astype(bf16))

        for at in range(quarters):
            total = 0.0
            for other in range(split):
                total += moved(refs[quarters * other + at][...], 0, Q_COLS, Q_COLS * (core ^ other))
            q_out[:, pl.ds(pl.multiple_of(cols * (place ^ at), LANES), cols)] = total
        for pair in range(quarters // 2):
            keys = values = 0.0
            for low in range(2):
                for other in range(split):
                    piece = refs[quarters * other + 2 * pair + low][...]
                    to = HEAD_DIM * (2 * ((place & 1) ^ low) + (core ^ other))
                    keys += moved(piece, Q_COLS, HEAD_DIM, to)
                    values += moved(piece, Q_COLS + HEAD_DIM, HEAD_DIM, to)
            start = pl.multiple_of(cols * ((place >> 1) ^ pair), LANES)
            k_out[:, pl.ds(start, cols)] = keys
            v_out[:, pl.ds(start, cols)] = values

    shapes = [(depth, quarters * split * w) for w in (Q_COLS, HEAD_DIM, HEAD_DIM)]
    return call(
        kernel, (1,), [fixed((depth, cols))] * count, [whole(s) for s in shapes], [(s, f32) for s in shapes], pieces, "head_columns", [where]
    )


def chip_layer(
    tokens, span_order, token_positions, attn_gain, w_query, w_key, w_value, w_out, mlp_gain, w_gate, w_up, w_down, cotangent
):
    seq_dev, local_len, width = tokens.shape
    n_ctx, n_shard = lax.axis_size("ctx"), lax.axis_size("shard")
    split = n_ctx // seq_dev
    full_len = local_len * n_ctx
    half_rows = full_len // split
    spans_dev = local_len // SPAN
    quarters = 4
    units = w_gate.shape[1] // (split * quarters)
    unit_cols = units // n_shard
    gain_width = attn_gain.shape[0]
    ctx, batch, shard = lax.axis_index("ctx"), lax.axis_index("batch"), lax.axis_index("shard")
    seq, core = ctx // split, ctx % split
    place = 2 * seq + batch

    perm_x = [(c, c ^ split) for c in range(n_ctx)]
    perm_core = [(c, c ^ 1) for c in range(n_ctx)]
    perm_both = [(c, c ^ (split | 1)) for c in range(n_ctx)]
    perm_diagonal = [(2 * c + b, 2 * (c ^ split) + (b ^ 1)) for c in range(n_ctx) for b in range(2)]
    over_x = lambda a: lax.ppermute(a, "ctx", perm_x)
    over_core = lambda a: lax.ppermute(a, "ctx", perm_core)
    over_both = lambda a: lax.ppermute(a, "ctx", perm_both)
    over_y = lambda a: lax.ppermute(a, "batch", [(0, 1), (1, 0)])
    over_diagonal = lambda a: lax.ppermute(a, ("ctx", "batch"), perm_diagonal)

    def over_z(piece):
        gathered = lax.all_gather(piece, "shard", axis=0, tiled=True)
        return gathered.reshape(n_shard, piece.shape[0], piece.shape[1])

    def pick(array, index, axis):
        return lax.dynamic_index_in_dim(array, index, axis, keepdims=False)

    def scatter(block):
        return lax.psum_scatter(block, "shard", scatter_dimension=0, tiled=True)

    def add(*terms):
        return functools.reduce(lambda a, b: a + b, [t.astype(f32) for t in terms]).astype(bf16)

    def fence(*arrays):
        return lax.optimization_barrier(arrays)

    column = split * place + core
    unit_at = quarters * core + place

    def columns_of(array, width_of):
        return lax.dynamic_slice_in_dim(array, column * width_of, width_of, 1)

    def units_of(array, at):
        blocks = [lax.dynamic_slice_in_dim(array, (split * quarters * z + at) * unit_cols, unit_cols, 1) for z in range(n_shard)]
        return jnp.concatenate(blocks, axis=1)

    def stacked(rows, cols):
        return jnp.concatenate([rows[:, cols * j : cols * (j + 1)] for j in range(rows.shape[1] // cols)], axis=0)

    head_piece = jnp.concatenate(
        [columns_of(w_query, Q_COLS), columns_of(w_key, HEAD_DIM), columns_of(w_value, HEAD_DIM)], axis=1
    )
    gains = jnp.pad(jnp.stack([attn_gain, mlp_gain]), ((0, PAD_ROWS - 2), (0, 0)))
    head_piece = jnp.concatenate([head_piece, gains], axis=0)

    def second_piece(at):
        return jnp.concatenate([units_of(w_up, at), stacked(lax.dynamic_slice_in_dim(w_down, at * unit_cols, unit_cols, 0), units)], axis=0)

    own_tokens, sent_tokens = pick(tokens, seq, 0), pick(tokens, 1 - seq, 0)
    positions = pick(token_positions, seq, 0)
    sent_positions = pick(token_positions, 1 - seq, 0)
    head_piece, own_tokens, sent_tokens, positions, sent_positions, w_out, w_gate, w_up, w_down = fence(
        head_piece, own_tokens, sent_tokens, positions, sent_positions, w_out, w_gate, w_up, w_down
    )
    head_own = over_z(head_piece)
    positions = jnp.stack([positions, over_x(sent_positions)])
    x_near = jnp.concatenate([own_tokens, over_x(sent_tokens)], axis=0)
    out_piece = stacked(lax.dynamic_slice_in_dim(w_out, unit_at * HALF, HALF, 0), GROUP_COLS)
    gate_piece, second_own, second_last = units_of(w_gate, unit_at), second_piece(unit_at), second_piece(unit_at ^ 3)
    head_own, out_piece, x_near, positions, gate_piece, second_own, second_last, cotangent = fence(
        head_own, out_piece, x_near, positions, gate_piece, second_own, second_last, cotangent
    )

    out_own, gate_own = over_z(out_piece), over_z(gate_piece)
    head_x, head_y, x_far = over_x(head_own), over_y(head_own), over_core(x_near)
    positions = jnp.concatenate([positions, over_core(positions)], axis=0).reshape(-1, SPAN)
    cot_own, cot_sent = pick(cotangent, seq, 0), pick(cotangent, 1 - seq, 0)
    order = pick(span_order, seq, 0)
    n_spans = order.shape[0]
    span_ids = jnp.arange(n_spans, dtype=jnp.int32)
    slot_of = jnp.sum(jnp.where(order[None, :] == span_ids[:, None], span_ids[None, :], 0), axis=1)
    owner = slot_of // spans_dev
    from_far = (owner % split) ^ core
    side_place = ((owner // split) ^ seq) * spans_dev + slot_of % spans_dev
    places = [
        jnp.where(from_far == 0, side_place, 0).astype(jnp.int32),
        jnp.where(from_far == 0, 0, side_place).astype(jnp.int32),
        from_far.astype(jnp.int32),
    ]
    head_x, head_y, x_far, positions, cot_own, cot_sent = fence(head_x, head_y, x_far, positions, cot_own, cot_sent)

    middle = n_shard // 2
    head_last = [over_x(head_y[:middle]), over_y(head_x[middle:])]
    choice = (from_far * seq_dev * spans_dev + side_place)[:, None] == span_ids[None, :]
    positions = jnp.sum(jnp.where(choice[:, :, None], positions[None], 0), axis=1).reshape(full_len)
    frequency = rope_base ** (-2.0 * jnp.arange(HALF, dtype=f32) / HEAD_DIM)
    angles = positions.astype(f32)[:, None] * frequency
    blank = jnp.zeros((full_len, SLOT - HALF), f32)
    cos_half, sin_half = jnp.cos(angles), jnp.sin(angles)
    cosine = jnp.concatenate([cos_half, blank, cos_half, blank], axis=1)
    sine = jnp.concatenate([-sin_half, blank, sin_half, blank], axis=1)
    gain_one = head_own[:, gain_width, :].reshape(1, width).astype(f32)
    gain_two = head_own[:, gain_width + 1, :].reshape(1, width).astype(f32)
    *head_last, cosine, sine, cot_sent, gate_own, second_own, out_own = fence(
        *head_last, cosine, sine, cot_sent, gate_own, second_own, out_own
    )

    out_blocks = [out_own, over_y(out_own), over_x(out_own), over_diagonal(out_own)]
    head_blocks = [head_own, head_y, head_x, *head_last]
    x, normed, normed_t, queries, keys, values, w_qkv = front(places, x_near, x_far, cosine, sine, gain_one, head_blocks)
    x, normed_t, queries, keys, values, w_qkv = fence(x, normed_t, queries, keys, values, w_qkv)

    second_own = over_z(second_own)
    cot_received, gate_y = over_x(cot_sent), over_y(gate_own)
    mixed, q_aug = attend(queries, keys, values)
    cot_near = jnp.concatenate([cot_own, cot_received], axis=0)
    up_own, down_own = second_own[:, :gain_width], second_own[:, gain_width:]
    mixed, q_aug, cot_near, gate_y, up_own, down_own, second_last, gate_sent, *out_blocks = fence(
        mixed, q_aug, cot_near, gate_y, up_own, down_own, second_last, gate_own, *out_blocks
    )

    second_last = over_z(second_last)
    gate_x, cot_far = over_x(gate_sent), over_core(cot_near)
    up_y = over_y(up_own)
    place_at = place.astype(jnp.int32)[None]
    w_out_rows = out_rows(place_at, out_blocks)
    mine = core.astype(jnp.int32)[None]
    other = 1 - mine
    row_tile = 256
    tiles_half = half_rows // row_tile
    full_out = (w_out_rows, w_out_rows.shape, (0, 0))

    def out_dot(left, right, store):
        store(slice(None), matmul(left[0][...], right[0][...]))

    def back_dot(left, right, store):
        total = 0.0
        for k, both in enumerate(left):
            for which in range(2):
                total += dot_nt(both[:, units * which : units * (which + 1)], flat(right[2 * k + which][...]))
        store(slice(None), total)

    def down_dot(left, right, store):
        for j in range(width // units):
            total = sum(matmul(a[...], down_columns(b, j, range(n_shard))) for a, b in zip(left, right))
            store(slice(units * j, units * (j + 1)), total)

    def in_dot(left, right, store):
        total = 0.0
        for which, weights in enumerate(right):
            total += dot_nt(jnp.concatenate([a[...] for a in left[which::3]], axis=1), weights[...])
        store(slice(None), total)

    def kept(dots, left, right):
        found = []
        dots(left, right, lambda at, total: found.append(total))
        return found[0]

    thirds = [slice(units * j, units * (j + 1)) for j in range(width // units)]

    def sent_parts(lhs, rhs, dots, name):
        def body(left, right, _, outs):
            def store(at, total):
                start = at.start or 0
                for out, place_of in zip(outs, thirds):
                    if start <= place_of.start < start + total.shape[1]:
                        out[...] = total[:, place_of.start - start : place_of.stop - start].astype(bf16)

            dots(left, right, store)

        tile = half_rows // 2
        return sum_rows_call(body, other * 2, lhs, rhs, [], [((half_rows, units), bf16)] * len(thirds), tile, name)

    def joined(refs):
        return jnp.concatenate([r[...] for r in refs], axis=1).astype(f32)

    received = [over_core(a) for a in sent_parts([mixed], [full_out], out_dot, "out_other")]

    def hidden_body(left, right, others, outs):
        x_ref, *received_refs, gain_ref = others
        hidden = x_ref[...].astype(f32) + kept(out_dot, left, right) + joined(received_refs)
        outs[0][...] = hidden
        normed_rows = (hidden * rms_scale(hidden) * gain_ref[...]).astype(bf16)
        for out, at in zip(outs[1:], thirds):
            out[...] = normed_rows[:, at]

    hidden, *normed_two_own = sum_rows_call(
        hidden_body,
        mine * tiles_half,
        [mixed],
        [full_out],
        [(x, "shifted"), *[(r, "plain") for r in received], (gain_two, "whole")],
        [((half_rows, width), f32)] + [((half_rows, units), bf16)] * len(thirds),
        row_tile,
        "out_own",
    )
    normed_two_far = [over_core(a) for a in normed_two_own]
    cot = span_join(places, cot_near, cot_far)
    normed_two_own, normed_two_far, cot, gate_x, up_y, up_own, down_own = fence(
        normed_two_own, normed_two_far, cot, gate_x, up_y, up_own, down_own
    )
    up_x, down_y = over_x(up_own), over_y(down_own)
    normed_two, normed_two_t = join_halves(mine, normed_two_own, normed_two_far)
    normed_two, normed_two_t, cot, down_own = fence(normed_two, normed_two_t, cot, down_own)

    def feed(normed_two, cot, weights, with_grads=True):
        product, d_both = hidden_units(normed_two, cot, weights)
        if not with_grads:
            return weights, product, d_both
        return weights, product, d_both, feed_grads(normed_two_t, cot, product, d_both)

    def apart(*arrays):
        return [whole_of(a) for a in arrays]

    fed = [feed(normed_two, cot, apart(gate_own, up_own, down_own))]
    own_grads, normed_two, up_x, down_y, gate_x, down_own = fence(fed[0][3], normed_two, up_x, down_y, gate_x, down_own)
    gate_last, down_x = over_y(gate_x), over_x(down_own)
    fed.append(feed(normed_two, cot, apart(gate_y, up_y, down_y)))
    (gate_gy, up_gy, down_gy), normed_two, gate_last, down_x, second_last = fence(fed[1][3], normed_two, gate_last, down_x, second_last)
    down_gy = over_y(down_gy)
    fed.append(feed(normed_two, cot, [whole_of(gate_last), third_of(second_last, 0), third_of(second_last, 1)]))
    (gate_gl, up_gl, down_gl), normed_two, gate_gy, up_gy, down_gy = fence(fed[2][3], normed_two, gate_gy, up_gy, down_gy)
    gate_gy, gate_gl = over_y(gate_gy), scatter(gate_gl)
    fed.append(feed(normed_two, cot, apart(gate_x, up_x, down_x)))
    products, d_boths = [f[1] for f in fed], [f[2] for f in fed]
    (gate_gx, up_gx, down_gx), d_boths, products, gate_gy, up_gy, gate_gl, up_gl, down_gl = fence(
        fed[3][3], d_boths, products, gate_gy, up_gy, gate_gl, up_gl, down_gl
    )

    back_rhs = [f[0][k] for f in fed for k in range(2)]
    downs = [f[0][2] for f in fed]
    up_gy, gate_gx, up_gl = over_y(up_gy), over_x(gate_gx), scatter(up_gl)

    received_two = [over_core(a) for a in sent_parts(d_boths, back_rhs, back_dot, "back_other")]
    out_sent = sent_parts(products, downs, down_dot, "down_other")
    received_two, out_sent, up_gy, gate_gx, up_gl, up_gx, down_gx, down_gl = fence(
        received_two, out_sent, up_gy, gate_gx, up_gl, up_gx, down_gx, down_gl
    )

    def back_body(left, right, others, outs):
        *received_refs, hidden_ref, cot_ref, gain_ref = others
        grad_normed = kept(back_dot, left, right) + joined(received_refs)
        values_ = hidden_ref[...]
        scale_rows = rms_scale(values_)
        grad_hidden = cot_ref[...].astype(f32) + norm_back(grad_normed, values_, scale_rows, gain_ref[...])
        outs[0][...] = grad_hidden
        outs[1][...] = grad_hidden.astype(bf16)

        @pl.when(pl.program_id(0) == 0)
        def _():
            outs[2][...] = jnp.zeros(outs[2].shape, f32)

        outs[2][...] += column_sums(grad_normed * values_ * scale_rows)

    up_gx, down_gl = over_x(up_gx), over_y(down_gl)
    received_out = [over_core(a) for a in out_sent]
    grad_hidden, grad_attended_own, gain_two_sums = sum_rows_call(
        back_body,
        mine * tiles_half,
        d_boths,
        back_rhs,
        [*[(r, "plain") for r in received_two], (hidden, "plain"), (cot, "shifted"), (gain_two, "whole")],
        [((half_rows, width), f32), ((half_rows, width), bf16), ((8, width), f32)],
        row_tile,
        "back_own",
    )
    gate_sum = scatter(add(own_grads[0], gate_gy, gate_gx))
    grad_attended_far = over_core(grad_attended_own)

    def down_body(left, right, others, outs):
        hidden_ref, *received_refs = others

        def store(at, total):
            received_rows = received_refs[at.start // units][...].astype(f32)
            outs[0][:, at] = (hidden_ref[:, at] + total + received_rows).astype(bf16)

        down_dot(left, right, store)

    (layer_rows,) = sum_rows_call(
        down_body,
        mine * tiles_half,
        products,
        downs,
        [(hidden, "plain"), *[(r, "plain") for r in received_out]],
        [((half_rows, width), bf16)],
        row_tile,
        "down_own",
    )
    down_gx = add(down_gx, down_gl)
    grad_attended_own, grad_attended_far, layer_rows, up_gx, down_gx, gate_sum, gate_gl, up_gl = fence(
        grad_attended_own, grad_attended_far, layer_rows, up_gx, down_gx, gate_sum, gate_gl, up_gl
    )

    pair_order = order.reshape(n_ctx, spans_dev // 2, 2)
    in_half = jnp.where(pair_order[..., 0] // (n_spans // 2) == core, pair_order[..., 0], pair_order[..., 1]) - core * (n_spans // 2)
    steps = jnp.arange(n_ctx, dtype=jnp.int32) ^ ctx
    send_places = in_half[steps].reshape(-1).astype(jnp.int32)
    my_order = lax.dynamic_slice_in_dim(span_order, ctx * spans_dev, spans_dev, 1)
    from_mine = (my_order // (n_spans // 2) == core).reshape(seq_dev, spans_dev // 2, 2, 1, 1)

    def to_slots(arranged):
        return [arranged[0], over_core(arranged[1]), over_x(arranged[2]), over_both(arranged[3])]

    def arrange(rows):
        arranged = span_copy(send_places, rows).reshape(n_ctx, -1, width)
        return [arranged[k] for k in range(n_ctx)]

    def from_slots(parts):
        parts = [p.reshape(spans_dev // 2, 1, SPAN, width) for p in parts]
        near = jnp.where(from_mine[seq], parts[0], parts[1])
        far = jnp.where(from_mine[1 - seq], parts[2], parts[3])
        near, far = near.reshape(local_len, width), far.reshape(local_len, width)
        return jnp.where(seq == 0, jnp.stack([near, far]), jnp.stack([far, near]))

    def both_cores(side):
        return side + [over_core(a) for a in side]

    up_sum = scatter(add(own_grads[1], up_gy, up_gx))
    down_gx = over_x(down_gx)
    both_gl = over_diagonal(jnp.concatenate([gate_gl, up_gl], axis=0))
    grad_attended, grad_mixed = mixed_back(mine, grad_attended_own, grad_attended_far, w_out_rows)
    out_grads = [b.reshape(-1, width) for b in out_grad_blocks(place_at, mixed, grad_attended)]
    layer_parts = arrange(layer_rows)
    grad_mixed, out_grads, down_gx, layer_parts, up_sum, both_gl = fence(grad_mixed, out_grads, down_gx, layer_parts, up_sum, both_gl)

    def back_of(group, q_aug):
        return attend_back(group, 1, q_aug, keys, values, grad_mixed, mixed, cosine, sine)

    down_sum = scatter(add(own_grads[2], down_gy, down_gx))
    layer_parts = to_slots(layer_parts)
    out_y, out_last = over_y(out_grads[1]), over_y(out_grads[3])
    back_last = back_of(3, q_aug)
    both_sum = add(jnp.concatenate([gate_sum, up_sum], axis=0), both_gl)
    back_last, q_aug, layer_parts, both_sum, out_y, out_last = fence(back_last, q_aug, layer_parts, both_sum, out_y, out_last)
    qkv_last = qkv_grad(normed_t, *back_last)
    out_x = add(out_grads[2], out_last)
    qkv_last, q_aug, out_x = fence(qkv_last, q_aug, out_x)

    qkv_last, out_x, both_x, both_y = over_y(qkv_last), over_x(out_x), over_x(both_sum), over_y(both_sum)
    back_x = back_of(2, q_aug)
    back_x, q_aug, qkv_last, out_x, both_x, both_y, down_sum = fence(back_x, q_aug, qkv_last, out_x, both_x, both_y, down_sum)
    qkv_x = add(qkv_grad(normed_t, *back_x), qkv_last)
    out_sum = add(out_grads[0], out_y, out_x)
    qkv_x, out_sum, q_aug = fence(qkv_x, out_sum, q_aug)

    out_sum = scatter(out_sum)
    qkv_x, both_last = over_x(qkv_x), over_y(both_x)
    both_far = [over_core(a) for a in (both_sum, both_y, both_x)]
    back_y = back_of(1, q_aug)
    back_y, q_aug, qkv_x, both_last, both_far, out_sum = fence(back_y, q_aug, qkv_x, both_last, both_far, out_sum)
    qkv_y = qkv_grad(normed_t, *back_y)
    row_sum = jnp.concatenate([down_sum, out_sum], axis=0)
    qkv_y, q_aug, row_sum = fence(qkv_y, q_aug, row_sum)

    qkv_y, row_x, row_y = over_y(qkv_y), over_x(row_sum), over_y(row_sum)
    both_far.append(over_core(both_last))
    back_own = back_of(0, q_aug)
    back_own, qkv_y, row_x, row_y, both_far = fence(back_own, qkv_y, row_x, row_y, both_far)

    depth = w_qkv.shape[0]
    q_width, k_width = queries.shape[1], keys.shape[1]
    in_rhs = [(w_qkv, (depth, q_width), (0, 0))]
    in_rhs += [(w_qkv, (depth, k_width), (0, q_width // k_width + which)) for which in range(2)]
    qkv_sum = add(qkv_grad(normed_t, *back_own), qkv_y, qkv_x)
    qkv_sum, back_own = fence(qkv_sum, back_own)
    in_lhs = [*back_own, *back_y, *back_x, *back_last]
    qkv_sum = scatter(qkv_sum)
    row_last = over_y(row_x)
    row_far = [over_core(row_sum)]
    received_in = [over_core(a) for a in sent_parts(in_lhs, in_rhs, in_dot, "in_other")]
    received_in, row_last, row_far = fence(received_in, row_last, row_far)
    row_far += [over_core(a) for a in (row_y, row_x, row_last)]

    def in_body(left, right, others, outs):
        *received_refs, x_ref, grad_ref, gain_ref = others
        grad_normed = kept(in_dot, left, right) + joined(received_refs)
        values_ = x_ref[...].astype(f32)
        scale_rows = rms_scale(values_)
        outs[0][...] = (grad_ref[...] + norm_back(grad_normed, values_, scale_rows, gain_ref[...])).astype(bf16)

        @pl.when(pl.program_id(0) == 0)
        def _():
            outs[1][...] = jnp.zeros(outs[1].shape, f32)

        outs[1][...] += column_sums(grad_normed * values_ * scale_rows)

    grad_rows, gain_one_sums = sum_rows_call(
        in_body,
        mine * tiles_half,
        in_lhs,
        in_rhs,
        [*[(r, "plain") for r in received_in], (x, "shifted"), (grad_hidden, "plain"), (gain_one, "whole")],
        [((half_rows, width), bf16), ((8, width), f32)],
        row_tile,
        "in_own",
    )
    sums = jnp.stack([gain_one_sums.sum(0), gain_two_sums.sum(0)])
    sums = sums + over_x(sums)
    token_parts, sums, qkv_sum, row_far = fence(arrange(grad_rows), sums, qkv_sum, row_far)

    qkv_x, qkv_y = over_x(qkv_sum), over_y(qkv_sum)
    layer_out = from_slots(layer_parts)
    token_parts, sums, qkv_x, qkv_y, layer_out = fence(token_parts, sums, qkv_x, qkv_y, layer_out)

    token_parts = to_slots(token_parts)
    qkv_last = over_y(qkv_x)
    where = jnp.stack([place, core]).astype(jnp.int32)
    both_pieces = [both_sum, both_y, both_x, both_last] + both_far
    grad_w_gate = unit_columns(where, both_pieces, n_shard, 0)
    grad_w_up = unit_columns(where, both_pieces, n_shard, 1)
    grad_w_down, grad_w_out = unit_rows(where, [row_sum, row_y, row_x, row_last] + row_far, unit_cols)
    for step in (over_core, over_y):
        sums = sums + step(sums)
    token_parts, grad_w_gate, grad_w_up, grad_w_down, grad_w_out, qkv_last, sums = fence(
        token_parts, grad_w_gate, grad_w_up, grad_w_down, grad_w_out, qkv_last, sums
    )

    total = lax.dynamic_slice_in_dim(sums, shard * gain_width, gain_width, 1)
    for step in range(1, n_shard):
        to = lax.dynamic_slice_in_dim(sums, (shard + step) % n_shard * gain_width, gain_width, 1)
        total = total + lax.ppermute(to, "shard", [(z, (z + step) % n_shard) for z in range(n_shard)])
    grad_w_query, grad_w_key, grad_w_value = head_columns(where, both_cores([qkv_sum, qkv_y, qkv_x, qkv_last]))
    grad_tokens = from_slots(token_parts)

    return (
        layer_out,
        grad_tokens,
        total[0],
        grad_w_query,
        grad_w_key,
        grad_w_value,
        grad_w_out,
        total[1],
        grad_w_gate,
        grad_w_up,
        grad_w_down,
    )


def rope_tables(positions):
    half_dim = HEAD_DIM // 2
    frequency = rope_base ** (-2.0 * jnp.arange(half_dim, dtype=jnp.float32) / HEAD_DIM)
    angles = positions.astype(jnp.float32)[..., None] * frequency
    return (jnp.cos(angles), jnp.sin(angles))


def rotate(values, cosine, sine_table):
    half_dim = values.shape[-1] // 2
    first_half = values[..., :half_dim]
    second_half = values[..., half_dim:]
    cosine = cosine[..., None, :]
    sine_table = sine_table[..., None, :]
    return jnp.concatenate(
        [
            first_half * cosine - second_half * sine_table,
            second_half * cosine + first_half * sine_table,
        ],
        axis=-1,
    )


def general_layer(
    tokens,
    span_order,
    token_positions,
    attn_gain,
    w_query,
    w_key,
    w_value,
    w_out,
    mlp_gain,
    w_gate,
    w_up,
    w_down,
    cotangent,
):
    seq_dev, local_len, model_width = tokens.shape
    row_count = seq_dev * local_len
    groups = HEADS // KV_HEADS
    kv_width = KV_HEADS * HEAD_DIM
    score_scale = HEAD_DIM ** (-0.5)
    full_len = local_len * lax.axis_size("ctx")
    ctx_index = lax.axis_index("ctx")
    slot_index = jnp.arange(full_len, dtype=jnp.int32)
    key_index = span_order[:, slot_index // SPAN] * SPAN + slot_index[None, :] % SPAN
    query_index = lax.dynamic_slice_in_dim(key_index, ctx_index * local_len, local_len, 1)
    allowed = query_index[:, :, None] >= key_index[:, None, :]
    cosine, sine_table = rope_tables(token_positions)
    gain_one, wq_full, wk_full, wv_full, wo_full = (
        lax.all_gather(attn_gain, "shard", axis=0, tiled=True),
        lax.all_gather(w_query, "shard", axis=0, tiled=True),
        lax.all_gather(w_key, "shard", axis=0, tiled=True),
        lax.all_gather(w_value, "shard", axis=0, tiled=True),
        lax.all_gather(w_out, "shard", axis=0, tiled=True),
    )
    x_rows = tokens.reshape(row_count, model_width).astype(jnp.float32)
    scale_one = rms_scale(x_rows)
    normed = (x_rows * scale_one * gain_one).astype(jnp.bfloat16)
    queries = rotate(
        matmul(normed, wq_full).reshape(seq_dev, local_len, HEADS, HEAD_DIM), cosine, sine_table
    ).astype(jnp.bfloat16)
    keys_local = rotate(
        matmul(normed, wk_full).reshape(seq_dev, local_len, KV_HEADS, HEAD_DIM), cosine, sine_table
    ).astype(jnp.bfloat16)
    values_local = matmul(normed, wv_full).astype(jnp.bfloat16)
    keys_all, values_all = (
        lax.all_gather(keys_local.reshape(seq_dev, local_len, kv_width), "ctx", axis=1, tiled=True),
        lax.all_gather(
            values_local.reshape(seq_dev, local_len, kv_width), "ctx", axis=1, tiled=True
        ),
    )
    query_heads = queries.reshape(seq_dev, local_len, KV_HEADS, groups, HEAD_DIM).transpose(
        2, 0, 1, 3, 4
    )
    key_heads = keys_all.reshape(seq_dev, full_len, KV_HEADS, HEAD_DIM).transpose(2, 0, 1, 3)
    value_heads = values_all.reshape(seq_dev, full_len, KV_HEADS, HEAD_DIM).transpose(2, 0, 1, 3)

    def scores_of(query_head, key_head):
        raw_scores = (
            jnp.einsum("sqjd,skd->sjqk", query_head, key_head, preferred_element_type=jnp.float32)
            * score_scale
        )
        return jnp.where(allowed[:, None], raw_scores, masked_value)

    def attend_head(pieces):
        query_head, key_head, value_head = pieces
        scores = scores_of(query_head, key_head)
        row_max = jnp.max(scores, axis=-1, keepdims=True)
        exponent = jnp.exp(scores - row_max)
        row_total = jnp.sum(exponent, axis=-1, keepdims=True)
        probabilities = (exponent / row_total).astype(jnp.bfloat16)
        mixed_head = jnp.einsum(
            "sjqk,skd->sqjd", probabilities, value_head, preferred_element_type=jnp.float32
        )
        return (mixed_head, row_max[..., 0] + jnp.log(row_total[..., 0]))

    mixed_heads, log_totals = lax.map(attend_head, (query_heads, key_heads, value_heads))
    mixed_low = (
        mixed_heads.transpose(1, 2, 0, 3, 4).reshape(row_count, model_width).astype(jnp.bfloat16)
    )
    hidden = x_rows + matmul(mixed_low, wo_full)
    scale_two = rms_scale(hidden)
    gain_two, wg_full, wu_full, wd_full = (
        lax.all_gather(mlp_gain, "shard", axis=0, tiled=True),
        lax.all_gather(w_gate, "shard", axis=0, tiled=True),
        lax.all_gather(w_up, "shard", axis=0, tiled=True),
        lax.all_gather(w_down, "shard", axis=0, tiled=True),
    )
    normed_two = (hidden * scale_two * gain_two).astype(jnp.bfloat16)
    gate_pre = matmul(normed_two, wg_full)
    up_pre = matmul(normed_two, wu_full)
    sigmoid_gate = jax.nn.sigmoid(gate_pre)
    activated = gate_pre * sigmoid_gate
    product = (activated * up_pre).astype(jnp.bfloat16)
    layer_out = (hidden + matmul(product, wd_full)).astype(jnp.bfloat16).reshape(tokens.shape)
    grad_out = cotangent.reshape(row_count, model_width)
    gain_two_back, wg_back, wu_back, wd_back = (
        lax.all_gather(mlp_gain, "shard", axis=0, tiled=True),
        lax.all_gather(w_gate, "shard", axis=0, tiled=True),
        lax.all_gather(w_up, "shard", axis=0, tiled=True),
        lax.all_gather(w_down, "shard", axis=0, tiled=True),
    )
    grad_product = matmul(grad_out, wd_back.T)
    grad_w_down = matmul(product.T, grad_out)
    grad_gate = (
        grad_product * up_pre * sigmoid_gate * (1.0 + gate_pre * (1.0 - sigmoid_gate))
    ).astype(jnp.bfloat16)
    grad_up = (grad_product * activated).astype(jnp.bfloat16)
    grad_w_gate = matmul(normed_two.T, grad_gate)
    grad_w_up = matmul(normed_two.T, grad_up)
    grad_normed_two = matmul(grad_gate, wg_back.T) + matmul(grad_up, wu_back.T)
    gain_two_f = gain_two_back.astype(jnp.float32)
    grad_mlp_gain = jnp.sum(grad_normed_two * hidden * scale_two, axis=0)
    grad_hidden = grad_out.astype(jnp.float32) + norm_back(
        grad_normed_two, hidden, scale_two, gain_two_f
    )
    gain_one_back, wq_back, wk_back, wv_back, wo_back = (
        lax.all_gather(attn_gain, "shard", axis=0, tiled=True),
        lax.all_gather(w_query, "shard", axis=0, tiled=True),
        lax.all_gather(w_key, "shard", axis=0, tiled=True),
        lax.all_gather(w_value, "shard", axis=0, tiled=True),
        lax.all_gather(w_out, "shard", axis=0, tiled=True),
    )
    grad_attended = grad_hidden.astype(jnp.bfloat16)
    grad_w_out = matmul(mixed_low.T, grad_attended)
    grad_mixed = matmul(grad_attended, wo_back.T).astype(jnp.bfloat16)
    grad_heads = grad_mixed.reshape(seq_dev, local_len, KV_HEADS, groups, HEAD_DIM).transpose(
        2, 0, 1, 3, 4
    )

    def attend_back(pieces):
        query_head, key_head, value_head, grad_head, log_total = pieces
        scores = scores_of(query_head, key_head)
        probabilities = jnp.exp(scores - log_total[..., None])
        grad_probs = jnp.einsum(
            "sqjd,skd->sjqk", grad_head, value_head, preferred_element_type=jnp.float32
        )
        inner_sum = jnp.sum(probabilities * grad_probs, axis=-1, keepdims=True)
        grad_scores = (probabilities * (grad_probs - inner_sum)).astype(jnp.bfloat16)
        grad_query = (
            jnp.einsum("sjqk,skd->sqjd", grad_scores, key_head, preferred_element_type=jnp.float32)
            * score_scale
        )
        grad_key = (
            jnp.einsum(
                "sjqk,sqjd->skd", grad_scores, query_head, preferred_element_type=jnp.float32
            )
            * score_scale
        )
        grad_value = jnp.einsum(
            "sjqk,sqjd->skd",
            probabilities.astype(jnp.bfloat16),
            grad_head,
            preferred_element_type=jnp.float32,
        )
        return (grad_query, grad_key, grad_value)

    grad_queries, key_terms, value_terms = lax.map(
        attend_back, (query_heads, key_heads, value_heads, grad_heads, log_totals)
    )
    key_terms = key_terms.transpose(1, 2, 0, 3).reshape(seq_dev, full_len, kv_width)
    value_terms = value_terms.transpose(1, 2, 0, 3).reshape(seq_dev, full_len, kv_width)
    grad_keys, grad_values = (
        lax.psum_scatter(
            key_terms.astype(jnp.bfloat16), "ctx", scatter_dimension=1, tiled=True
        ).astype(jnp.float32),
        lax.psum_scatter(
            value_terms.astype(jnp.bfloat16), "ctx", scatter_dimension=1, tiled=True
        ).astype(jnp.float32),
    )
    grad_queries = grad_queries.transpose(1, 2, 0, 3, 4).reshape(
        seq_dev, local_len, HEADS, HEAD_DIM
    )
    grad_q_low = (
        rotate(grad_queries, cosine, -sine_table)
        .reshape(row_count, model_width)
        .astype(jnp.bfloat16)
    )
    grad_k_low = (
        rotate(grad_keys.reshape(seq_dev, local_len, KV_HEADS, HEAD_DIM), cosine, -sine_table)
        .reshape(row_count, kv_width)
        .astype(jnp.bfloat16)
    )
    grad_v_low = grad_values.reshape(row_count, kv_width).astype(jnp.bfloat16)
    grad_w_query = matmul(normed.T, grad_q_low)
    grad_w_key = matmul(normed.T, grad_k_low)
    grad_w_value = matmul(normed.T, grad_v_low)
    grad_normed = (
        matmul(grad_q_low, wq_back.T)
        + matmul(grad_k_low, wk_back.T)
        + matmul(grad_v_low, wv_back.T)
    )
    gain_one_f = gain_one_back.astype(jnp.float32)
    grad_attn_gain = jnp.sum(grad_normed * x_rows * scale_one, axis=0)
    grad_tokens = (grad_hidden + norm_back(grad_normed, x_rows, scale_one, gain_one_f)).astype(
        jnp.bfloat16
    )
    grad_tokens = grad_tokens.reshape(tokens.shape)
    part_gain_two, part_gate, part_up, part_down = (
        lax.psum_scatter(
            grad_mlp_gain.astype(jnp.bfloat16), "shard", scatter_dimension=0, tiled=True
        ).astype(jnp.float32),
        lax.psum_scatter(
            grad_w_gate.astype(jnp.bfloat16), "shard", scatter_dimension=0, tiled=True
        ).astype(jnp.float32),
        lax.psum_scatter(
            grad_w_up.astype(jnp.bfloat16), "shard", scatter_dimension=0, tiled=True
        ).astype(jnp.float32),
        lax.psum_scatter(
            grad_w_down.astype(jnp.bfloat16), "shard", scatter_dimension=0, tiled=True
        ).astype(jnp.float32),
    )
    part_gain_one, part_query, part_key, part_value, part_out = (
        lax.psum_scatter(
            grad_attn_gain.astype(jnp.bfloat16), "shard", scatter_dimension=0, tiled=True
        ).astype(jnp.float32),
        lax.psum_scatter(
            grad_w_query.astype(jnp.bfloat16), "shard", scatter_dimension=0, tiled=True
        ).astype(jnp.float32),
        lax.psum_scatter(
            grad_w_key.astype(jnp.bfloat16), "shard", scatter_dimension=0, tiled=True
        ).astype(jnp.float32),
        lax.psum_scatter(
            grad_w_value.astype(jnp.bfloat16), "shard", scatter_dimension=0, tiled=True
        ).astype(jnp.float32),
        lax.psum_scatter(
            grad_w_out.astype(jnp.bfloat16), "shard", scatter_dimension=0, tiled=True
        ).astype(jnp.float32),
    )
    summed = (
        lax.psum(part_gain_one.astype(jnp.bfloat16), ("ctx", "batch")).astype(jnp.float32),
        lax.psum(part_query.astype(jnp.bfloat16), ("ctx", "batch")).astype(jnp.float32),
        lax.psum(part_key.astype(jnp.bfloat16), ("ctx", "batch")).astype(jnp.float32),
        lax.psum(part_value.astype(jnp.bfloat16), ("ctx", "batch")).astype(jnp.float32),
        lax.psum(part_out.astype(jnp.bfloat16), ("ctx", "batch")).astype(jnp.float32),
        lax.psum(part_gain_two.astype(jnp.bfloat16), ("ctx", "batch")).astype(jnp.float32),
        lax.psum(part_gate.astype(jnp.bfloat16), ("ctx", "batch")).astype(jnp.float32),
        lax.psum(part_up.astype(jnp.bfloat16), ("ctx", "batch")).astype(jnp.float32),
        lax.psum(part_down.astype(jnp.bfloat16), ("ctx", "batch")).astype(jnp.float32),
    )
    return (
        layer_out,
        grad_tokens,
        summed[0],
        summed[1],
        summed[2],
        summed[3],
        summed[4],
        summed[5],
        summed[6],
        summed[7],
        summed[8],
    )


def fits(mesh):
    split = mesh.shape["ctx"] // 2
    return split == 2 and mesh.shape["batch"] == 2 and mesh.shape["shard"] * split == KV_HEADS and mesh.shape["shard"] == 4


def solution(mesh):
    in_specs = (
        P(("shard", "batch"), "ctx", None),
        P(("shard", "batch"), None),
        P(("shard", "batch"), "ctx"),
        P("shard"),
        P("shard", None),
        P("shard", None),
        P("shard", None),
        P("shard", None),
        P("shard"),
        P("shard", None),
        P("shard", None),
        P("shard", None),
        P(("shard", "batch"), "ctx", None),
    )
    out_specs = (
        P(("shard", "batch"), "ctx", None),
        P(("shard", "batch"), "ctx", None),
        P("shard"),
        P("shard", None),
        P("shard", None),
        P("shard", None),
        P("shard", None),
        P("shard"),
        P("shard", None),
        P("shard", None),
        P("shard", None),
    )
    layer = chip_layer if fits(mesh) else general_layer
    return jax.shard_map(layer, mesh=mesh, in_specs=in_specs, out_specs=out_specs, check_vma=False)
```

```python
import functools

import jax
import jax.numpy as jnp
import numpy as np
from jax import lax
from jax.experimental import pallas as pl
from jax.experimental.pallas import tpu as pltpu
from jax.sharding import PartitionSpec as P

HEADS = 16
KV_HEADS = 8
HEAD_DIM = 96
SPAN = 128
GROUPS = HEADS // KV_HEADS
HALF = HEAD_DIM // 2
LANES = 128
SLOT = LANES // 2
GROUP_COLS = (GROUPS + 2) * HEAD_DIM
Q_COLS = GROUPS * HEAD_DIM
Q_LANES = GROUPS * LANES
PAD_ROWS = 16

norm_eps = 1e-05
rope_base = 100000.0
masked_value = -1e30
score_scale = HEAD_DIM ** (-0.5)
exp2_scale = score_scale * 1.4426950408889634

bf16 = jnp.bfloat16
f32 = jnp.float32
MIB = 1 << 20
NT = (((1,), (1,)), ((), ()))
TN = (((0,), (0,)), ((), ()))


def rms_scale(values):
    return lax.rsqrt(jnp.mean(values * values, axis=-1, keepdims=True) + norm_eps)


def matmul(left, right):
    return jnp.dot(left, right, preferred_element_type=f32)


def dot_nt(left, right):
    return lax.dot_general(left, right, NT, preferred_element_type=f32)


def dot_tn(left, right):
    return lax.dot_general(left, right, TN, preferred_element_type=f32)


def params(limit):
    return pltpu.CompilerParams(vmem_limit_bytes=limit * MIB)


def short():
    return pl.CostEstimate(flops=1000, bytes_accessed=1000, transcendentals=0)


def whole(shape):
    return pl.BlockSpec(shape, lambda *_: (0,) * len(shape))


def part(block, index):
    return pl.BlockSpec(block, lambda *_: index, pipeline_mode=pl.Buffered(1))


def fixed(shape):
    return part(shape, (0,) * len(shape))


def call(kernel, grid, in_specs, out_specs, out_shape, operands, name, prefetch=(), scratch=(), limit=60):
    return pl.pallas_call(
        kernel,
        grid_spec=pltpu.PrefetchScalarGridSpec(
            num_scalar_prefetch=len(prefetch), grid=grid, in_specs=in_specs, out_specs=out_specs, scratch_shapes=list(scratch)
        ),
        out_shape=[jax.ShapeDtypeStruct(shape, dtype) for shape, dtype in out_shape],
        compiler_params=params(limit),
        cost_estimate=short(),
        name=name,
    )(*prefetch, *operands)


def spread_matrix():
    spread = np.zeros((GROUP_COLS, (GROUPS + 2) * LANES), np.float32)
    for row in range(spread.shape[0]):
        head, feature = divmod(row, HEAD_DIM)
        half, place = divmod(feature, HALF)
        spread[row, head * LANES + half * SLOT + place] = 1.0
    return spread


def front_kernel(near_ref, far_ref, flag_ref, *refs):
    spans = 4
    near, far, refs = refs[:spans], refs[spans : 2 * spans], refs[2 * spans :]
    cos_ref, sin_ref, gain_ref, spread_ref, w0, w1, w2, w3a, w3b, x_out, n_out, nt_out, q_out, k_out, v_out, w_out = refs
    q_width, k_width = q_out.shape[1], k_out.shape[1]
    step_at = pl.program_id(0)

    @pl.when(step_at == 0)
    def _():
        depth = w0.shape[1]
        halves = w3a.shape[0]
        for at, piece in enumerate((w0, w1, w2, None)):
            for z in range(w0.shape[0]):
                block = piece[z] if piece is not None else (w3a[z] if z < halves else w3b[z - halves])
                spread = matmul(block, spread_ref[...]).astype(bf16)
                rows = slice(z * depth, (z + 1) * depth)
                w_out[rows, Q_LANES * at : Q_LANES * (at + 1)] = spread[:, :Q_LANES]
                w_out[rows, q_width + LANES * at : q_width + LANES * (at + 1)] = spread[:, Q_LANES : Q_LANES + LANES]
                at_v = q_width + k_width + LANES * at
                w_out[rows, at_v : at_v + LANES] = spread[:, Q_LANES + LANES :]

    for k in range(spans):
        rows = slice(k * SPAN, (k + 1) * SPAN)

        @pl.when(flag_ref[spans * step_at + k] == 0)
        def _():
            x_out[rows, :] = near[k][0]

        @pl.when(flag_ref[spans * step_at + k] != 0)
        def _():
            x_out[rows, :] = far[k][0]

    x = x_out[...].astype(f32)
    normed = (x * rms_scale(x) * gain_ref[...]).astype(bf16)
    n_out[...] = normed
    nt_out[...] = normed.T
    cosine, sine = cos_ref[...], sin_ref[...]
    lane = lax.broadcasted_iota(jnp.int32, (1, LANES), 1)
    ones = jnp.where((lane >= HALF) & (lane < HALF + 3), 1.0, 0.0)
    step = 4 * LANES
    for start in range(0, w_out.shape[1], step):
        raw = matmul(normed, w_out[:, start : start + step])
        for piece in range(0, step, LANES):
            at = start + piece
            head = raw[:, piece : piece + LANES]
            if at < q_width + k_width:
                head = head * cosine + pltpu.roll(head, SLOT, 1) * sine
            if at < q_width:
                q_out[:, at : at + LANES] = head.astype(bf16)
            elif at < q_width + k_width:
                k_out[:, at - q_width : at - q_width + LANES] = (head + ones).astype(bf16)
            else:
                v_out[:, at - q_width - k_width : at - q_width - k_width + LANES] = (head + ones).astype(bf16)


def span_specs(width, count):
    def near(k):
        return pl.BlockSpec((1, SPAN, width), lambda i, near, far, flag: (near[count * i + k], 0, 0))

    def far(k):
        return pl.BlockSpec((1, SPAN, width), lambda i, near, far, flag: (far[count * i + k], 0, 0))

    return [near(k) for k in range(count)] + [far(k) for k in range(count)]


def as_spans(array):
    return array.reshape(array.shape[0] // SPAN, SPAN, array.shape[1])


def front(places, near, far, cosine, sine, gain, pieces):
    rows, width = 2 * near.shape[0], near.shape[1]
    groups = len(pieces) - 1
    n_shard = pieces[0].shape[0]
    depth = width // n_shard
    spread = jnp.asarray(spread_matrix(), bf16)
    spans = 4
    tile = spans * SPAN
    q_width, k_width = groups * Q_LANES, groups * LANES
    total = q_width + 2 * k_width

    def rows_spec(cols):
        return pl.BlockSpec((tile, cols), lambda i, *_: (i, 0))

    near, far = as_spans(near), as_spans(far)
    return call(
        front_kernel,
        (rows // tile,),
        span_specs(width, spans)
        + [rows_spec(LANES), rows_spec(LANES), fixed(gain.shape), fixed(spread.shape)]
        + [part((p.shape[0], depth, p.shape[2]), (0, 0, 0)) for p in pieces],
        [rows_spec(width), rows_spec(width), pl.BlockSpec((width, tile), lambda i, *_: (0, i))]
        + [rows_spec(q_width), rows_spec(k_width), rows_spec(k_width), whole((n_shard * depth, total))],
        [
            ((rows, width), bf16),
            ((rows, width), bf16),
            ((width, rows), bf16),
            ((rows, q_width), bf16),
            ((rows, k_width), bf16),
            ((rows, k_width), bf16),
            ((n_shard * depth, total), bf16),
        ],
        [near] * spans + [far] * spans + [cosine, sine, gain, spread, *pieces],
        "front",
        places,
    )


def span_copy(places, source):
    width = source.shape[1]
    count = places.shape[0]
    step = 2

    def kernel(place_ref, *refs):
        for k in range(step):
            refs[step][k] = refs[k][0]

    spans = as_spans(source)
    (out,) = call(
        kernel,
        (count // step,),
        [pl.BlockSpec((1, SPAN, width), lambda i, place, k=k: (place[step * i + k], 0, 0)) for k in range(step)],
        [pl.BlockSpec((step, SPAN, width), lambda i, place: (i, 0, 0))],
        [((count, SPAN, width), source.dtype)],
        [spans] * step,
        "span_copy",
        [places],
    )
    return out.reshape(count * SPAN, width)


def span_join(places, near, far):
    width = near.shape[1]
    count = 2 * near.shape[0] // SPAN
    step = 4

    def kernel(near_ref, far_ref, flag_ref, *refs):
        out_ref = refs[-1]
        for k in range(step):
            is_far = flag_ref[step * pl.program_id(0) + k] != 0

            @pl.when(jnp.logical_not(is_far))
            def _():
                out_ref[k] = refs[k][0]

            @pl.when(is_far)
            def _():
                out_ref[k] = refs[step + k][0]

    (out,) = call(
        kernel,
        (count // step,),
        span_specs(width, step),
        [pl.BlockSpec((step, SPAN, width), lambda i, *_: (i, 0, 0))],
        [((count, SPAN, width), near.dtype)],
        [as_spans(near)] * step + [as_spans(far)] * step,
        "span_join",
        places,
    )
    return out.reshape(count * SPAN, width)


def three_parts(values):
    first = values.astype(bf16).astype(f32)
    second = (values - first).astype(bf16).astype(f32)
    third = values - first - second
    return first, second, third


def with_lanes(block, column):
    lane = lax.broadcasted_iota(jnp.int32, block.shape, 1)
    first, second, third = three_parts(column)
    wide = block.astype(f32)
    wide = jnp.where(lane == HALF, first, wide)
    wide = jnp.where(lane == HALF + 1, second, wide)
    wide = jnp.where(lane == HALF + 2, third, wide)
    return wide.astype(bf16)


Q_TILE = 256
K_CHUNK = 512


def heads_down(block):
    return jnp.concatenate([block[:, LANES * h : LANES * (h + 1)] for h in range(GROUPS)], axis=0)


def attend_kernel(q_ref, k_ref, v_ref, mixed_ref, q_aug_ref):
    rows = q_ref.shape[0]
    for tile in range(rows // Q_TILE):
        first_row = tile * Q_TILE
        query = heads_down(q_ref[first_row : first_row + Q_TILE, :])
        end = first_row + Q_TILE
        top = acc = None
        for start in range(0, end, K_CHUNK):
            size = min(K_CHUNK, end - start)
            key = k_ref[start : start + size, :]
            value = v_ref[start : start + size, :]
            scores = dot_nt(query, key)
            if start + size > first_row:
                row = lax.broadcasted_iota(jnp.int32, (Q_TILE, size), 0) + first_row
                column = lax.broadcasted_iota(jnp.int32, (Q_TILE, size), 1) + start
                allowed = row >= column
                scores = jnp.where(jnp.concatenate([allowed] * GROUPS, axis=0), scores, masked_value)
            chunk_top = jnp.max(scores, axis=-1, keepdims=True)
            new_top = chunk_top if top is None else jnp.maximum(top, chunk_top)
            weights = jnp.exp2((scores - new_top) * exp2_scale).astype(bf16)
            part = matmul(weights, value)
            acc = part if top is None else acc * jnp.exp2((top - new_top) * exp2_scale) + part
            top = new_top
        total = acc[:, HALF : HALF + 1]
        mixed = (acc * (1.0 / total)).astype(bf16)
        log_total = top + jnp.log2(total) * (1.0 / exp2_scale)
        marked = with_lanes(query, -log_total)
        for h in range(GROUPS):
            mixed_ref[first_row : first_row + Q_TILE, LANES * h : LANES * (h + 1)] = mixed[Q_TILE * h : Q_TILE * (h + 1)]
            q_aug_ref[first_row : first_row + Q_TILE, LANES * h : LANES * (h + 1)] = marked[Q_TILE * h : Q_TILE * (h + 1)]


def attend(queries, keys, values):
    rows, k_width = keys.shape
    groups = k_width // LANES
    pair = pl.BlockSpec((rows, Q_LANES), lambda g: (0, g))
    single = pl.BlockSpec((rows, LANES), lambda g: (0, g))
    return call(
        attend_kernel, (groups,), [pair, single, single], [pair, pair], [(queries.shape, bf16)] * 2, [queries, keys, values], "attend"
    )


def attend_back_kernel(q_ref, k_ref, v_ref, do_ref, o_ref, cos_ref, sin_ref, dq_ref, dk_ref, dv_ref, q_s, do_s, dq_s, dk_s, dv_s):
    rows = q_ref.shape[0]
    tiles = rows // Q_TILE
    for tile in range(tiles):
        at = slice(tile * Q_TILE, (tile + 1) * Q_TILE)
        q_s[tile] = heads_down(q_ref[at, :])
        grad = heads_down(do_ref[at, :])
        inner = jnp.sum(grad.astype(f32) * heads_down(o_ref[at, :]).astype(f32), axis=-1, keepdims=True)
        do_s[tile] = with_lanes(grad, -inner)
        dq_s[tile] = jnp.zeros(dq_s.shape[1:], f32)

    def unit(tile, key_start, size, mask_from):
        key = k_ref[key_start : key_start + size, :]
        value = v_ref[key_start : key_start + size, :]
        query, grad = q_s[tile], do_s[tile]
        probs = jnp.exp2(dot_nt(key, query) * exp2_scale)
        if mask_from is not None:
            row = lax.broadcasted_iota(jnp.int32, (size, Q_TILE), 0)
            column = lax.broadcasted_iota(jnp.int32, (size, Q_TILE), 1) + mask_from
            allowed = jnp.concatenate([row <= column] * GROUPS, axis=1)
            probs = jnp.where(allowed, probs, 0.0)
        d_scores = (probs * dot_nt(value, grad)).astype(bf16)
        dv_s[:size] += matmul(probs.astype(bf16), grad)
        dk_s[:size] += matmul(d_scores, query)
        dq_s[tile] += dot_tn(d_scores, key)

    for key_start in range(0, rows, K_CHUNK):
        dk_s[...] = jnp.zeros(dk_s.shape, f32)
        dv_s[...] = jnp.zeros(dv_s.shape, f32)
        tile = key_start // Q_TILE
        unit(tile, key_start, Q_TILE, 0)
        unit(tile + 1, key_start, K_CHUNK, Q_TILE)
        if tile + 2 < tiles:

            @pl.loop(tile + 2, tiles)
            def _(later):
                unit(later, key_start, K_CHUNK, None)

        at = slice(key_start, key_start + K_CHUNK)
        turned = dk_s[...] * score_scale
        turned = turned * cos_ref[at, :] - pltpu.roll(turned, SLOT, 1) * sin_ref[at, :]
        dk_ref[at, :] = turned.astype(bf16)
        dv_ref[at, :] = dv_s[...].astype(bf16)
    for tile in range(tiles):
        at = slice(tile * Q_TILE, (tile + 1) * Q_TILE)
        cosine, sine = cos_ref[at, :], sin_ref[at, :]
        for h in range(GROUPS):
            turned = dq_s[tile, Q_TILE * h : Q_TILE * (h + 1), :] * score_scale
            turned = turned * cosine - pltpu.roll(turned, SLOT, 1) * sine
            dq_ref[at, LANES * h : LANES * (h + 1)] = turned.astype(bf16)


def attend_back(first, groups, q_aug, keys, values, grad, mixed, cosine, sine):
    rows = keys.shape[0]
    tiles = rows // Q_TILE
    pair = pl.BlockSpec((rows, Q_LANES), lambda g: (0, g + first))
    single = pl.BlockSpec((rows, LANES), lambda g: (0, g + first))
    pair_out = pl.BlockSpec((rows, Q_LANES), lambda g: (0, g))
    single_out = pl.BlockSpec((rows, LANES), lambda g: (0, g))
    stacked = (tiles, GROUPS * Q_TILE, LANES)
    table = fixed((rows, LANES))
    return call(
        attend_back_kernel,
        (groups,),
        [pair, single, single, pair, pair, table, table],
        [pair_out, single_out, single_out],
        [((rows, groups * Q_LANES), bf16), ((rows, groups * LANES), bf16), ((rows, groups * LANES), bf16)],
        [q_aug, keys, values, grad, mixed, cosine, sine],
        "attend_back",
        scratch=[
            pltpu.VMEM(stacked, bf16),
            pltpu.VMEM(stacked, bf16),
            pltpu.VMEM(stacked, f32),
            pltpu.VMEM((K_CHUNK, LANES), f32),
            pltpu.VMEM((K_CHUNK, LANES), f32),
        ],
    )


def flat(block):
    return block.reshape(block.shape[0] * block.shape[1], block.shape[2])


def down_columns(down_ref, j, zs):
    rows = down_ref.shape[1] // 3
    return jnp.concatenate([down_ref[z, rows * j : rows * (j + 1), :] for z in zs], axis=0)


def hidden_kernel(n_ref, cot_ref, gate_ref, up_ref, down_ref, product_ref, dboth_ref):
    n_shard, units = gate_ref.shape[0], gate_ref.shape[2]
    third = cot_ref.shape[1] // 3
    step = 256
    for start in range(0, units, step):
        at = slice(start, start + step)
        zs = range(start * n_shard // units, (start + step) * n_shard // units)
        gate = matmul(n_ref[...], flat(gate_ref[:, :, at]))
        up = matmul(n_ref[...], flat(up_ref[:, :, at]))
        d_product = sum(dot_nt(cot_ref[:, third * j : third * (j + 1)], down_columns(down_ref, j, zs)) for j in range(3))
        sigmoid = 1.0 / (1.0 + jnp.exp(-gate))
        silu = gate * sigmoid
        product_ref[:, at] = (silu * up).astype(bf16)
        dboth_ref[:, at] = (d_product * up * sigmoid * (1.0 + gate * (1.0 - sigmoid))).astype(bf16)
        dboth_ref[:, units + start : units + start + step] = (d_product * silu).astype(bf16)


def feed_grads(normed_t, cot, product, d_both):
    width, rows = normed_t.shape
    units = product.shape[1]
    steps = width // units

    def kernel(n_ref, cot_ref, product_ref, both_ref, gate_ref, up_ref, down_ref, turned_ref):
        step = pl.program_id(0)

        @pl.when(step < steps)
        def _():
            gate_ref[...] = matmul(n_ref[...], both_ref[:, :units]).astype(bf16)
            up_ref[...] = matmul(n_ref[...], both_ref[:, units:]).astype(bf16)

        @pl.when(step == steps)
        def _():
            turned_ref[...] = product_ref[...].T

        @pl.when(step >= steps)
        def _():
            down_ref[...] = matmul(turned_ref[...], cot_ref[...]).astype(bf16)

    early = lambda i: (jnp.minimum(i, steps - 1), 0)
    late = lambda i: (0, jnp.maximum(i - steps, 0))
    return call(
        kernel,
        (2 * steps,),
        [pl.BlockSpec((units, rows), early), pl.BlockSpec((rows, units), late), fixed(product.shape), fixed(d_both.shape)],
        [pl.BlockSpec((units, units), early), pl.BlockSpec((units, units), early), pl.BlockSpec((units, units), late)],
        [((width, units), bf16), ((width, units), bf16), ((units, width), bf16)],
        [normed_t, cot, product, d_both],
        "feed_grads",
        scratch=[pltpu.VMEM((units, rows), bf16)],
    )


def whole_of(array):
    return array, array.shape, (0,) * array.ndim


def third_of(array, index):
    rows = 384
    return array, (array.shape[0], rows, array.shape[2]), (0, index, 0)


def hidden_units(normed, cot, weights):
    rows, width = normed.shape
    units = weights[0][0].shape[2]
    tile = 512
    wide = pl.BlockSpec((tile, width), lambda i: (i, 0))
    thin = pl.BlockSpec((tile, units), lambda i: (i, 0))
    return call(
        hidden_kernel,
        (rows // tile,),
        [wide, wide] + [part(block, index) for _, block, index in weights],
        [thin, pl.BlockSpec((tile, 2 * units), lambda i: (i, 0))],
        [((rows, units), bf16), ((rows, 2 * units), bf16)],
        [normed, cot] + [a for a, _, _ in weights],
        "hidden_units",
    )


def sum_rows_call(body, base, lhs, rhs, others, outs, tile, name):
    rows = outs[0][0][0]

    def shifted(cols):
        return pl.BlockSpec((tile, cols), lambda i, base: (base[0] + i, 0))

    def plain(cols):
        return pl.BlockSpec((tile, cols), lambda i, base: (i, 0))

    in_specs = [shifted(a.shape[1]) for a in lhs] + [part(block, index) for _, block, index in rhs]
    for a, kind in others:
        in_specs.append(fixed(a.shape) if kind == "whole" else {"shifted": shifted, "plain": plain}[kind](a.shape[1]))
    out_specs = [plain(shape[1]) if shape[0] == rows else whole(shape) for shape, _ in outs]
    n_lhs, n_rhs, n_other = len(lhs), len(rhs), len(others)

    def kernel(base_ref, *refs):
        left, refs = refs[:n_lhs], refs[n_lhs:]
        right, refs = refs[:n_rhs], refs[n_rhs:]
        body(left, right, refs[:n_other], refs[n_other:])

    return call(
        kernel,
        (rows // tile,),
        in_specs,
        out_specs,
        outs,
        [*lhs, *[a for a, _, _ in rhs], *[a for a, _ in others]],
        name,
        [base],
    )


def norm_back(grad_normed, values, scale_rows, gain):
    scaled = grad_normed * gain
    return scale_rows * scaled - values * (scale_rows * scale_rows * scale_rows) * jnp.mean(scaled * values, axis=-1, keepdims=True)


def column_sums(values):
    return jnp.sum(values.reshape(-1, 8, values.shape[-1]), axis=0)


def half_specs(tile, tiles, width):
    own = pl.BlockSpec((tile, width), lambda i, core: (jnp.clip(i - tiles * core[0], 0, tiles - 1), 0))
    far = pl.BlockSpec((tile, width), lambda i, core: (jnp.clip(i - tiles * (1 - core[0]), 0, tiles - 1), 0))
    return [own, far]


def place_half(core_ref, tiles, own_refs, far_refs, out_ref):
    is_own = pl.program_id(0) // tiles == core_ref[0]

    def place(refs):
        start = 0
        for ref in refs:
            out_ref[:, start : start + ref.shape[1]] = ref[...]
            start += ref.shape[1]

    @pl.when(is_own)
    def _():
        place(own_refs)

    @pl.when(jnp.logical_not(is_own))
    def _():
        place(far_refs)


def join_halves(core, own, far):
    rows, cols = own[0].shape
    count = len(own)
    width = count * cols
    tile = 256
    tiles = rows // tile

    def kernel(core_ref, *refs):
        out_ref, turned_ref = refs[2 * count :]
        place_half(core_ref, tiles, refs[:count], refs[count : 2 * count], out_ref)
        turned_ref[...] = out_ref[...].T

    own_spec, far_spec = half_specs(tile, tiles, cols)
    return call(
        kernel,
        (2 * tiles,),
        [own_spec] * count + [far_spec] * count,
        [pl.BlockSpec((tile, width), lambda i, _: (i, 0)), pl.BlockSpec((width, tile), lambda i, _: (0, i))],
        [((2 * rows, width), bf16), ((width, 2 * rows), bf16)],
        [*own, *far],
        "join_halves",
        [core],
    )


def mixed_back(core, own, far, w_out_rows):
    rows, cols = own[0].shape
    count = len(own)
    width = count * cols
    heads = w_out_rows.shape[0]
    tile = 512
    tiles = rows // tile

    own_spec, far_spec = half_specs(tile, tiles, cols)

    def kernel(core_ref, *refs):
        w_ref, out_ref, grad_ref = refs[2 * count :]
        place_half(core_ref, tiles, refs[:count], refs[count : 2 * count], out_ref)
        grad_ref[...] = dot_nt(out_ref[...], w_ref[...]).astype(bf16)

    return call(
        kernel,
        (2 * tiles,),
        [own_spec] * count + [far_spec] * count + [fixed(w_out_rows.shape)],
        [pl.BlockSpec((tile, width), lambda i, _: (i, 0)), pl.BlockSpec((tile, heads), lambda i, _: (i, 0))],
        [((2 * rows, width), bf16), ((2 * rows, heads), bf16)],
        [*own, *far, w_out_rows],
        "mixed_back",
        [core],
    )


def out_rows(place, blocks):
    n_shard, rows_in, cols = blocks[0].shape
    chunks = rows_in // HALF
    quarters = len(blocks)
    shape = (quarters * quarters * SLOT, chunks * cols)

    def kernel(place_ref, *refs):
        out_ref = refs[-1]
        out_ref[...] = jnp.zeros(shape, bf16)
        for group in range(quarters):
            for at in range(quarters):
                row = pl.multiple_of(Q_LANES * group + SLOT * (at ^ place_ref[0]), SLOT)
                for j in range(chunks):
                    out_ref[pl.ds(row, HALF), cols * j : cols * (j + 1)] = refs[at][group ^ place_ref[0], HALF * j : HALF * (j + 1), :]

    (out,) = call(
        kernel,
        (1,),
        [fixed((n_shard, rows_in, cols))] * quarters,
        [whole(shape)],
        [(shape, bf16)],
        blocks,
        "out_rows",
        [place],
    )
    return out


def out_grad_blocks(place, mixed, grad):
    rows, heads = mixed.shape
    width = grad.shape[1]
    quarters = heads // Q_LANES
    tile = 512

    def kernel(place_ref, mixed_ref, grad_ref, *refs):
        outs = refs[:quarters]
        group = pl.program_id(0)
        sums = dot_tn(mixed_ref[...], grad_ref[...]).astype(bf16)
        refs[quarters][...] = sums
        shard = group ^ place_ref[0]
        for at in range(quarters):
            row = pl.multiple_of(SLOT * (at ^ place_ref[0]), SLOT)
            outs[at][shard] = refs[quarters][pl.ds(row, HALF), :]

    return call(
        kernel,
        (quarters,),
        [pl.BlockSpec((rows, Q_LANES), lambda g, _: (0, g)), fixed((rows, width))],
        [whole((quarters, HALF, width))] * quarters,
        [((quarters, HALF, width), bf16)] * quarters,
        [mixed, grad],
        "out_grads",
        [place],
        [pltpu.VMEM((Q_LANES, width), bf16)],
    )


def qkv_grad(normed_t, d_query, d_key, d_value):
    width, rows = normed_t.shape
    spread = jnp.asarray(spread_matrix(), bf16)
    tile = 512

    def kernel(n_ref, q_ref, k_ref, v_ref, spread_ref, out_ref):
        query = matmul(n_ref[...], q_ref[...]).astype(bf16)
        both = matmul(n_ref[...], jnp.concatenate([k_ref[...], v_ref[...]], axis=1)).astype(bf16)
        out_ref[...] = dot_nt(jnp.concatenate([query, both], axis=1), spread_ref[...]).astype(bf16)

    (out,) = call(
        kernel,
        (width // tile,),
        [
            pl.BlockSpec((tile, rows), lambda i: (i, 0)),
            fixed(d_query.shape),
            fixed(d_key.shape),
            fixed(d_value.shape),
            fixed(spread.shape),
        ],
        [pl.BlockSpec((tile, GROUP_COLS), lambda i: (i, 0))],
        [((width, GROUP_COLS), bf16)],
        [normed_t, d_query, d_key, d_value, spread],
        "qkv_grad",
    )
    return out


def unit_columns(where, pieces, n_shard, index):
    depth, cols = pieces[0].shape[0] // 2, pieces[0].shape[1]
    tile = 96
    count = len(pieces)
    quarters = count // 2
    unit_cols = cols // n_shard

    def kernel(where_ref, *refs):
        out_ref = refs[-1]
        for k in range(count):
            unit = quarters * (where_ref[1] ^ (k // quarters)) + (where_ref[0] ^ (k % quarters))
            for z in range(n_shard):
                at = pl.multiple_of((count * z + unit) * unit_cols, unit_cols)
                out_ref[:, pl.ds(at, unit_cols)] = refs[k][:, unit_cols * z : unit_cols * (z + 1)].astype(f32)

    steps = depth // tile
    (out,) = call(
        kernel,
        (depth // tile,),
        [pl.BlockSpec((tile, cols), lambda i, _: (index * steps + i, 0))] * count,
        [pl.BlockSpec((tile, cols * count), lambda i, _: (i, 0))],
        [((depth, cols * count), f32)],
        pieces,
        "unit_columns",
        [where],
    )
    return out


def unit_rows(where, pieces, down_depth):
    depth, width = pieces[0].shape
    count = len(pieces)
    quarters = count // 2
    out_depth = depth - down_depth

    def unit_at(i, where_ref):
        return quarters * (where_ref[1] ^ (i // quarters)) + (where_ref[0] ^ (i % quarters))

    def kernel(where_ref, *refs):
        for k in range(count):

            @pl.when(pl.program_id(0) == k)
            def _():
                refs[count][...] = refs[k][:down_depth, :].astype(f32)
                refs[count + 1][...] = refs[k][down_depth:, :].astype(f32)

    return call(
        kernel,
        (count,),
        [fixed((depth, width))] * count,
        [
            pl.BlockSpec((down_depth, width), lambda i, where: (unit_at(i, where), 0)),
            pl.BlockSpec((out_depth, width), lambda i, where: (unit_at(i, where), 0)),
        ],
        [((down_depth * count, width), f32), ((out_depth * count, width), f32)],
        pieces,
        "unit_rows",
        [where],
    )


def head_columns(where, pieces):
    depth, cols = pieces[0].shape
    count = len(pieces)
    quarters = count // 2
    split = 2

    def kernel(where_ref, *refs):
        q_out, k_out, v_out = refs[count:]
        place, core = where_ref[0], where_ref[1]
        row = lax.broadcasted_iota(jnp.int32, (cols, cols), 0)
        column = lax.broadcasted_iota(jnp.int32, (cols, cols), 1)

        def moved(piece, start, size, to):
            chosen = (row >= start) & (row < start + size) & (row - start == column - to)
            return matmul(piece, jnp.where(chosen, 1.0, 0.0).astype(bf16))

        for at in range(quarters):
            total = 0.0
            for other in range(split):
                total += moved(refs[quarters * other + at][...], 0, Q_COLS, Q_COLS * (core ^ other))
            q_out[:, pl.ds(pl.multiple_of(cols * (place ^ at), LANES), cols)] = total
        for pair in range(quarters // 2):
            keys = values = 0.0
            for low in range(2):
                for other in range(split):
                    piece = refs[quarters * other + 2 * pair + low][...]
                    to = HEAD_DIM * (2 * ((place & 1) ^ low) + (core ^ other))
                    keys += moved(piece, Q_COLS, HEAD_DIM, to)
                    values += moved(piece, Q_COLS + HEAD_DIM, HEAD_DIM, to)
            start = pl.multiple_of(cols * ((place >> 1) ^ pair), LANES)
            k_out[:, pl.ds(start, cols)] = keys
            v_out[:, pl.ds(start, cols)] = values

    shapes = [(depth, quarters * split * w) for w in (Q_COLS, HEAD_DIM, HEAD_DIM)]
    return call(
        kernel, (1,), [fixed((depth, cols))] * count, [whole(s) for s in shapes], [(s, f32) for s in shapes], pieces, "head_columns", [where]
    )


def chip_layer(
    tokens, span_order, token_positions, attn_gain, w_query, w_key, w_value, w_out, mlp_gain, w_gate, w_up, w_down, cotangent
):
    seq_dev, local_len, width = tokens.shape
    n_ctx, n_shard = lax.axis_size("ctx"), lax.axis_size("shard")
    split = n_ctx // seq_dev
    full_len = local_len * n_ctx
    half_rows = full_len // split
    spans_dev = local_len // SPAN
    quarters = 4
    units = w_gate.shape[1] // (split * quarters)
    unit_cols = units // n_shard
    gain_width = attn_gain.shape[0]
    ctx, batch, shard = lax.axis_index("ctx"), lax.axis_index("batch"), lax.axis_index("shard")
    seq, core = ctx // split, ctx % split
    place = 2 * seq + batch

    perm_x = [(c, c ^ split) for c in range(n_ctx)]
    perm_core = [(c, c ^ 1) for c in range(n_ctx)]
    perm_both = [(c, c ^ (split | 1)) for c in range(n_ctx)]
    perm_diagonal = [(2 * c + b, 2 * (c ^ split) + (b ^ 1)) for c in range(n_ctx) for b in range(2)]
    over_x = lambda a: lax.ppermute(a, "ctx", perm_x)
    over_core = lambda a: lax.ppermute(a, "ctx", perm_core)
    over_both = lambda a: lax.ppermute(a, "ctx", perm_both)
    over_y = lambda a: lax.ppermute(a, "batch", [(0, 1), (1, 0)])
    over_diagonal = lambda a: lax.ppermute(a, ("ctx", "batch"), perm_diagonal)

    def over_z(piece):
        gathered = lax.all_gather(piece, "shard", axis=0, tiled=True)
        return gathered.reshape(n_shard, piece.shape[0], piece.shape[1])

    def pick(array, index, axis):
        return lax.dynamic_index_in_dim(array, index, axis, keepdims=False)

    def scatter(block):
        return lax.psum_scatter(block, "shard", scatter_dimension=0, tiled=True)

    def add(*terms):
        return functools.reduce(lambda a, b: a + b, [t.astype(f32) for t in terms]).astype(bf16)

    def fence(*arrays):
        return lax.optimization_barrier(arrays)

    column = split * place + core
    unit_at = quarters * core + place

    def columns_of(array, width_of):
        return lax.dynamic_slice_in_dim(array, column * width_of, width_of, 1)

    def units_of(array, at):
        blocks = [lax.dynamic_slice_in_dim(array, (split * quarters * z + at) * unit_cols, unit_cols, 1) for z in range(n_shard)]
        return jnp.concatenate(blocks, axis=1)

    def stacked(rows, cols):
        return jnp.concatenate([rows[:, cols * j : cols * (j + 1)] for j in range(rows.shape[1] // cols)], axis=0)

    head_piece = jnp.concatenate(
        [columns_of(w_query, Q_COLS), columns_of(w_key, HEAD_DIM), columns_of(w_value, HEAD_DIM)], axis=1
    )
    gains = jnp.pad(jnp.stack([attn_gain, mlp_gain]), ((0, PAD_ROWS - 2), (0, 0)))
    head_piece = jnp.concatenate([head_piece, gains], axis=0)

    def second_piece(at):
        return jnp.concatenate([units_of(w_up, at), stacked(lax.dynamic_slice_in_dim(w_down, at * unit_cols, unit_cols, 0), units)], axis=0)

    own_tokens, sent_tokens = pick(tokens, seq, 0), pick(tokens, 1 - seq, 0)
    positions = pick(token_positions, seq, 0)
    sent_positions = pick(token_positions, 1 - seq, 0)
    head_piece, own_tokens, sent_tokens, positions, sent_positions, w_out, w_gate, w_up, w_down = fence(
        head_piece, own_tokens, sent_tokens, positions, sent_positions, w_out, w_gate, w_up, w_down
    )
    head_own = over_z(head_piece)
    positions = jnp.stack([positions, over_x(sent_positions)])
    x_near = jnp.concatenate([own_tokens, over_x(sent_tokens)], axis=0)
    out_piece = stacked(lax.dynamic_slice_in_dim(w_out, unit_at * HALF, HALF, 0), GROUP_COLS)
    gate_piece, second_own, second_last = units_of(w_gate, unit_at), second_piece(unit_at), second_piece(unit_at ^ 3)
    head_own, out_piece, x_near, positions, gate_piece, second_own, second_last, cotangent = fence(
        head_own, out_piece, x_near, positions, gate_piece, second_own, second_last, cotangent
    )

    out_own, gate_own = over_z(out_piece), over_z(gate_piece)
    head_x, head_y, x_far = over_x(head_own), over_y(head_own), over_core(x_near)
    positions = jnp.concatenate([positions, over_core(positions)], axis=0).reshape(-1, SPAN)
    cot_own, cot_sent = pick(cotangent, seq, 0), pick(cotangent, 1 - seq, 0)
    order = pick(span_order, seq, 0)
    n_spans = order.shape[0]
    span_ids = jnp.arange(n_spans, dtype=jnp.int32)
    slot_of = jnp.sum(jnp.where(order[None, :] == span_ids[:, None], span_ids[None, :], 0), axis=1)
    owner = slot_of // spans_dev
    from_far = (owner % split) ^ core
    side_place = ((owner // split) ^ seq) * spans_dev + slot_of % spans_dev
    places = [
        jnp.where(from_far == 0, side_place, 0).astype(jnp.int32),
        jnp.where(from_far == 0, 0, side_place).astype(jnp.int32),
        from_far.astype(jnp.int32),
    ]
    head_x, head_y, x_far, positions, cot_own, cot_sent = fence(head_x, head_y, x_far, positions, cot_own, cot_sent)

    middle = n_shard // 2
    head_last = [over_x(head_y[:middle]), over_y(head_x[middle:])]
    choice = (from_far * seq_dev * spans_dev + side_place)[:, None] == span_ids[None, :]
    positions = jnp.sum(jnp.where(choice[:, :, None], positions[None], 0), axis=1).reshape(full_len)
    frequency = rope_base ** (-2.0 * jnp.arange(HALF, dtype=f32) / HEAD_DIM)
    angles = positions.astype(f32)[:, None] * frequency
    blank = jnp.zeros((full_len, SLOT - HALF), f32)
    cos_half, sin_half = jnp.cos(angles), jnp.sin(angles)
    cosine = jnp.concatenate([cos_half, blank, cos_half, blank], axis=1)
    sine = jnp.concatenate([-sin_half, blank, sin_half, blank], axis=1)
    gain_one = head_own[:, gain_width, :].reshape(1, width).astype(f32)
    gain_two = head_own[:, gain_width + 1, :].reshape(1, width).astype(f32)
    *head_last, cosine, sine, cot_sent, gate_own, second_own, out_own = fence(
        *head_last, cosine, sine, cot_sent, gate_own, second_own, out_own
    )

    out_blocks = [out_own, over_y(out_own), over_x(out_own), over_diagonal(out_own)]
    head_blocks = [head_own, head_y, head_x, *head_last]
    x, normed, normed_t, queries, keys, values, w_qkv = front(places, x_near, x_far, cosine, sine, gain_one, head_blocks)
    x, normed_t, queries, keys, values, w_qkv = fence(x, normed_t, queries, keys, values, w_qkv)

    second_own = over_z(second_own)
    cot_received, gate_y = over_x(cot_sent), over_y(gate_own)
    mixed, q_aug = attend(queries, keys, values)
    cot_near = jnp.concatenate([cot_own, cot_received], axis=0)
    up_own, down_own = second_own[:, :gain_width], second_own[:, gain_width:]
    mixed, q_aug, cot_near, gate_y, up_own, down_own, second_last, gate_sent, *out_blocks = fence(
        mixed, q_aug, cot_near, gate_y, up_own, down_own, second_last, gate_own, *out_blocks
    )

    second_last = over_z(second_last)
    gate_x, cot_far = over_x(gate_sent), over_core(cot_near)
    up_y = over_y(up_own)
    place_at = place.astype(jnp.int32)[None]
    w_out_rows = out_rows(place_at, out_blocks)
    mine = core.astype(jnp.int32)[None]
    other = 1 - mine
    row_tile = 256
    tiles_half = half_rows // row_tile
    full_out = (w_out_rows, w_out_rows.shape, (0, 0))

    def out_dot(left, right, store):
        store(slice(None), matmul(left[0][...], right[0][...]))

    def back_dot(left, right, store):
        total = 0.0
        for k, both in enumerate(left):
            for which in range(2):
                total += dot_nt(both[:, units * which : units * (which + 1)], flat(right[2 * k + which][...]))
        store(slice(None), total)

    def down_dot(left, right, store):
        for j in range(width // units):
            total = sum(matmul(a[...], down_columns(b, j, range(n_shard))) for a, b in zip(left, right))
            store(slice(units * j, units * (j + 1)), total)

    def in_dot(left, right, store):
        total = 0.0
        for which, weights in enumerate(right):
            total += dot_nt(jnp.concatenate([a[...] for a in left[which::3]], axis=1), weights[...])
        store(slice(None), total)

    def kept(dots, left, right):
        found = []
        dots(left, right, lambda at, total: found.append(total))
        return found[0]

    thirds = [slice(units * j, units * (j + 1)) for j in range(width // units)]

    def sent_parts(lhs, rhs, dots, name):
        def body(left, right, _, outs):
            def store(at, total):
                start = at.start or 0
                for out, place_of in zip(outs, thirds):
                    if start <= place_of.start < start + total.shape[1]:
                        out[...] = total[:, place_of.start - start : place_of.stop - start].astype(bf16)

            dots(left, right, store)

        tile = half_rows // 2
        return sum_rows_call(body, other * 2, lhs, rhs, [], [((half_rows, units), bf16)] * len(thirds), tile, name)

    def joined(refs):
        return jnp.concatenate([r[...] for r in refs], axis=1).astype(f32)

    received = [over_core(a) for a in sent_parts([mixed], [full_out], out_dot, "out_other")]

    def hidden_body(left, right, others, outs):
        x_ref, *received_refs, gain_ref = others
        hidden = x_ref[...].astype(f32) + kept(out_dot, left, right) + joined(received_refs)
        outs[0][...] = hidden
        normed_rows = (hidden * rms_scale(hidden) * gain_ref[...]).astype(bf16)
        for out, at in zip(outs[1:], thirds):
            out[...] = normed_rows[:, at]

    hidden, *normed_two_own = sum_rows_call(
        hidden_body,
        mine * tiles_half,
        [mixed],
        [full_out],
        [(x, "shifted"), *[(r, "plain") for r in received], (gain_two, "whole")],
        [((half_rows, width), f32)] + [((half_rows, units), bf16)] * len(thirds),
        row_tile,
        "out_own",
    )
    normed_two_far = [over_core(a) for a in normed_two_own]
    cot = span_join(places, cot_near, cot_far)
    normed_two_own, normed_two_far, cot, gate_x, up_y, up_own, down_own = fence(
        normed_two_own, normed_two_far, cot, gate_x, up_y, up_own, down_own
    )
    up_x, down_y = over_x(up_own), over_y(down_own)
    normed_two, normed_two_t = join_halves(mine, normed_two_own, normed_two_far)
    normed_two, normed_two_t, cot, down_own = fence(normed_two, normed_two_t, cot, down_own)

    def feed(normed_two, cot, weights, with_grads=True):
        product, d_both = hidden_units(normed_two, cot, weights)
        if not with_grads:
            return weights, product, d_both
        return weights, product, d_both, feed_grads(normed_two_t, cot, product, d_both)

    def apart(*arrays):
        return [whole_of(a) for a in arrays]

    fed = [feed(normed_two, cot, apart(gate_own, up_own, down_own))]
    own_grads, normed_two, up_x, down_y, gate_x, down_own = fence(fed[0][3], normed_two, up_x, down_y, gate_x, down_own)
    gate_last, down_x = over_y(gate_x), over_x(down_own)
    fed.append(feed(normed_two, cot, apart(gate_y, up_y, down_y)))
    (gate_gy, up_gy, down_gy), normed_two, gate_last, down_x, second_last = fence(fed[1][3], normed_two, gate_last, down_x, second_last)
    down_gy = over_y(down_gy)
    fed.append(feed(normed_two, cot, [whole_of(gate_last), third_of(second_last, 0), third_of(second_last, 1)]))
    (gate_gl, up_gl, down_gl), normed_two, gate_gy, up_gy, down_gy = fence(fed[2][3], normed_two, gate_gy, up_gy, down_gy)
    gate_gy, gate_gl = over_y(gate_gy), scatter(gate_gl)
    fed.append(feed(normed_two, cot, apart(gate_x, up_x, down_x)))
    products, d_boths = [f[1] for f in fed], [f[2] for f in fed]
    (gate_gx, up_gx, down_gx), d_boths, products, gate_gy, up_gy, gate_gl, up_gl, down_gl = fence(
        fed[3][3], d_boths, products, gate_gy, up_gy, gate_gl, up_gl, down_gl
    )

    back_rhs = [f[0][k] for f in fed for k in range(2)]
    downs = [f[0][2] for f in fed]
    up_gy, gate_gx, up_gl = over_y(up_gy), over_x(gate_gx), scatter(up_gl)

    received_two = [over_core(a) for a in sent_parts(d_boths, back_rhs, back_dot, "back_other")]
    out_sent = sent_parts(products, downs, down_dot, "down_other")
    received_two, out_sent, up_gy, gate_gx, up_gl, up_gx, down_gx, down_gl = fence(
        received_two, out_sent, up_gy, gate_gx, up_gl, up_gx, down_gx, down_gl
    )

    def back_body(left, right, others, outs):
        *received_refs, hidden_ref, cot_ref, gain_ref = others
        grad_normed = kept(back_dot, left, right) + joined(received_refs)
        values_ = hidden_ref[...]
        scale_rows = rms_scale(values_)
        grad_hidden = cot_ref[...].astype(f32) + norm_back(grad_normed, values_, scale_rows, gain_ref[...])
        outs[0][...] = grad_hidden
        for out, at in zip(outs[2:], thirds):
            out[...] = grad_hidden[:, at].astype(bf16)

        @pl.when(pl.program_id(0) == 0)
        def _():
            outs[1][...] = jnp.zeros(outs[1].shape, f32)

        outs[1][...] += column_sums(grad_normed * values_ * scale_rows)

    up_gx, down_gl = over_x(up_gx), over_y(down_gl)
    received_out = [over_core(a) for a in out_sent]
    grad_hidden, gain_two_sums, *grad_attended_own = sum_rows_call(
        back_body,
        mine * tiles_half,
        d_boths,
        back_rhs,
        [*[(r, "plain") for r in received_two], (hidden, "plain"), (cot, "shifted"), (gain_two, "whole")],
        [((half_rows, width), f32), ((8, width), f32)] + [((half_rows, units), bf16)] * len(thirds),
        row_tile,
        "back_own",
    )
    gate_sum = scatter(add(own_grads[0], gate_gy, gate_gx))
    grad_attended_far = [over_core(a) for a in grad_attended_own]

    def down_body(left, right, others, outs):
        hidden_ref, *received_refs = others

        def store(at, total):
            received_rows = received_refs[at.start // units][...].astype(f32)
            outs[0][:, at] = (hidden_ref[:, at] + total + received_rows).astype(bf16)

        down_dot(left, right, store)

    (layer_rows,) = sum_rows_call(
        down_body,
        mine * tiles_half,
        products,
        downs,
        [(hidden, "plain"), *[(r, "plain") for r in received_out]],
        [((half_rows, width), bf16)],
        row_tile,
        "down_own",
    )
    grad_attended_own, grad_attended_far, layer_rows, up_gx, down_gl, gate_sum, gate_gl, up_gl = fence(
        grad_attended_own, grad_attended_far, layer_rows, up_gx, down_gl, gate_sum, gate_gl, up_gl
    )
    down_gx = add(down_gx, down_gl)

    pair_order = order.reshape(n_ctx, spans_dev // 2, 2)
    in_half = jnp.where(pair_order[..., 0] // (n_spans // 2) == core, pair_order[..., 0], pair_order[..., 1]) - core * (n_spans // 2)
    steps = jnp.arange(n_ctx, dtype=jnp.int32) ^ ctx
    send_places = in_half[steps].reshape(-1).astype(jnp.int32)
    my_order = lax.dynamic_slice_in_dim(span_order, ctx * spans_dev, spans_dev, 1)
    from_mine = (my_order // (n_spans // 2) == core).reshape(seq_dev, spans_dev // 2, 2, 1, 1)

    def to_slots(arranged):
        return [arranged[0], over_core(arranged[1]), over_x(arranged[2]), over_both(arranged[3])]

    def arrange(rows):
        arranged = span_copy(send_places, rows).reshape(n_ctx, -1, width)
        return [arranged[k] for k in range(n_ctx)]

    def from_slots(parts):
        parts = [p.reshape(spans_dev // 2, 1, SPAN, width) for p in parts]
        near = jnp.where(from_mine[seq], parts[0], parts[1])
        far = jnp.where(from_mine[1 - seq], parts[2], parts[3])
        near, far = near.reshape(local_len, width), far.reshape(local_len, width)
        return jnp.where(seq == 0, jnp.stack([near, far]), jnp.stack([far, near]))

    def both_cores(side):
        return side + [over_core(a) for a in side]

    up_sum = scatter(add(own_grads[1], up_gy, up_gx))
    down_gx = over_x(down_gx)
    both_gl = over_y(jnp.concatenate([gate_gl, up_gl], axis=0))
    grad_attended, grad_mixed = mixed_back(mine, grad_attended_own, grad_attended_far, w_out_rows)
    out_grads = [b.reshape(-1, width) for b in out_grad_blocks(place_at, mixed, grad_attended)]
    layer_parts = arrange(layer_rows)
    grad_mixed, out_grads, down_gx, layer_parts, up_sum, both_gl = fence(grad_mixed, out_grads, down_gx, layer_parts, up_sum, both_gl)

    def back_of(group, q_aug):
        return attend_back(group, 1, q_aug, keys, values, grad_mixed, mixed, cosine, sine)

    down_sum = scatter(add(own_grads[2], down_gy, down_gx))
    layer_parts = [layer_parts[0], over_core(layer_parts[1]), over_x(layer_parts[2]), layer_parts[3]]
    both_gl, out_y, out_last = over_x(both_gl), over_y(out_grads[1]), over_y(out_grads[3])
    back_last = back_of(3, q_aug)
    back_last, q_aug, both_gl, out_last = fence(back_last, q_aug, both_gl, out_last)
    both_sum = add(jnp.concatenate([gate_sum, up_sum], axis=0), both_gl)
    qkv_last = qkv_grad(normed_t, *back_last)
    out_x = add(out_grads[2], out_last)
    qkv_last, q_aug, out_x, both_sum, layer_parts, out_y = fence(qkv_last, q_aug, out_x, both_sum, layer_parts, out_y)

    qkv_last, out_x, both_x = over_y(qkv_last), over_x(out_x), over_x(both_sum)
    back_x = back_of(2, q_aug)
    back_x, q_aug, qkv_last, out_x, down_sum = fence(back_x, q_aug, qkv_last, out_x, down_sum)
    qkv_x = add(qkv_grad(normed_t, *back_x), qkv_last)
    out_sum = add(out_grads[0], out_y, out_x)
    qkv_x, out_sum, q_aug, both_sum, both_x = fence(qkv_x, out_sum, q_aug, both_sum, both_x)

    out_sum = scatter(out_sum)
    qkv_x, both_last, both_y = over_x(qkv_x), over_y(both_x), over_y(both_sum)
    both_far = [over_core(a) for a in (both_sum, both_x)]
    back_y = back_of(1, q_aug)
    back_y, q_aug, both_far, out_sum = fence(back_y, q_aug, both_far, out_sum)
    qkv_y = qkv_grad(normed_t, *back_y)
    row_sum = jnp.concatenate([down_sum, out_sum], axis=0)
    qkv_y, q_aug, row_sum, qkv_x, both_y, both_last, layer_parts = fence(qkv_y, q_aug, row_sum, qkv_x, both_y, both_last, layer_parts)

    layer_parts[3] = over_both(layer_parts[3])
    qkv_y, row_x, row_y = over_y(qkv_y), over_x(row_sum), over_y(row_sum)
    both_far = [both_far[0], over_core(both_y), both_far[1], over_core(both_last)]
    back_own = back_of(0, q_aug)
    back_own, both_far = fence(back_own, both_far)

    depth = w_qkv.shape[0]
    q_width, k_width = queries.shape[1], keys.shape[1]
    in_rhs = [(w_qkv, (depth, q_width), (0, 0))]
    in_rhs += [(w_qkv, (depth, k_width), (0, q_width // k_width + which)) for which in range(2)]
    qkv_sum = add(qkv_grad(normed_t, *back_own), qkv_y, qkv_x)
    qkv_sum, back_own, row_x, row_y, layer_parts = fence(qkv_sum, back_own, row_x, row_y, layer_parts)
    in_lhs = [*back_own, *back_y, *back_x, *back_last]
    qkv_sum = scatter(qkv_sum)
    row_last = over_y(row_x)
    received_in = [over_core(a) for a in sent_parts(in_lhs, in_rhs, in_dot, "in_other")]
    row_far = [over_core(a) for a in (row_sum, row_y, row_x, row_last)]

    def in_body(left, right, others, outs):
        *received_refs, x_ref, grad_ref, gain_ref = others
        grad_normed = kept(in_dot, left, right) + joined(received_refs)
        values_ = x_ref[...].astype(f32)
        scale_rows = rms_scale(values_)
        outs[0][...] = (grad_ref[...] + norm_back(grad_normed, values_, scale_rows, gain_ref[...])).astype(bf16)

        @pl.when(pl.program_id(0) == 0)
        def _():
            outs[1][...] = jnp.zeros(outs[1].shape, f32)

        outs[1][...] += column_sums(grad_normed * values_ * scale_rows)

    grad_rows, gain_one_sums = sum_rows_call(
        in_body,
        mine * tiles_half,
        in_lhs,
        in_rhs,
        [*[(r, "plain") for r in received_in], (x, "shifted"), (grad_hidden, "plain"), (gain_one, "whole")],
        [((half_rows, width), bf16), ((8, width), f32)],
        row_tile,
        "in_own",
    )
    sums = jnp.stack([gain_one_sums.sum(0), gain_two_sums.sum(0)])
    sums = sums + over_x(sums)
    token_parts, sums, qkv_sum, row_far = fence(arrange(grad_rows), sums, qkv_sum, row_far)

    qkv_x, qkv_y = over_x(qkv_sum), over_y(qkv_sum)
    layer_out = from_slots(layer_parts)
    token_parts, sums, qkv_x, qkv_y, layer_out = fence(token_parts, sums, qkv_x, qkv_y, layer_out)

    token_parts = to_slots(token_parts)
    qkv_last = over_y(qkv_x)
    where = jnp.stack([place, core]).astype(jnp.int32)
    both_pieces = [both_sum, both_y, both_x, both_last] + both_far
    grad_w_gate = unit_columns(where, both_pieces, n_shard, 0)
    grad_w_up = unit_columns(where, both_pieces, n_shard, 1)
    grad_w_down, grad_w_out = unit_rows(where, [row_sum, row_y, row_x, row_last] + row_far, unit_cols)
    for step in (over_core, over_y):
        sums = sums + step(sums)
    total = lax.dynamic_slice_in_dim(sums, shard * gain_width, gain_width, 1)
    for step in range(1, n_shard):
        to = lax.dynamic_slice_in_dim(sums, (shard + step) % n_shard * gain_width, gain_width, 1)
        total = total + lax.ppermute(to, "shard", [(z, (z + step) % n_shard) for z in range(n_shard)])
    head_grads = head_columns(where, both_cores([qkv_sum, qkv_y, qkv_x, qkv_last]))
    token_parts, grad_w_gate, grad_w_up, grad_w_down, grad_w_out, head_grads, total = fence(
        token_parts, grad_w_gate, grad_w_up, grad_w_down, grad_w_out, head_grads, total
    )
    grad_w_query, grad_w_key, grad_w_value = head_grads
    grad_tokens = from_slots(token_parts)

    return (
        layer_out,
        grad_tokens,
        total[0],
        grad_w_query,
        grad_w_key,
        grad_w_value,
        grad_w_out,
        total[1],
        grad_w_gate,
        grad_w_up,
        grad_w_down,
    )


def rope_tables(positions):
    half_dim = HEAD_DIM // 2
    frequency = rope_base ** (-2.0 * jnp.arange(half_dim, dtype=jnp.float32) / HEAD_DIM)
    angles = positions.astype(jnp.float32)[..., None] * frequency
    return (jnp.cos(angles), jnp.sin(angles))


def rotate(values, cosine, sine_table):
    half_dim = values.shape[-1] // 2
    first_half = values[..., :half_dim]
    second_half = values[..., half_dim:]
    cosine = cosine[..., None, :]
    sine_table = sine_table[..., None, :]
    return jnp.concatenate(
        [
            first_half * cosine - second_half * sine_table,
            second_half * cosine + first_half * sine_table,
        ],
        axis=-1,
    )


def general_layer(
    tokens,
    span_order,
    token_positions,
    attn_gain,
    w_query,
    w_key,
    w_value,
    w_out,
    mlp_gain,
    w_gate,
    w_up,
    w_down,
    cotangent,
):
    seq_dev, local_len, model_width = tokens.shape
    row_count = seq_dev * local_len
    groups = HEADS // KV_HEADS
    kv_width = KV_HEADS * HEAD_DIM
    score_scale = HEAD_DIM ** (-0.5)
    full_len = local_len * lax.axis_size("ctx")
    ctx_index = lax.axis_index("ctx")
    slot_index = jnp.arange(full_len, dtype=jnp.int32)
    key_index = span_order[:, slot_index // SPAN] * SPAN + slot_index[None, :] % SPAN
    query_index = lax.dynamic_slice_in_dim(key_index, ctx_index * local_len, local_len, 1)
    allowed = query_index[:, :, None] >= key_index[:, None, :]
    cosine, sine_table = rope_tables(token_positions)
    gain_one, wq_full, wk_full, wv_full, wo_full = (
        lax.all_gather(attn_gain, "shard", axis=0, tiled=True),
        lax.all_gather(w_query, "shard", axis=0, tiled=True),
        lax.all_gather(w_key, "shard", axis=0, tiled=True),
        lax.all_gather(w_value, "shard", axis=0, tiled=True),
        lax.all_gather(w_out, "shard", axis=0, tiled=True),
    )
    x_rows = tokens.reshape(row_count, model_width).astype(jnp.float32)
    scale_one = rms_scale(x_rows)
    normed = (x_rows * scale_one * gain_one).astype(jnp.bfloat16)
    queries = rotate(
        matmul(normed, wq_full).reshape(seq_dev, local_len, HEADS, HEAD_DIM), cosine, sine_table
    ).astype(jnp.bfloat16)
    keys_local = rotate(
        matmul(normed, wk_full).reshape(seq_dev, local_len, KV_HEADS, HEAD_DIM), cosine, sine_table
    ).astype(jnp.bfloat16)
    values_local = matmul(normed, wv_full).astype(jnp.bfloat16)
    keys_all, values_all = (
        lax.all_gather(keys_local.reshape(seq_dev, local_len, kv_width), "ctx", axis=1, tiled=True),
        lax.all_gather(
            values_local.reshape(seq_dev, local_len, kv_width), "ctx", axis=1, tiled=True
        ),
    )
    query_heads = queries.reshape(seq_dev, local_len, KV_HEADS, groups, HEAD_DIM).transpose(
        2, 0, 1, 3, 4
    )
    key_heads = keys_all.reshape(seq_dev, full_len, KV_HEADS, HEAD_DIM).transpose(2, 0, 1, 3)
    value_heads = values_all.reshape(seq_dev, full_len, KV_HEADS, HEAD_DIM).transpose(2, 0, 1, 3)

    def scores_of(query_head, key_head):
        raw_scores = (
            jnp.einsum("sqjd,skd->sjqk", query_head, key_head, preferred_element_type=jnp.float32)
            * score_scale
        )
        return jnp.where(allowed[:, None], raw_scores, masked_value)

    def attend_head(pieces):
        query_head, key_head, value_head = pieces
        scores = scores_of(query_head, key_head)
        row_max = jnp.max(scores, axis=-1, keepdims=True)
        exponent = jnp.exp(scores - row_max)
        row_total = jnp.sum(exponent, axis=-1, keepdims=True)
        probabilities = (exponent / row_total).astype(jnp.bfloat16)
        mixed_head = jnp.einsum(
            "sjqk,skd->sqjd", probabilities, value_head, preferred_element_type=jnp.float32
        )
        return (mixed_head, row_max[..., 0] + jnp.log(row_total[..., 0]))

    mixed_heads, log_totals = lax.map(attend_head, (query_heads, key_heads, value_heads))
    mixed_low = (
        mixed_heads.transpose(1, 2, 0, 3, 4).reshape(row_count, model_width).astype(jnp.bfloat16)
    )
    hidden = x_rows + matmul(mixed_low, wo_full)
    scale_two = rms_scale(hidden)
    gain_two, wg_full, wu_full, wd_full = (
        lax.all_gather(mlp_gain, "shard", axis=0, tiled=True),
        lax.all_gather(w_gate, "shard", axis=0, tiled=True),
        lax.all_gather(w_up, "shard", axis=0, tiled=True),
        lax.all_gather(w_down, "shard", axis=0, tiled=True),
    )
    normed_two = (hidden * scale_two * gain_two).astype(jnp.bfloat16)
    gate_pre = matmul(normed_two, wg_full)
    up_pre = matmul(normed_two, wu_full)
    sigmoid_gate = jax.nn.sigmoid(gate_pre)
    activated = gate_pre * sigmoid_gate
    product = (activated * up_pre).astype(jnp.bfloat16)
    layer_out = (hidden + matmul(product, wd_full)).astype(jnp.bfloat16).reshape(tokens.shape)
    grad_out = cotangent.reshape(row_count, model_width)
    gain_two_back, wg_back, wu_back, wd_back = (
        lax.all_gather(mlp_gain, "shard", axis=0, tiled=True),
        lax.all_gather(w_gate, "shard", axis=0, tiled=True),
        lax.all_gather(w_up, "shard", axis=0, tiled=True),
        lax.all_gather(w_down, "shard", axis=0, tiled=True),
    )
    grad_product = matmul(grad_out, wd_back.T)
    grad_w_down = matmul(product.T, grad_out)
    grad_gate = (
        grad_product * up_pre * sigmoid_gate * (1.0 + gate_pre * (1.0 - sigmoid_gate))
    ).astype(jnp.bfloat16)
    grad_up = (grad_product * activated).astype(jnp.bfloat16)
    grad_w_gate = matmul(normed_two.T, grad_gate)
    grad_w_up = matmul(normed_two.T, grad_up)
    grad_normed_two = matmul(grad_gate, wg_back.T) + matmul(grad_up, wu_back.T)
    gain_two_f = gain_two_back.astype(jnp.float32)
    grad_mlp_gain = jnp.sum(grad_normed_two * hidden * scale_two, axis=0)
    grad_hidden = grad_out.astype(jnp.float32) + norm_back(
        grad_normed_two, hidden, scale_two, gain_two_f
    )
    gain_one_back, wq_back, wk_back, wv_back, wo_back = (
        lax.all_gather(attn_gain, "shard", axis=0, tiled=True),
        lax.all_gather(w_query, "shard", axis=0, tiled=True),
        lax.all_gather(w_key, "shard", axis=0, tiled=True),
        lax.all_gather(w_value, "shard", axis=0, tiled=True),
        lax.all_gather(w_out, "shard", axis=0, tiled=True),
    )
    grad_attended = grad_hidden.astype(jnp.bfloat16)
    grad_w_out = matmul(mixed_low.T, grad_attended)
    grad_mixed = matmul(grad_attended, wo_back.T).astype(jnp.bfloat16)
    grad_heads = grad_mixed.reshape(seq_dev, local_len, KV_HEADS, groups, HEAD_DIM).transpose(
        2, 0, 1, 3, 4
    )

    def attend_back(pieces):
        query_head, key_head, value_head, grad_head, log_total = pieces
        scores = scores_of(query_head, key_head)
        probabilities = jnp.exp(scores - log_total[..., None])
        grad_probs = jnp.einsum(
            "sqjd,skd->sjqk", grad_head, value_head, preferred_element_type=jnp.float32
        )
        inner_sum = jnp.sum(probabilities * grad_probs, axis=-1, keepdims=True)
        grad_scores = (probabilities * (grad_probs - inner_sum)).astype(jnp.bfloat16)
        grad_query = (
            jnp.einsum("sjqk,skd->sqjd", grad_scores, key_head, preferred_element_type=jnp.float32)
            * score_scale
        )
        grad_key = (
            jnp.einsum(
                "sjqk,sqjd->skd", grad_scores, query_head, preferred_element_type=jnp.float32
            )
            * score_scale
        )
        grad_value = jnp.einsum(
            "sjqk,sqjd->skd",
            probabilities.astype(jnp.bfloat16),
            grad_head,
            preferred_element_type=jnp.float32,
        )
        return (grad_query, grad_key, grad_value)

    grad_queries, key_terms, value_terms = lax.map(
        attend_back, (query_heads, key_heads, value_heads, grad_heads, log_totals)
    )
    key_terms = key_terms.transpose(1, 2, 0, 3).reshape(seq_dev, full_len, kv_width)
    value_terms = value_terms.transpose(1, 2, 0, 3).reshape(seq_dev, full_len, kv_width)
    grad_keys, grad_values = (
        lax.psum_scatter(
            key_terms.astype(jnp.bfloat16), "ctx", scatter_dimension=1, tiled=True
        ).astype(jnp.float32),
        lax.psum_scatter(
            value_terms.astype(jnp.bfloat16), "ctx", scatter_dimension=1, tiled=True
        ).astype(jnp.float32),
    )
    grad_queries = grad_queries.transpose(1, 2, 0, 3, 4).reshape(
        seq_dev, local_len, HEADS, HEAD_DIM
    )
    grad_q_low = (
        rotate(grad_queries, cosine, -sine_table)
        .reshape(row_count, model_width)
        .astype(jnp.bfloat16)
    )
    grad_k_low = (
        rotate(grad_keys.reshape(seq_dev, local_len, KV_HEADS, HEAD_DIM), cosine, -sine_table)
        .reshape(row_count, kv_width)
        .astype(jnp.bfloat16)
    )
    grad_v_low = grad_values.reshape(row_count, kv_width).astype(jnp.bfloat16)
    grad_w_query = matmul(normed.T, grad_q_low)
    grad_w_key = matmul(normed.T, grad_k_low)
    grad_w_value = matmul(normed.T, grad_v_low)
    grad_normed = (
        matmul(grad_q_low, wq_back.T)
        + matmul(grad_k_low, wk_back.T)
        + matmul(grad_v_low, wv_back.T)
    )
    gain_one_f = gain_one_back.astype(jnp.float32)
    grad_attn_gain = jnp.sum(grad_normed * x_rows * scale_one, axis=0)
    grad_tokens = (grad_hidden + norm_back(grad_normed, x_rows, scale_one, gain_one_f)).astype(
        jnp.bfloat16
    )
    grad_tokens = grad_tokens.reshape(tokens.shape)
    part_gain_two, part_gate, part_up, part_down = (
        lax.psum_scatter(
            grad_mlp_gain.astype(jnp.bfloat16), "shard", scatter_dimension=0, tiled=True
        ).astype(jnp.float32),
        lax.psum_scatter(
            grad_w_gate.astype(jnp.bfloat16), "shard", scatter_dimension=0, tiled=True
        ).astype(jnp.float32),
        lax.psum_scatter(
            grad_w_up.astype(jnp.bfloat16), "shard", scatter_dimension=0, tiled=True
        ).astype(jnp.float32),
        lax.psum_scatter(
            grad_w_down.astype(jnp.bfloat16), "shard", scatter_dimension=0, tiled=True
        ).astype(jnp.float32),
    )
    part_gain_one, part_query, part_key, part_value, part_out = (
        lax.psum_scatter(
            grad_attn_gain.astype(jnp.bfloat16), "shard", scatter_dimension=0, tiled=True
        ).astype(jnp.float32),
        lax.psum_scatter(
            grad_w_query.astype(jnp.bfloat16), "shard", scatter_dimension=0, tiled=True
        ).astype(jnp.float32),
        lax.psum_scatter(
            grad_w_key.astype(jnp.bfloat16), "shard", scatter_dimension=0, tiled=True
        ).astype(jnp.float32),
        lax.psum_scatter(
            grad_w_value.astype(jnp.bfloat16), "shard", scatter_dimension=0, tiled=True
        ).astype(jnp.float32),
        lax.psum_scatter(
            grad_w_out.astype(jnp.bfloat16), "shard", scatter_dimension=0, tiled=True
        ).astype(jnp.float32),
    )
    summed = (
        lax.psum(part_gain_one.astype(jnp.bfloat16), ("ctx", "batch")).astype(jnp.float32),
        lax.psum(part_query.astype(jnp.bfloat16), ("ctx", "batch")).astype(jnp.float32),
        lax.psum(part_key.astype(jnp.bfloat16), ("ctx", "batch")).astype(jnp.float32),
        lax.psum(part_value.astype(jnp.bfloat16), ("ctx", "batch")).astype(jnp.float32),
        lax.psum(part_out.astype(jnp.bfloat16), ("ctx", "batch")).astype(jnp.float32),
        lax.psum(part_gain_two.astype(jnp.bfloat16), ("ctx", "batch")).astype(jnp.float32),
        lax.psum(part_gate.astype(jnp.bfloat16), ("ctx", "batch")).astype(jnp.float32),
        lax.psum(part_up.astype(jnp.bfloat16), ("ctx", "batch")).astype(jnp.float32),
        lax.psum(part_down.astype(jnp.bfloat16), ("ctx", "batch")).astype(jnp.float32),
    )
    return (
        layer_out,
        grad_tokens,
        summed[0],
        summed[1],
        summed[2],
        summed[3],
        summed[4],
        summed[5],
        summed[6],
        summed[7],
        summed[8],
    )


def fits(mesh):
    split = mesh.shape["ctx"] // 2
    return split == 2 and mesh.shape["batch"] == 2 and mesh.shape["shard"] * split == KV_HEADS and mesh.shape["shard"] == 4


def solution(mesh):
    in_specs = (
        P(("shard", "batch"), "ctx", None),
        P(("shard", "batch"), None),
        P(("shard", "batch"), "ctx"),
        P("shard"),
        P("shard", None),
        P("shard", None),
        P("shard", None),
        P("shard", None),
        P("shard"),
        P("shard", None),
        P("shard", None),
        P("shard", None),
        P(("shard", "batch"), "ctx", None),
    )
    out_specs = (
        P(("shard", "batch"), "ctx", None),
        P(("shard", "batch"), "ctx", None),
        P("shard"),
        P("shard", None),
        P("shard", None),
        P("shard", None),
        P("shard", None),
        P("shard"),
        P("shard", None),
        P("shard", None),
        P("shard", None),
    )
    layer = chip_layer if fits(mesh) else general_layer
    return jax.shard_map(layer, mesh=mesh, in_specs=in_specs, out_specs=out_specs, check_vma=False)
```

```python
import functools

import jax
import jax.numpy as jnp
import numpy as np
from jax import lax
from jax.experimental import pallas as pl
from jax.experimental.pallas import tpu as pltpu
from jax.sharding import PartitionSpec as P

HEADS = 16
KV_HEADS = 8
HEAD_DIM = 96
SPAN = 128
GROUPS = HEADS // KV_HEADS
HALF = HEAD_DIM // 2
LANES = 128
SLOT = LANES // 2
GROUP_COLS = (GROUPS + 2) * HEAD_DIM
Q_COLS = GROUPS * HEAD_DIM
Q_LANES = GROUPS * LANES
PAD_ROWS = 16

norm_eps = 1e-05
rope_base = 100000.0
masked_value = -1e30
score_scale = HEAD_DIM ** (-0.5)
exp2_scale = score_scale * 1.4426950408889634

bf16 = jnp.bfloat16
f32 = jnp.float32
MIB = 1 << 20
NT = (((1,), (1,)), ((), ()))
TN = (((0,), (0,)), ((), ()))


def rms_scale(values):
    return lax.rsqrt(jnp.mean(values * values, axis=-1, keepdims=True) + norm_eps)


def matmul(left, right):
    return jnp.dot(left, right, preferred_element_type=f32)


def dot_nt(left, right):
    return lax.dot_general(left, right, NT, preferred_element_type=f32)


def dot_tn(left, right):
    return lax.dot_general(left, right, TN, preferred_element_type=f32)


def params(limit):
    return pltpu.CompilerParams(vmem_limit_bytes=limit * MIB)


def short():
    return pl.CostEstimate(flops=1000, bytes_accessed=1000, transcendentals=0)


def whole(shape):
    return pl.BlockSpec(shape, lambda *_: (0,) * len(shape))


def part(block, index):
    return pl.BlockSpec(block, lambda *_: index, pipeline_mode=pl.Buffered(1))


def fixed(shape):
    return part(shape, (0,) * len(shape))


def call(kernel, grid, in_specs, out_specs, out_shape, operands, name, prefetch=(), scratch=(), limit=60):
    return pl.pallas_call(
        kernel,
        grid_spec=pltpu.PrefetchScalarGridSpec(
            num_scalar_prefetch=len(prefetch), grid=grid, in_specs=in_specs, out_specs=out_specs, scratch_shapes=list(scratch)
        ),
        out_shape=[jax.ShapeDtypeStruct(shape, dtype) for shape, dtype in out_shape],
        compiler_params=params(limit),
        cost_estimate=short(),
        name=name,
    )(*prefetch, *operands)


def spread_matrix():
    spread = np.zeros((GROUP_COLS, (GROUPS + 2) * LANES), np.float32)
    for row in range(spread.shape[0]):
        head, feature = divmod(row, HEAD_DIM)
        half, place = divmod(feature, HALF)
        spread[row, head * LANES + half * SLOT + place] = 1.0
    return spread


def front_kernel(near_ref, far_ref, flag_ref, *refs):
    spans = 4
    near, far, refs = refs[:spans], refs[spans : 2 * spans], refs[2 * spans :]
    cos_ref, sin_ref, gain_ref, spread_ref, w0, w1, w2, w3a, w3b, x_out, n_out, nt_out, q_out, k_out, v_out, w_out = refs
    q_width, k_width = q_out.shape[1], k_out.shape[1]
    step_at = pl.program_id(0)

    @pl.when(step_at == 0)
    def _():
        depth = w0.shape[1]
        halves = w3a.shape[0]
        for at, piece in enumerate((w0, w1, w2, None)):
            for z in range(w0.shape[0]):
                block = piece[z] if piece is not None else (w3a[z] if z < halves else w3b[z - halves])
                spread = matmul(block, spread_ref[...]).astype(bf16)
                rows = slice(z * depth, (z + 1) * depth)
                w_out[rows, Q_LANES * at : Q_LANES * (at + 1)] = spread[:, :Q_LANES]
                w_out[rows, q_width + LANES * at : q_width + LANES * (at + 1)] = spread[:, Q_LANES : Q_LANES + LANES]
                at_v = q_width + k_width + LANES * at
                w_out[rows, at_v : at_v + LANES] = spread[:, Q_LANES + LANES :]

    for k in range(spans):
        rows = slice(k * SPAN, (k + 1) * SPAN)

        @pl.when(flag_ref[spans * step_at + k] == 0)
        def _():
            x_out[rows, :] = near[k][0]

        @pl.when(flag_ref[spans * step_at + k] != 0)
        def _():
            x_out[rows, :] = far[k][0]

    x = x_out[...].astype(f32)
    normed = (x * rms_scale(x) * gain_ref[...]).astype(bf16)
    n_out[...] = normed
    nt_out[...] = normed.T
    cosine, sine = cos_ref[...], sin_ref[...]
    lane = lax.broadcasted_iota(jnp.int32, (1, LANES), 1)
    ones = jnp.where((lane >= HALF) & (lane < HALF + 3), 1.0, 0.0)
    step = 4 * LANES
    for start in range(0, w_out.shape[1], step):
        raw = matmul(normed, w_out[:, start : start + step])
        for piece in range(0, step, LANES):
            at = start + piece
            head = raw[:, piece : piece + LANES]
            if at < q_width + k_width:
                head = head * cosine + pltpu.roll(head, SLOT, 1) * sine
            if at < q_width:
                q_out[:, at : at + LANES] = head.astype(bf16)
            elif at < q_width + k_width:
                k_out[:, at - q_width : at - q_width + LANES] = (head + ones).astype(bf16)
            else:
                v_out[:, at - q_width - k_width : at - q_width - k_width + LANES] = (head + ones).astype(bf16)


def span_specs(width, count):
    def near(k):
        return pl.BlockSpec((1, SPAN, width), lambda i, near, far, flag: (near[count * i + k], 0, 0))

    def far(k):
        return pl.BlockSpec((1, SPAN, width), lambda i, near, far, flag: (far[count * i + k], 0, 0))

    return [near(k) for k in range(count)] + [far(k) for k in range(count)]


def as_spans(array):
    return array.reshape(array.shape[0] // SPAN, SPAN, array.shape[1])


def front(places, near, far, cosine, sine, gain, pieces):
    rows, width = 2 * near.shape[0], near.shape[1]
    groups = len(pieces) - 1
    n_shard = pieces[0].shape[0]
    depth = width // n_shard
    spread = jnp.asarray(spread_matrix(), bf16)
    spans = 4
    tile = spans * SPAN
    q_width, k_width = groups * Q_LANES, groups * LANES
    total = q_width + 2 * k_width

    def rows_spec(cols):
        return pl.BlockSpec((tile, cols), lambda i, *_: (i, 0))

    near, far = as_spans(near), as_spans(far)
    return call(
        front_kernel,
        (rows // tile,),
        span_specs(width, spans)
        + [rows_spec(LANES), rows_spec(LANES), fixed(gain.shape), fixed(spread.shape)]
        + [part((p.shape[0], depth, p.shape[2]), (0, 0, 0)) for p in pieces],
        [rows_spec(width), rows_spec(width), pl.BlockSpec((width, tile), lambda i, *_: (0, i))]
        + [rows_spec(q_width), rows_spec(k_width), rows_spec(k_width), whole((n_shard * depth, total))],
        [
            ((rows, width), bf16),
            ((rows, width), bf16),
            ((width, rows), bf16),
            ((rows, q_width), bf16),
            ((rows, k_width), bf16),
            ((rows, k_width), bf16),
            ((n_shard * depth, total), bf16),
        ],
        [near] * spans + [far] * spans + [cosine, sine, gain, spread, *pieces],
        "front",
        places,
    )


def span_copy(places, source):
    width = source.shape[1]
    count = places.shape[0]
    step = 2

    def kernel(place_ref, *refs):
        for k in range(step):
            refs[step][k] = refs[k][0]

    spans = as_spans(source)
    (out,) = call(
        kernel,
        (count // step,),
        [pl.BlockSpec((1, SPAN, width), lambda i, place, k=k: (place[step * i + k], 0, 0)) for k in range(step)],
        [pl.BlockSpec((step, SPAN, width), lambda i, place: (i, 0, 0))],
        [((count, SPAN, width), source.dtype)],
        [spans] * step,
        "span_copy",
        [places],
    )
    return out.reshape(count * SPAN, width)


def span_join(places, near, far):
    width = near.shape[1]
    count = 2 * near.shape[0] // SPAN
    step = 4

    def kernel(near_ref, far_ref, flag_ref, *refs):
        out_ref = refs[-1]
        for k in range(step):
            is_far = flag_ref[step * pl.program_id(0) + k] != 0

            @pl.when(jnp.logical_not(is_far))
            def _():
                out_ref[k] = refs[k][0]

            @pl.when(is_far)
            def _():
                out_ref[k] = refs[step + k][0]

    (out,) = call(
        kernel,
        (count // step,),
        span_specs(width, step),
        [pl.BlockSpec((step, SPAN, width), lambda i, *_: (i, 0, 0))],
        [((count, SPAN, width), near.dtype)],
        [as_spans(near)] * step + [as_spans(far)] * step,
        "span_join",
        places,
    )
    return out.reshape(count * SPAN, width)


def three_parts(values):
    first = values.astype(bf16).astype(f32)
    second = (values - first).astype(bf16).astype(f32)
    third = values - first - second
    return first, second, third


def with_lanes(block, column):
    lane = lax.broadcasted_iota(jnp.int32, block.shape, 1)
    first, second, third = three_parts(column)
    wide = block.astype(f32)
    wide = jnp.where(lane == HALF, first, wide)
    wide = jnp.where(lane == HALF + 1, second, wide)
    wide = jnp.where(lane == HALF + 2, third, wide)
    return wide.astype(bf16)


Q_TILE = 256
K_CHUNK = 512


def heads_down(block):
    return jnp.concatenate([block[:, LANES * h : LANES * (h + 1)] for h in range(GROUPS)], axis=0)


def attend_kernel(q_ref, k_ref, v_ref, mixed_ref, q_aug_ref):
    rows = q_ref.shape[0]
    for tile in range(rows // Q_TILE):
        first_row = tile * Q_TILE
        query = heads_down(q_ref[first_row : first_row + Q_TILE, :])
        end = first_row + Q_TILE
        top = acc = None
        for start in range(0, end, K_CHUNK):
            size = min(K_CHUNK, end - start)
            key = k_ref[start : start + size, :]
            value = v_ref[start : start + size, :]
            scores = dot_nt(query, key)
            if start + size > first_row:
                row = lax.broadcasted_iota(jnp.int32, (Q_TILE, size), 0) + first_row
                column = lax.broadcasted_iota(jnp.int32, (Q_TILE, size), 1) + start
                allowed = row >= column
                scores = jnp.where(jnp.concatenate([allowed] * GROUPS, axis=0), scores, masked_value)
            chunk_top = jnp.max(scores, axis=-1, keepdims=True)
            new_top = chunk_top if top is None else jnp.maximum(top, chunk_top)
            weights = jnp.exp2((scores - new_top) * exp2_scale).astype(bf16)
            part = matmul(weights, value)
            acc = part if top is None else acc * jnp.exp2((top - new_top) * exp2_scale) + part
            top = new_top
        total = acc[:, HALF : HALF + 1]
        mixed = (acc * (1.0 / total)).astype(bf16)
        log_total = top + jnp.log2(total) * (1.0 / exp2_scale)
        marked = with_lanes(query, -log_total)
        for h in range(GROUPS):
            mixed_ref[first_row : first_row + Q_TILE, LANES * h : LANES * (h + 1)] = mixed[Q_TILE * h : Q_TILE * (h + 1)]
            q_aug_ref[first_row : first_row + Q_TILE, LANES * h : LANES * (h + 1)] = marked[Q_TILE * h : Q_TILE * (h + 1)]


def attend(queries, keys, values):
    rows, k_width = keys.shape
    groups = k_width // LANES
    pair = pl.BlockSpec((rows, Q_LANES), lambda g: (0, g))
    single = pl.BlockSpec((rows, LANES), lambda g: (0, g))
    return call(
        attend_kernel, (groups,), [pair, single, single], [pair, pair], [(queries.shape, bf16)] * 2, [queries, keys, values], "attend"
    )


def attend_back_kernel(q_ref, k_ref, v_ref, do_ref, o_ref, cos_ref, sin_ref, dq_ref, dk_ref, dv_ref, q_s, do_s, dq_s, dk_s, dv_s):
    rows = q_ref.shape[0]
    tiles = rows // Q_TILE
    for tile in range(tiles):
        at = slice(tile * Q_TILE, (tile + 1) * Q_TILE)
        q_s[tile] = heads_down(q_ref[at, :])
        grad = heads_down(do_ref[at, :])
        inner = jnp.sum(grad.astype(f32) * heads_down(o_ref[at, :]).astype(f32), axis=-1, keepdims=True)
        do_s[tile] = with_lanes(grad, -inner)
        dq_s[tile] = jnp.zeros(dq_s.shape[1:], f32)

    def unit(tile, key_start, size, mask_from):
        key = k_ref[key_start : key_start + size, :]
        value = v_ref[key_start : key_start + size, :]
        query, grad = q_s[tile], do_s[tile]
        probs = jnp.exp2(dot_nt(key, query) * exp2_scale)
        if mask_from is not None:
            row = lax.broadcasted_iota(jnp.int32, (size, Q_TILE), 0)
            column = lax.broadcasted_iota(jnp.int32, (size, Q_TILE), 1) + mask_from
            allowed = jnp.concatenate([row <= column] * GROUPS, axis=1)
            probs = jnp.where(allowed, probs, 0.0)
        d_scores = (probs * dot_nt(value, grad)).astype(bf16)
        dv_s[:size] += matmul(probs.astype(bf16), grad)
        dk_s[:size] += matmul(d_scores, query)
        dq_s[tile] += dot_tn(d_scores, key)

    for key_start in range(0, rows, K_CHUNK):
        dk_s[...] = jnp.zeros(dk_s.shape, f32)
        dv_s[...] = jnp.zeros(dv_s.shape, f32)
        tile = key_start // Q_TILE
        unit(tile, key_start, Q_TILE, 0)
        unit(tile + 1, key_start, K_CHUNK, Q_TILE)
        if tile + 2 < tiles:

            @pl.loop(tile + 2, tiles)
            def _(later):
                unit(later, key_start, K_CHUNK, None)

        at = slice(key_start, key_start + K_CHUNK)
        turned = dk_s[...] * score_scale
        turned = turned * cos_ref[at, :] - pltpu.roll(turned, SLOT, 1) * sin_ref[at, :]
        dk_ref[at, :] = turned.astype(bf16)
        dv_ref[at, :] = dv_s[...].astype(bf16)
    for tile in range(tiles):
        at = slice(tile * Q_TILE, (tile + 1) * Q_TILE)
        cosine, sine = cos_ref[at, :], sin_ref[at, :]
        for h in range(GROUPS):
            turned = dq_s[tile, Q_TILE * h : Q_TILE * (h + 1), :] * score_scale
            turned = turned * cosine - pltpu.roll(turned, SLOT, 1) * sine
            dq_ref[at, LANES * h : LANES * (h + 1)] = turned.astype(bf16)


def attend_back(first, groups, q_aug, keys, values, grad, mixed, cosine, sine):
    rows = keys.shape[0]
    tiles = rows // Q_TILE
    pair = pl.BlockSpec((rows, Q_LANES), lambda g: (0, g + first))
    single = pl.BlockSpec((rows, LANES), lambda g: (0, g + first))
    pair_out = pl.BlockSpec((rows, Q_LANES), lambda g: (0, g))
    single_out = pl.BlockSpec((rows, LANES), lambda g: (0, g))
    stacked = (tiles, GROUPS * Q_TILE, LANES)
    table = fixed((rows, LANES))
    return call(
        attend_back_kernel,
        (groups,),
        [pair, single, single, pair, pair, table, table],
        [pair_out, single_out, single_out],
        [((rows, groups * Q_LANES), bf16), ((rows, groups * LANES), bf16), ((rows, groups * LANES), bf16)],
        [q_aug, keys, values, grad, mixed, cosine, sine],
        "attend_back",
        scratch=[
            pltpu.VMEM(stacked, bf16),
            pltpu.VMEM(stacked, bf16),
            pltpu.VMEM(stacked, f32),
            pltpu.VMEM((K_CHUNK, LANES), f32),
            pltpu.VMEM((K_CHUNK, LANES), f32),
        ],
    )


def flat(block):
    return block.reshape(block.shape[0] * block.shape[1], block.shape[2])


def down_columns(down_ref, j, zs):
    rows = down_ref.shape[1] // 3
    return jnp.concatenate([down_ref[z, rows * j : rows * (j + 1), :] for z in zs], axis=0)


def hidden_kernel(n_ref, cot_ref, gate_ref, up_ref, down_ref, product_ref, dboth_ref):
    n_shard, units = gate_ref.shape[0], gate_ref.shape[2]
    third = cot_ref.shape[1] // 3
    step = 256
    for start in range(0, units, step):
        at = slice(start, start + step)
        zs = range(start * n_shard // units, (start + step) * n_shard // units)
        gate = matmul(n_ref[...], flat(gate_ref[:, :, at]))
        up = matmul(n_ref[...], flat(up_ref[:, :, at]))
        d_product = sum(dot_nt(cot_ref[:, third * j : third * (j + 1)], down_columns(down_ref, j, zs)) for j in range(3))
        sigmoid = 1.0 / (1.0 + jnp.exp(-gate))
        silu = gate * sigmoid
        product_ref[:, at] = (silu * up).astype(bf16)
        dboth_ref[:, at] = (d_product * up * sigmoid * (1.0 + gate * (1.0 - sigmoid))).astype(bf16)
        dboth_ref[:, units + start : units + start + step] = (d_product * silu).astype(bf16)


def feed_grads(normed_t, cot, product, d_both):
    width, rows = normed_t.shape
    units = product.shape[1]
    steps = width // units

    def kernel(n_ref, cot_ref, product_ref, both_ref, gate_ref, up_ref, down_ref, turned_ref):
        step = pl.program_id(0)

        @pl.when(step < steps)
        def _():
            gate_ref[...] = matmul(n_ref[...], both_ref[:, :units]).astype(bf16)
            up_ref[...] = matmul(n_ref[...], both_ref[:, units:]).astype(bf16)

        @pl.when(step == steps)
        def _():
            turned_ref[...] = product_ref[...].T

        @pl.when(step >= steps)
        def _():
            down_ref[...] = matmul(turned_ref[...], cot_ref[...]).astype(bf16)

    early = lambda i: (jnp.minimum(i, steps - 1), 0)
    late = lambda i: (0, jnp.maximum(i - steps, 0))
    return call(
        kernel,
        (2 * steps,),
        [pl.BlockSpec((units, rows), early), pl.BlockSpec((rows, units), late), fixed(product.shape), fixed(d_both.shape)],
        [pl.BlockSpec((units, units), early), pl.BlockSpec((units, units), early), pl.BlockSpec((units, units), late)],
        [((width, units), bf16), ((width, units), bf16), ((units, width), bf16)],
        [normed_t, cot, product, d_both],
        "feed_grads",
        scratch=[pltpu.VMEM((units, rows), bf16)],
    )


def whole_of(array):
    return array, array.shape, (0,) * array.ndim


def third_of(array, index):
    rows = 384
    return array, (array.shape[0], rows, array.shape[2]), (0, index, 0)


def hidden_units(normed, cot, weights):
    rows, width = normed.shape
    units = weights[0][0].shape[2]
    tile = 512
    wide = pl.BlockSpec((tile, width), lambda i: (i, 0))
    thin = pl.BlockSpec((tile, units), lambda i: (i, 0))
    return call(
        hidden_kernel,
        (rows // tile,),
        [wide, wide] + [part(block, index) for _, block, index in weights],
        [thin, pl.BlockSpec((tile, 2 * units), lambda i: (i, 0))],
        [((rows, units), bf16), ((rows, 2 * units), bf16)],
        [normed, cot] + [a for a, _, _ in weights],
        "hidden_units",
    )


def sum_rows_call(body, base, lhs, rhs, others, outs, tile, name):
    rows = outs[0][0][0]

    def shifted(cols):
        return pl.BlockSpec((tile, cols), lambda i, base: (base[0] + i, 0))

    def plain(cols):
        return pl.BlockSpec((tile, cols), lambda i, base: (i, 0))

    in_specs = [shifted(a.shape[1]) for a in lhs] + [part(block, index) for _, block, index in rhs]
    for a, kind in others:
        in_specs.append(fixed(a.shape) if kind == "whole" else {"shifted": shifted, "plain": plain}[kind](a.shape[1]))
    out_specs = [plain(shape[1]) if shape[0] == rows else whole(shape) for shape, _ in outs]
    n_lhs, n_rhs, n_other = len(lhs), len(rhs), len(others)

    def kernel(base_ref, *refs):
        left, refs = refs[:n_lhs], refs[n_lhs:]
        right, refs = refs[:n_rhs], refs[n_rhs:]
        body(left, right, refs[:n_other], refs[n_other:])

    return call(
        kernel,
        (rows // tile,),
        in_specs,
        out_specs,
        outs,
        [*lhs, *[a for a, _, _ in rhs], *[a for a, _ in others]],
        name,
        [base],
    )


def norm_back(grad_normed, values, scale_rows, gain):
    scaled = grad_normed * gain
    return scale_rows * scaled - values * (scale_rows * scale_rows * scale_rows) * jnp.mean(scaled * values, axis=-1, keepdims=True)


def column_sums(values):
    return jnp.sum(values.reshape(-1, 8, values.shape[-1]), axis=0)


def half_specs(tile, tiles, width):
    own = pl.BlockSpec((tile, width), lambda i, core: (jnp.clip(i - tiles * core[0], 0, tiles - 1), 0))
    far = pl.BlockSpec((tile, width), lambda i, core: (jnp.clip(i - tiles * (1 - core[0]), 0, tiles - 1), 0))
    return [own, far]


def place_half(core_ref, tiles, own_refs, far_refs, out_ref):
    is_own = pl.program_id(0) // tiles == core_ref[0]

    def place(refs):
        start = 0
        for ref in refs:
            out_ref[:, start : start + ref.shape[1]] = ref[...]
            start += ref.shape[1]

    @pl.when(is_own)
    def _():
        place(own_refs)

    @pl.when(jnp.logical_not(is_own))
    def _():
        place(far_refs)


def join_halves(core, own, far):
    rows, cols = own[0].shape
    count = len(own)
    width = count * cols
    tile = 256
    tiles = rows // tile

    def kernel(core_ref, *refs):
        out_ref, turned_ref = refs[2 * count :]
        place_half(core_ref, tiles, refs[:count], refs[count : 2 * count], out_ref)
        turned_ref[...] = out_ref[...].T

    own_spec, far_spec = half_specs(tile, tiles, cols)
    return call(
        kernel,
        (2 * tiles,),
        [own_spec] * count + [far_spec] * count,
        [pl.BlockSpec((tile, width), lambda i, _: (i, 0)), pl.BlockSpec((width, tile), lambda i, _: (0, i))],
        [((2 * rows, width), bf16), ((width, 2 * rows), bf16)],
        [*own, *far],
        "join_halves",
        [core],
    )


def mixed_back(core, own, far, w_out_rows):
    rows, cols = own[0].shape
    count = len(own)
    width = count * cols
    heads = w_out_rows.shape[0]
    tile = 512
    tiles = rows // tile

    own_spec, far_spec = half_specs(tile, tiles, cols)

    def kernel(core_ref, *refs):
        w_ref, out_ref, grad_ref = refs[2 * count :]
        place_half(core_ref, tiles, refs[:count], refs[count : 2 * count], out_ref)
        grad_ref[...] = dot_nt(out_ref[...], w_ref[...]).astype(bf16)

    return call(
        kernel,
        (2 * tiles,),
        [own_spec] * count + [far_spec] * count + [fixed(w_out_rows.shape)],
        [pl.BlockSpec((tile, width), lambda i, _: (i, 0)), pl.BlockSpec((tile, heads), lambda i, _: (i, 0))],
        [((2 * rows, width), bf16), ((2 * rows, heads), bf16)],
        [*own, *far, w_out_rows],
        "mixed_back",
        [core],
    )


def out_rows(place, blocks):
    n_shard, rows_in, cols = blocks[0].shape
    chunks = rows_in // HALF
    quarters = len(blocks)
    shape = (quarters * quarters * SLOT, chunks * cols)

    def kernel(place_ref, *refs):
        out_ref = refs[-1]
        out_ref[...] = jnp.zeros(shape, bf16)
        for group in range(quarters):
            for at in range(quarters):
                row = pl.multiple_of(Q_LANES * group + SLOT * (at ^ place_ref[0]), SLOT)
                for j in range(chunks):
                    out_ref[pl.ds(row, HALF), cols * j : cols * (j + 1)] = refs[at][group ^ place_ref[0], HALF * j : HALF * (j + 1), :]

    (out,) = call(
        kernel,
        (1,),
        [fixed((n_shard, rows_in, cols))] * quarters,
        [whole(shape)],
        [(shape, bf16)],
        blocks,
        "out_rows",
        [place],
    )
    return out


def out_grad_blocks(place, mixed, grad):
    rows, heads = mixed.shape
    width = grad.shape[1]
    quarters = heads // Q_LANES
    tile = 512

    def kernel(place_ref, mixed_ref, grad_ref, *refs):
        outs = refs[:quarters]
        group = pl.program_id(0)
        sums = dot_tn(mixed_ref[...], grad_ref[...]).astype(bf16)
        refs[quarters][...] = sums
        shard = group ^ place_ref[0]
        for at in range(quarters):
            row = pl.multiple_of(SLOT * (at ^ place_ref[0]), SLOT)
            outs[at][shard] = refs[quarters][pl.ds(row, HALF), :]

    return call(
        kernel,
        (quarters,),
        [pl.BlockSpec((rows, Q_LANES), lambda g, _: (0, g)), fixed((rows, width))],
        [whole((quarters, HALF, width))] * quarters,
        [((quarters, HALF, width), bf16)] * quarters,
        [mixed, grad],
        "out_grads",
        [place],
        [pltpu.VMEM((Q_LANES, width), bf16)],
    )


def qkv_grad(normed_t, d_query, d_key, d_value):
    width, rows = normed_t.shape
    spread = jnp.asarray(spread_matrix(), bf16)
    tile = 512

    def kernel(n_ref, q_ref, k_ref, v_ref, spread_ref, out_ref):
        query = matmul(n_ref[...], q_ref[...]).astype(bf16)
        both = matmul(n_ref[...], jnp.concatenate([k_ref[...], v_ref[...]], axis=1)).astype(bf16)
        out_ref[...] = dot_nt(jnp.concatenate([query, both], axis=1), spread_ref[...]).astype(bf16)

    (out,) = call(
        kernel,
        (width // tile,),
        [
            pl.BlockSpec((tile, rows), lambda i: (i, 0)),
            fixed(d_query.shape),
            fixed(d_key.shape),
            fixed(d_value.shape),
            fixed(spread.shape),
        ],
        [pl.BlockSpec((tile, GROUP_COLS), lambda i: (i, 0))],
        [((width, GROUP_COLS), bf16)],
        [normed_t, d_query, d_key, d_value, spread],
        "qkv_grad",
    )
    return out


def unit_columns(where, pieces, n_shard, index):
    depth, cols = pieces[0].shape[0] // 2, pieces[0].shape[1]
    tile = 96
    count = len(pieces)
    quarters = count // 2
    unit_cols = cols // n_shard

    def kernel(where_ref, *refs):
        out_ref = refs[-1]
        for k in range(count):
            unit = quarters * (where_ref[1] ^ (k // quarters)) + (where_ref[0] ^ (k % quarters))
            for z in range(n_shard):
                at = pl.multiple_of((count * z + unit) * unit_cols, unit_cols)
                out_ref[:, pl.ds(at, unit_cols)] = refs[k][:, unit_cols * z : unit_cols * (z + 1)].astype(f32)

    steps = depth // tile
    (out,) = call(
        kernel,
        (depth // tile,),
        [pl.BlockSpec((tile, cols), lambda i, _: (index * steps + i, 0))] * count,
        [pl.BlockSpec((tile, cols * count), lambda i, _: (i, 0))],
        [((depth, cols * count), f32)],
        pieces,
        "unit_columns",
        [where],
    )
    return out


def unit_rows(where, pieces, down_depth):
    depth, width = pieces[0].shape
    count = len(pieces)
    quarters = count // 2
    out_depth = depth - down_depth

    def unit_at(i, where_ref):
        return quarters * (where_ref[1] ^ (i // quarters)) + (where_ref[0] ^ (i % quarters))

    def kernel(where_ref, *refs):
        for k in range(count):

            @pl.when(pl.program_id(0) == k)
            def _():
                refs[count][...] = refs[k][:down_depth, :].astype(f32)
                refs[count + 1][...] = refs[k][down_depth:, :].astype(f32)

    return call(
        kernel,
        (count,),
        [fixed((depth, width))] * count,
        [
            pl.BlockSpec((down_depth, width), lambda i, where: (unit_at(i, where), 0)),
            pl.BlockSpec((out_depth, width), lambda i, where: (unit_at(i, where), 0)),
        ],
        [((down_depth * count, width), f32), ((out_depth * count, width), f32)],
        pieces,
        "unit_rows",
        [where],
    )


def head_columns(where, pieces):
    depth, cols = pieces[0].shape
    count = len(pieces)
    quarters = count // 2
    split = 2

    def kernel(where_ref, *refs):
        q_out, k_out, v_out = refs[count:]
        place, core = where_ref[0], where_ref[1]
        row = lax.broadcasted_iota(jnp.int32, (cols, cols), 0)
        column = lax.broadcasted_iota(jnp.int32, (cols, cols), 1)

        def moved(piece, start, size, to):
            chosen = (row >= start) & (row < start + size) & (row - start == column - to)
            return matmul(piece, jnp.where(chosen, 1.0, 0.0).astype(bf16))

        for at in range(quarters):
            total = 0.0
            for other in range(split):
                total += moved(refs[quarters * other + at][...], 0, Q_COLS, Q_COLS * (core ^ other))
            q_out[:, pl.ds(pl.multiple_of(cols * (place ^ at), LANES), cols)] = total
        for pair in range(quarters // 2):
            keys = values = 0.0
            for low in range(2):
                for other in range(split):
                    piece = refs[quarters * other + 2 * pair + low][...]
                    to = HEAD_DIM * (2 * ((place & 1) ^ low) + (core ^ other))
                    keys += moved(piece, Q_COLS, HEAD_DIM, to)
                    values += moved(piece, Q_COLS + HEAD_DIM, HEAD_DIM, to)
            start = pl.multiple_of(cols * ((place >> 1) ^ pair), LANES)
            k_out[:, pl.ds(start, cols)] = keys
            v_out[:, pl.ds(start, cols)] = values

    shapes = [(depth, quarters * split * w) for w in (Q_COLS, HEAD_DIM, HEAD_DIM)]
    return call(
        kernel, (1,), [fixed((depth, cols))] * count, [whole(s) for s in shapes], [(s, f32) for s in shapes], pieces, "head_columns", [where]
    )


def chip_layer(
    tokens, span_order, token_positions, attn_gain, w_query, w_key, w_value, w_out, mlp_gain, w_gate, w_up, w_down, cotangent
):
    seq_dev, local_len, width = tokens.shape
    n_ctx, n_shard = lax.axis_size("ctx"), lax.axis_size("shard")
    split = n_ctx // seq_dev
    full_len = local_len * n_ctx
    half_rows = full_len // split
    spans_dev = local_len // SPAN
    quarters = 4
    units = w_gate.shape[1] // (split * quarters)
    unit_cols = units // n_shard
    gain_width = attn_gain.shape[0]
    ctx, batch, shard = lax.axis_index("ctx"), lax.axis_index("batch"), lax.axis_index("shard")
    seq, core = ctx // split, ctx % split
    place = 2 * seq + batch

    perm_x = [(c, c ^ split) for c in range(n_ctx)]
    perm_core = [(c, c ^ 1) for c in range(n_ctx)]
    perm_both = [(c, c ^ (split | 1)) for c in range(n_ctx)]
    perm_diagonal = [(2 * c + b, 2 * (c ^ split) + (b ^ 1)) for c in range(n_ctx) for b in range(2)]
    over_x = lambda a: lax.ppermute(a, "ctx", perm_x)
    over_core = lambda a: lax.ppermute(a, "ctx", perm_core)
    over_both = lambda a: lax.ppermute(a, "ctx", perm_both)
    over_y = lambda a: lax.ppermute(a, "batch", [(0, 1), (1, 0)])
    over_diagonal = lambda a: lax.ppermute(a, ("ctx", "batch"), perm_diagonal)

    def over_z(piece):
        gathered = lax.all_gather(piece, "shard", axis=0, tiled=True)
        return gathered.reshape(n_shard, piece.shape[0], piece.shape[1])

    def pick(array, index, axis):
        return lax.dynamic_index_in_dim(array, index, axis, keepdims=False)

    def scatter(block):
        return lax.psum_scatter(block, "shard", scatter_dimension=0, tiled=True)

    def add(*terms):
        return functools.reduce(lambda a, b: a + b, [t.astype(f32) for t in terms]).astype(bf16)

    def fence(*arrays):
        return lax.optimization_barrier(arrays)

    column = split * place + core
    unit_at = quarters * core + place

    def columns_of(array, width_of):
        return lax.dynamic_slice_in_dim(array, column * width_of, width_of, 1)

    def units_of(array, at):
        blocks = [lax.dynamic_slice_in_dim(array, (split * quarters * z + at) * unit_cols, unit_cols, 1) for z in range(n_shard)]
        return jnp.concatenate(blocks, axis=1)

    def stacked(rows, cols):
        return jnp.concatenate([rows[:, cols * j : cols * (j + 1)] for j in range(rows.shape[1] // cols)], axis=0)

    head_piece = jnp.concatenate(
        [columns_of(w_query, Q_COLS), columns_of(w_key, HEAD_DIM), columns_of(w_value, HEAD_DIM)], axis=1
    )
    gains = jnp.pad(jnp.stack([attn_gain, mlp_gain]), ((0, PAD_ROWS - 2), (0, 0)))
    head_piece = jnp.concatenate([head_piece, gains], axis=0)

    def second_piece(at):
        return jnp.concatenate([units_of(w_up, at), stacked(lax.dynamic_slice_in_dim(w_down, at * unit_cols, unit_cols, 0), units)], axis=0)

    own_tokens, sent_tokens = pick(tokens, seq, 0), pick(tokens, 1 - seq, 0)
    positions = pick(token_positions, seq, 0)
    sent_positions = pick(token_positions, 1 - seq, 0)
    head_piece, own_tokens, sent_tokens, positions, sent_positions, w_out, w_gate, w_up, w_down = fence(
        head_piece, own_tokens, sent_tokens, positions, sent_positions, w_out, w_gate, w_up, w_down
    )
    head_own = over_z(head_piece)
    positions = jnp.stack([positions, over_x(sent_positions)])
    x_near = jnp.concatenate([own_tokens, over_x(sent_tokens)], axis=0)
    out_piece = stacked(lax.dynamic_slice_in_dim(w_out, unit_at * HALF, HALF, 0), GROUP_COLS)
    gate_piece, second_own, second_last = units_of(w_gate, unit_at), second_piece(unit_at), second_piece(unit_at ^ 3)
    head_own, out_piece, x_near, positions, gate_piece, second_own, second_last, cotangent = fence(
        head_own, out_piece, x_near, positions, gate_piece, second_own, second_last, cotangent
    )

    out_own, gate_own = over_z(out_piece), over_z(gate_piece)
    head_x, head_y, x_far = over_x(head_own), over_y(head_own), over_core(x_near)
    positions = jnp.concatenate([positions, over_core(positions)], axis=0).reshape(-1, SPAN)
    cot_own, cot_sent = pick(cotangent, seq, 0), pick(cotangent, 1 - seq, 0)
    order = pick(span_order, seq, 0)
    n_spans = order.shape[0]
    span_ids = jnp.arange(n_spans, dtype=jnp.int32)
    slot_of = jnp.sum(jnp.where(order[None, :] == span_ids[:, None], span_ids[None, :], 0), axis=1)
    owner = slot_of // spans_dev
    from_far = (owner % split) ^ core
    side_place = ((owner // split) ^ seq) * spans_dev + slot_of % spans_dev
    places = [
        jnp.where(from_far == 0, side_place, 0).astype(jnp.int32),
        jnp.where(from_far == 0, 0, side_place).astype(jnp.int32),
        from_far.astype(jnp.int32),
    ]
    head_x, head_y, x_far, positions, cot_own, cot_sent = fence(head_x, head_y, x_far, positions, cot_own, cot_sent)

    middle = n_shard // 2
    head_last = [over_x(head_y[:middle]), over_y(head_x[middle:])]
    choice = (from_far * seq_dev * spans_dev + side_place)[:, None] == span_ids[None, :]
    positions = jnp.sum(jnp.where(choice[:, :, None], positions[None], 0), axis=1).reshape(full_len)
    frequency = rope_base ** (-2.0 * jnp.arange(HALF, dtype=f32) / HEAD_DIM)
    angles = positions.astype(f32)[:, None] * frequency
    blank = jnp.zeros((full_len, SLOT - HALF), f32)
    cos_half, sin_half = jnp.cos(angles), jnp.sin(angles)
    cosine = jnp.concatenate([cos_half, blank, cos_half, blank], axis=1)
    sine = jnp.concatenate([-sin_half, blank, sin_half, blank], axis=1)
    gain_one = head_own[:, gain_width, :].reshape(1, width).astype(f32)
    gain_two = head_own[:, gain_width + 1, :].reshape(1, width).astype(f32)
    *head_last, cosine, sine, cot_sent, gate_own, second_own, out_own = fence(
        *head_last, cosine, sine, cot_sent, gate_own, second_own, out_own
    )

    out_blocks = [out_own, over_y(out_own), over_x(out_own), over_diagonal(out_own)]
    head_blocks = [head_own, head_y, head_x, *head_last]
    x, normed, normed_t, queries, keys, values, w_qkv = front(places, x_near, x_far, cosine, sine, gain_one, head_blocks)
    x, normed_t, queries, keys, values, w_qkv = fence(x, normed_t, queries, keys, values, w_qkv)

    second_own = over_z(second_own)
    cot_received, gate_y = over_x(cot_sent), over_y(gate_own)
    mixed, q_aug = attend(queries, keys, values)
    cot_near = jnp.concatenate([cot_own, cot_received], axis=0)
    up_own = second_own[:, :gain_width]
    mixed, q_aug, cot_near, gate_y, up_own, second_own, second_last, gate_sent, *out_blocks = fence(
        mixed, q_aug, cot_near, gate_y, up_own, second_own, second_last, gate_own, *out_blocks
    )

    second_last = over_z(second_last)
    gate_x, cot_far = over_x(gate_sent), over_core(cot_near)
    up_y = over_y(up_own)
    place_at = place.astype(jnp.int32)[None]
    w_out_rows = out_rows(place_at, out_blocks)
    mine = core.astype(jnp.int32)[None]
    other = 1 - mine
    row_tile = 256
    tiles_half = half_rows // row_tile
    full_out = (w_out_rows, w_out_rows.shape, (0, 0))

    def out_dot(left, right, store):
        store(slice(None), matmul(left[0][...], right[0][...]))

    def back_dot(left, right, store):
        total = 0.0
        for k, both in enumerate(left):
            for which in range(2):
                total += dot_nt(both[:, units * which : units * (which + 1)], flat(right[2 * k + which][...]))
        store(slice(None), total)

    def down_dot(left, right, store):
        for j in range(width // units):
            total = sum(matmul(a[...], down_columns(b, j, range(n_shard))) for a, b in zip(left, right))
            store(slice(units * j, units * (j + 1)), total)

    def in_dot(left, right, store):
        total = 0.0
        for which, weights in enumerate(right):
            total += dot_nt(jnp.concatenate([a[...] for a in left[which::3]], axis=1), weights[...])
        store(slice(None), total)

    def kept(dots, left, right):
        found = []
        dots(left, right, lambda at, total: found.append(total))
        return found[0]

    thirds = [slice(units * j, units * (j + 1)) for j in range(width // units)]

    def sent_parts(lhs, rhs, dots, name):
        def body(left, right, _, outs):
            def store(at, total):
                start = at.start or 0
                for out, place_of in zip(outs, thirds):
                    if start <= place_of.start < start + total.shape[1]:
                        out[...] = total[:, place_of.start - start : place_of.stop - start].astype(bf16)

            dots(left, right, store)

        tile = half_rows // 2
        return sum_rows_call(body, other * 2, lhs, rhs, [], [((half_rows, units), bf16)] * len(thirds), tile, name)

    def joined(refs):
        return jnp.concatenate([r[...] for r in refs], axis=1).astype(f32)

    received = [over_core(a) for a in sent_parts([mixed], [full_out], out_dot, "out_other")]

    def hidden_body(left, right, others, outs):
        x_ref, *received_refs, gain_ref = others
        hidden = x_ref[...].astype(f32) + kept(out_dot, left, right) + joined(received_refs)
        outs[0][...] = hidden
        normed_rows = (hidden * rms_scale(hidden) * gain_ref[...]).astype(bf16)
        for out, at in zip(outs[1:], thirds):
            out[...] = normed_rows[:, at]

    hidden, *normed_two_own = sum_rows_call(
        hidden_body,
        mine * tiles_half,
        [mixed],
        [full_out],
        [(x, "shifted"), *[(r, "plain") for r in received], (gain_two, "whole")],
        [((half_rows, width), f32)] + [((half_rows, units), bf16)] * len(thirds),
        row_tile,
        "out_own",
    )
    normed_two_far = [over_core(a) for a in normed_two_own]
    cot = span_join(places, cot_near, cot_far)
    down_own = second_own[:, gain_width:]
    normed_two_own, normed_two_far, cot, gate_x, up_y, up_own, down_own = fence(
        normed_two_own, normed_two_far, cot, gate_x, up_y, up_own, down_own
    )
    up_x, down_y = over_x(up_own), over_y(down_own)
    normed_two, normed_two_t = join_halves(mine, normed_two_own, normed_two_far)
    normed_two, normed_two_t, cot, down_own = fence(normed_two, normed_two_t, cot, down_own)

    def feed(normed_two, cot, weights, with_grads=True):
        product, d_both = hidden_units(normed_two, cot, weights)
        if not with_grads:
            return weights, product, d_both
        return weights, product, d_both, feed_grads(normed_two_t, cot, product, d_both)

    def apart(*arrays):
        return [whole_of(a) for a in arrays]

    fed = [feed(normed_two, cot, apart(gate_own, up_own, down_own))]
    own_grads, normed_two, up_x, down_y, gate_x, down_own = fence(fed[0][3], normed_two, up_x, down_y, gate_x, down_own)
    gate_last, down_x = over_y(gate_x), over_x(down_own)
    fed.append(feed(normed_two, cot, apart(gate_y, up_y, down_y)))
    (gate_gy, up_gy, down_gy), normed_two, gate_last, down_x, second_last = fence(fed[1][3], normed_two, gate_last, down_x, second_last)
    down_gy = over_y(down_gy)
    fed.append(feed(normed_two, cot, [whole_of(gate_last), third_of(second_last, 0), third_of(second_last, 1)]))
    (gate_gl, up_gl, down_gl), normed_two, gate_gy, up_gy, down_gy = fence(fed[2][3], normed_two, gate_gy, up_gy, down_gy)
    gate_gy, gate_gl = over_y(gate_gy), scatter(gate_gl)
    fed.append(feed(normed_two, cot, apart(gate_x, up_x, down_x)))
    products, d_boths = [f[1] for f in fed], [f[2] for f in fed]
    (gate_gx, up_gx, down_gx), d_boths, products, gate_gy, up_gy, gate_gl, up_gl, down_gl = fence(
        fed[3][3], d_boths, products, gate_gy, up_gy, gate_gl, up_gl, down_gl
    )

    back_rhs = [f[0][k] for f in fed for k in range(2)]
    downs = [f[0][2] for f in fed]
    up_gy, gate_gx, up_gl = over_y(up_gy), over_x(gate_gx), scatter(up_gl)

    received_two = [over_core(a) for a in sent_parts(d_boths, back_rhs, back_dot, "back_other")]
    out_sent = sent_parts(products, downs, down_dot, "down_other")
    received_two, out_sent, up_gy, gate_gx, up_gl, up_gx, down_gx, down_gl = fence(
        received_two, out_sent, up_gy, gate_gx, up_gl, up_gx, down_gx, down_gl
    )

    def back_body(left, right, others, outs):
        *received_refs, hidden_ref, cot_ref, gain_ref = others
        grad_normed = kept(back_dot, left, right) + joined(received_refs)
        values_ = hidden_ref[...]
        scale_rows = rms_scale(values_)
        grad_hidden = cot_ref[...].astype(f32) + norm_back(grad_normed, values_, scale_rows, gain_ref[...])
        outs[0][...] = grad_hidden
        for out, at in zip(outs[2:], thirds):
            out[...] = grad_hidden[:, at].astype(bf16)

        @pl.when(pl.program_id(0) == 0)
        def _():
            outs[1][...] = jnp.zeros(outs[1].shape, f32)

        outs[1][...] += column_sums(grad_normed * values_ * scale_rows)

    up_gx, down_gl = over_x(up_gx), over_y(down_gl)
    received_out = [over_core(a) for a in out_sent]
    grad_hidden, gain_two_sums, *grad_attended_own = sum_rows_call(
        back_body,
        mine * tiles_half,
        d_boths,
        back_rhs,
        [*[(r, "plain") for r in received_two], (hidden, "plain"), (cot, "shifted"), (gain_two, "whole")],
        [((half_rows, width), f32), ((8, width), f32)] + [((half_rows, units), bf16)] * len(thirds),
        row_tile,
        "back_own",
    )
    gate_sum = scatter(add(own_grads[0], gate_gy, gate_gx))
    grad_attended_far = [over_core(a) for a in grad_attended_own]

    def down_body(left, right, others, outs):
        hidden_ref, *received_refs = others

        def store(at, total):
            received_rows = received_refs[at.start // units][...].astype(f32)
            outs[0][:, at] = (hidden_ref[:, at] + total + received_rows).astype(bf16)

        down_dot(left, right, store)

    (layer_rows,) = sum_rows_call(
        down_body,
        mine * tiles_half,
        products,
        downs,
        [(hidden, "plain"), *[(r, "plain") for r in received_out]],
        [((half_rows, width), bf16)],
        row_tile,
        "down_own",
    )
    grad_attended_own, grad_attended_far, layer_rows, up_gx, down_gl, gate_sum, gate_gl, up_gl = fence(
        grad_attended_own, grad_attended_far, layer_rows, up_gx, down_gl, gate_sum, gate_gl, up_gl
    )
    down_gx = add(down_gx, down_gl)

    pair_order = order.reshape(n_ctx, spans_dev // 2, 2)
    in_half = jnp.where(pair_order[..., 0] // (n_spans // 2) == core, pair_order[..., 0], pair_order[..., 1]) - core * (n_spans // 2)
    steps = jnp.arange(n_ctx, dtype=jnp.int32) ^ ctx
    send_places = in_half[steps].reshape(-1).astype(jnp.int32)
    my_order = lax.dynamic_slice_in_dim(span_order, ctx * spans_dev, spans_dev, 1)
    from_mine = (my_order // (n_spans // 2) == core).reshape(seq_dev, spans_dev // 2, 2, 1, 1)

    def to_slots(arranged):
        return [arranged[0], over_core(arranged[1]), over_x(arranged[2]), over_both(arranged[3])]

    def arrange(rows):
        arranged = span_copy(send_places, rows).reshape(n_ctx, -1, width)
        return [arranged[k] for k in range(n_ctx)]

    def from_slots(parts):
        parts = [p.reshape(spans_dev // 2, 1, SPAN, width) for p in parts]
        near = jnp.where(from_mine[seq], parts[0], parts[1])
        far = jnp.where(from_mine[1 - seq], parts[2], parts[3])
        near, far = near.reshape(local_len, width), far.reshape(local_len, width)
        return jnp.where(seq == 0, jnp.stack([near, far]), jnp.stack([far, near]))

    def both_cores(side):
        return side + [over_core(a) for a in side]

    up_sum = scatter(add(own_grads[1], up_gy, up_gx))
    down_gx = over_x(down_gx)
    both_gl = over_y(jnp.concatenate([gate_gl, up_gl], axis=0))
    grad_attended, grad_mixed = mixed_back(mine, grad_attended_own, grad_attended_far, w_out_rows)
    out_grads = [b.reshape(-1, width) for b in out_grad_blocks(place_at, mixed, grad_attended)]
    layer_parts = arrange(layer_rows)
    grad_mixed, out_grads, down_gx, layer_parts, up_sum, both_gl = fence(grad_mixed, out_grads, down_gx, layer_parts, up_sum, both_gl)

    def back_of(group, q_aug):
        return attend_back(group, 1, q_aug, keys, values, grad_mixed, mixed, cosine, sine)

    down_sum = scatter(add(own_grads[2], down_gy, down_gx))
    layer_parts = [layer_parts[0], over_core(layer_parts[1]), over_x(layer_parts[2]), layer_parts[3]]
    both_gl, out_y, out_last = over_x(both_gl), over_y(out_grads[1]), over_y(out_grads[3])
    back_last = back_of(3, q_aug)
    back_last, q_aug, both_gl, out_last = fence(back_last, q_aug, both_gl, out_last)
    both_sum = add(jnp.concatenate([gate_sum, up_sum], axis=0), both_gl)
    qkv_last = qkv_grad(normed_t, *back_last)
    out_x = add(out_grads[2], out_last)
    qkv_last, q_aug, out_x, both_sum, layer_parts, out_y = fence(qkv_last, q_aug, out_x, both_sum, layer_parts, out_y)

    qkv_last, out_x, both_x = over_y(qkv_last), over_x(out_x), over_x(both_sum)
    back_x = back_of(2, q_aug)
    back_x, q_aug, qkv_last, out_x, down_sum = fence(back_x, q_aug, qkv_last, out_x, down_sum)
    qkv_x = add(qkv_grad(normed_t, *back_x), qkv_last)
    out_sum = add(out_grads[0], out_y, out_x)
    qkv_x, out_sum, q_aug, both_sum, both_x = fence(qkv_x, out_sum, q_aug, both_sum, both_x)

    out_sum = scatter(out_sum)
    qkv_x, both_last, both_y = over_x(qkv_x), over_y(both_x), over_y(both_sum)
    both_far = [over_core(a) for a in (both_sum, both_x)]
    back_y = back_of(1, q_aug)
    back_y, q_aug, both_far, out_sum = fence(back_y, q_aug, both_far, out_sum)
    qkv_y = qkv_grad(normed_t, *back_y)
    row_sum = jnp.concatenate([down_sum, out_sum], axis=0)
    qkv_y, q_aug, row_sum, qkv_x, both_y, both_last, layer_parts = fence(qkv_y, q_aug, row_sum, qkv_x, both_y, both_last, layer_parts)

    layer_parts[3] = over_both(layer_parts[3])
    qkv_y, row_x, row_y = over_y(qkv_y), over_x(row_sum), over_y(row_sum)
    both_far = [both_far[0], over_core(both_y), both_far[1], over_core(both_last)]
    back_own = back_of(0, q_aug)
    back_own, both_far = fence(back_own, both_far)

    depth = w_qkv.shape[0]
    q_width, k_width = queries.shape[1], keys.shape[1]
    in_rhs = [(w_qkv, (depth, q_width), (0, 0))]
    in_rhs += [(w_qkv, (depth, k_width), (0, q_width // k_width + which)) for which in range(2)]
    qkv_sum = add(qkv_grad(normed_t, *back_own), qkv_y, qkv_x)
    qkv_sum, back_own, row_x, row_y, layer_parts = fence(qkv_sum, back_own, row_x, row_y, layer_parts)
    in_lhs = [*back_own, *back_y, *back_x, *back_last]
    qkv_sum = scatter(qkv_sum)
    row_last = over_y(row_x)
    received_in = [over_core(a) for a in sent_parts(in_lhs, in_rhs, in_dot, "in_other")]
    row_far = [over_core(a) for a in (row_sum, row_y, row_x)]

    def in_body(left, right, others, outs):
        *received_refs, x_ref, grad_ref, gain_ref = others
        grad_normed = kept(in_dot, left, right) + joined(received_refs)
        values_ = x_ref[...].astype(f32)
        scale_rows = rms_scale(values_)
        outs[0][...] = (grad_ref[...] + norm_back(grad_normed, values_, scale_rows, gain_ref[...])).astype(bf16)

        @pl.when(pl.program_id(0) == 0)
        def _():
            outs[1][...] = jnp.zeros(outs[1].shape, f32)

        outs[1][...] += column_sums(grad_normed * values_ * scale_rows)

    grad_rows, gain_one_sums = sum_rows_call(
        in_body,
        mine * tiles_half,
        in_lhs,
        in_rhs,
        [*[(r, "plain") for r in received_in], (x, "shifted"), (grad_hidden, "plain"), (gain_one, "whole")],
        [((half_rows, width), bf16), ((8, width), f32)],
        row_tile,
        "in_own",
    )
    sums = jnp.stack([gain_one_sums.sum(0), gain_two_sums.sum(0)])
    sums = sums + over_x(sums)
    sums = sums + over_core(sums)
    token_parts, sums, qkv_sum, row_far, row_last = fence(arrange(grad_rows), sums, qkv_sum, row_far, row_last)

    qkv_x, qkv_y = over_x(qkv_sum), over_y(qkv_sum)
    row_far.append(over_core(row_last))
    sums = sums + over_y(sums)
    layer_out = from_slots(layer_parts)
    token_parts, sums, qkv_x, qkv_y, layer_out, row_far = fence(token_parts, sums, qkv_x, qkv_y, layer_out, row_far)

    token_parts = to_slots(token_parts)
    qkv_last = over_y(qkv_x)
    where = jnp.stack([place, core]).astype(jnp.int32)
    both_pieces = [both_sum, both_y, both_x, both_last] + both_far
    grad_w_gate = unit_columns(where, both_pieces, n_shard, 0)
    grad_w_up = unit_columns(where, both_pieces, n_shard, 1)
    grad_w_down, grad_w_out = unit_rows(where, [row_sum, row_y, row_x, row_last] + row_far, unit_cols)
    total = lax.dynamic_slice_in_dim(sums, shard * gain_width, gain_width, 1)
    for step in range(1, n_shard):
        to = lax.dynamic_slice_in_dim(sums, (shard + step) % n_shard * gain_width, gain_width, 1)
        total = total + lax.ppermute(to, "shard", [(z, (z + step) % n_shard) for z in range(n_shard)])
    head_grads = head_columns(where, both_cores([qkv_sum, qkv_y, qkv_x, qkv_last]))
    token_parts, grad_w_gate, grad_w_up, grad_w_down, grad_w_out, head_grads, total = fence(
        token_parts, grad_w_gate, grad_w_up, grad_w_down, grad_w_out, head_grads, total
    )
    grad_w_query, grad_w_key, grad_w_value = head_grads
    grad_tokens = from_slots(token_parts)

    return (
        layer_out,
        grad_tokens,
        total[0],
        grad_w_query,
        grad_w_key,
        grad_w_value,
        grad_w_out,
        total[1],
        grad_w_gate,
        grad_w_up,
        grad_w_down,
    )


def rope_tables(positions):
    half_dim = HEAD_DIM // 2
    frequency = rope_base ** (-2.0 * jnp.arange(half_dim, dtype=jnp.float32) / HEAD_DIM)
    angles = positions.astype(jnp.float32)[..., None] * frequency
    return (jnp.cos(angles), jnp.sin(angles))


def rotate(values, cosine, sine_table):
    half_dim = values.shape[-1] // 2
    first_half = values[..., :half_dim]
    second_half = values[..., half_dim:]
    cosine = cosine[..., None, :]
    sine_table = sine_table[..., None, :]
    return jnp.concatenate(
        [
            first_half * cosine - second_half * sine_table,
            second_half * cosine + first_half * sine_table,
        ],
        axis=-1,
    )


def general_layer(
    tokens,
    span_order,
    token_positions,
    attn_gain,
    w_query,
    w_key,
    w_value,
    w_out,
    mlp_gain,
    w_gate,
    w_up,
    w_down,
    cotangent,
):
    seq_dev, local_len, model_width = tokens.shape
    row_count = seq_dev * local_len
    groups = HEADS // KV_HEADS
    kv_width = KV_HEADS * HEAD_DIM
    score_scale = HEAD_DIM ** (-0.5)
    full_len = local_len * lax.axis_size("ctx")
    ctx_index = lax.axis_index("ctx")
    slot_index = jnp.arange(full_len, dtype=jnp.int32)
    key_index = span_order[:, slot_index // SPAN] * SPAN + slot_index[None, :] % SPAN
    query_index = lax.dynamic_slice_in_dim(key_index, ctx_index * local_len, local_len, 1)
    allowed = query_index[:, :, None] >= key_index[:, None, :]
    cosine, sine_table = rope_tables(token_positions)
    gain_one, wq_full, wk_full, wv_full, wo_full = (
        lax.all_gather(attn_gain, "shard", axis=0, tiled=True),
        lax.all_gather(w_query, "shard", axis=0, tiled=True),
        lax.all_gather(w_key, "shard", axis=0, tiled=True),
        lax.all_gather(w_value, "shard", axis=0, tiled=True),
        lax.all_gather(w_out, "shard", axis=0, tiled=True),
    )
    x_rows = tokens.reshape(row_count, model_width).astype(jnp.float32)
    scale_one = rms_scale(x_rows)
    normed = (x_rows * scale_one * gain_one).astype(jnp.bfloat16)
    queries = rotate(
        matmul(normed, wq_full).reshape(seq_dev, local_len, HEADS, HEAD_DIM), cosine, sine_table
    ).astype(jnp.bfloat16)
    keys_local = rotate(
        matmul(normed, wk_full).reshape(seq_dev, local_len, KV_HEADS, HEAD_DIM), cosine, sine_table
    ).astype(jnp.bfloat16)
    values_local = matmul(normed, wv_full).astype(jnp.bfloat16)
    keys_all, values_all = (
        lax.all_gather(keys_local.reshape(seq_dev, local_len, kv_width), "ctx", axis=1, tiled=True),
        lax.all_gather(
            values_local.reshape(seq_dev, local_len, kv_width), "ctx", axis=1, tiled=True
        ),
    )
    query_heads = queries.reshape(seq_dev, local_len, KV_HEADS, groups, HEAD_DIM).transpose(
        2, 0, 1, 3, 4
    )
    key_heads = keys_all.reshape(seq_dev, full_len, KV_HEADS, HEAD_DIM).transpose(2, 0, 1, 3)
    value_heads = values_all.reshape(seq_dev, full_len, KV_HEADS, HEAD_DIM).transpose(2, 0, 1, 3)

    def scores_of(query_head, key_head):
        raw_scores = (
            jnp.einsum("sqjd,skd->sjqk", query_head, key_head, preferred_element_type=jnp.float32)
            * score_scale
        )
        return jnp.where(allowed[:, None], raw_scores, masked_value)

    def attend_head(pieces):
        query_head, key_head, value_head = pieces
        scores = scores_of(query_head, key_head)
        row_max = jnp.max(scores, axis=-1, keepdims=True)
        exponent = jnp.exp(scores - row_max)
        row_total = jnp.sum(exponent, axis=-1, keepdims=True)
        probabilities = (exponent / row_total).astype(jnp.bfloat16)
        mixed_head = jnp.einsum(
            "sjqk,skd->sqjd", probabilities, value_head, preferred_element_type=jnp.float32
        )
        return (mixed_head, row_max[..., 0] + jnp.log(row_total[..., 0]))

    mixed_heads, log_totals = lax.map(attend_head, (query_heads, key_heads, value_heads))
    mixed_low = (
        mixed_heads.transpose(1, 2, 0, 3, 4).reshape(row_count, model_width).astype(jnp.bfloat16)
    )
    hidden = x_rows + matmul(mixed_low, wo_full)
    scale_two = rms_scale(hidden)
    gain_two, wg_full, wu_full, wd_full = (
        lax.all_gather(mlp_gain, "shard", axis=0, tiled=True),
        lax.all_gather(w_gate, "shard", axis=0, tiled=True),
        lax.all_gather(w_up, "shard", axis=0, tiled=True),
        lax.all_gather(w_down, "shard", axis=0, tiled=True),
    )
    normed_two = (hidden * scale_two * gain_two).astype(jnp.bfloat16)
    gate_pre = matmul(normed_two, wg_full)
    up_pre = matmul(normed_two, wu_full)
    sigmoid_gate = jax.nn.sigmoid(gate_pre)
    activated = gate_pre * sigmoid_gate
    product = (activated * up_pre).astype(jnp.bfloat16)
    layer_out = (hidden + matmul(product, wd_full)).astype(jnp.bfloat16).reshape(tokens.shape)
    grad_out = cotangent.reshape(row_count, model_width)
    gain_two_back, wg_back, wu_back, wd_back = (
        lax.all_gather(mlp_gain, "shard", axis=0, tiled=True),
        lax.all_gather(w_gate, "shard", axis=0, tiled=True),
        lax.all_gather(w_up, "shard", axis=0, tiled=True),
        lax.all_gather(w_down, "shard", axis=0, tiled=True),
    )
    grad_product = matmul(grad_out, wd_back.T)
    grad_w_down = matmul(product.T, grad_out)
    grad_gate = (
        grad_product * up_pre * sigmoid_gate * (1.0 + gate_pre * (1.0 - sigmoid_gate))
    ).astype(jnp.bfloat16)
    grad_up = (grad_product * activated).astype(jnp.bfloat16)
    grad_w_gate = matmul(normed_two.T, grad_gate)
    grad_w_up = matmul(normed_two.T, grad_up)
    grad_normed_two = matmul(grad_gate, wg_back.T) + matmul(grad_up, wu_back.T)
    gain_two_f = gain_two_back.astype(jnp.float32)
    grad_mlp_gain = jnp.sum(grad_normed_two * hidden * scale_two, axis=0)
    grad_hidden = grad_out.astype(jnp.float32) + norm_back(
        grad_normed_two, hidden, scale_two, gain_two_f
    )
    gain_one_back, wq_back, wk_back, wv_back, wo_back = (
        lax.all_gather(attn_gain, "shard", axis=0, tiled=True),
        lax.all_gather(w_query, "shard", axis=0, tiled=True),
        lax.all_gather(w_key, "shard", axis=0, tiled=True),
        lax.all_gather(w_value, "shard", axis=0, tiled=True),
        lax.all_gather(w_out, "shard", axis=0, tiled=True),
    )
    grad_attended = grad_hidden.astype(jnp.bfloat16)
    grad_w_out = matmul(mixed_low.T, grad_attended)
    grad_mixed = matmul(grad_attended, wo_back.T).astype(jnp.bfloat16)
    grad_heads = grad_mixed.reshape(seq_dev, local_len, KV_HEADS, groups, HEAD_DIM).transpose(
        2, 0, 1, 3, 4
    )

    def attend_back(pieces):
        query_head, key_head, value_head, grad_head, log_total = pieces
        scores = scores_of(query_head, key_head)
        probabilities = jnp.exp(scores - log_total[..., None])
        grad_probs = jnp.einsum(
            "sqjd,skd->sjqk", grad_head, value_head, preferred_element_type=jnp.float32
        )
        inner_sum = jnp.sum(probabilities * grad_probs, axis=-1, keepdims=True)
        grad_scores = (probabilities * (grad_probs - inner_sum)).astype(jnp.bfloat16)
        grad_query = (
            jnp.einsum("sjqk,skd->sqjd", grad_scores, key_head, preferred_element_type=jnp.float32)
            * score_scale
        )
        grad_key = (
            jnp.einsum(
                "sjqk,sqjd->skd", grad_scores, query_head, preferred_element_type=jnp.float32
            )
            * score_scale
        )
        grad_value = jnp.einsum(
            "sjqk,sqjd->skd",
            probabilities.astype(jnp.bfloat16),
            grad_head,
            preferred_element_type=jnp.float32,
        )
        return (grad_query, grad_key, grad_value)

    grad_queries, key_terms, value_terms = lax.map(
        attend_back, (query_heads, key_heads, value_heads, grad_heads, log_totals)
    )
    key_terms = key_terms.transpose(1, 2, 0, 3).reshape(seq_dev, full_len, kv_width)
    value_terms = value_terms.transpose(1, 2, 0, 3).reshape(seq_dev, full_len, kv_width)
    grad_keys, grad_values = (
        lax.psum_scatter(
            key_terms.astype(jnp.bfloat16), "ctx", scatter_dimension=1, tiled=True
        ).astype(jnp.float32),
        lax.psum_scatter(
            value_terms.astype(jnp.bfloat16), "ctx", scatter_dimension=1, tiled=True
        ).astype(jnp.float32),
    )
    grad_queries = grad_queries.transpose(1, 2, 0, 3, 4).reshape(
        seq_dev, local_len, HEADS, HEAD_DIM
    )
    grad_q_low = (
        rotate(grad_queries, cosine, -sine_table)
        .reshape(row_count, model_width)
        .astype(jnp.bfloat16)
    )
    grad_k_low = (
        rotate(grad_keys.reshape(seq_dev, local_len, KV_HEADS, HEAD_DIM), cosine, -sine_table)
        .reshape(row_count, kv_width)
        .astype(jnp.bfloat16)
    )
    grad_v_low = grad_values.reshape(row_count, kv_width).astype(jnp.bfloat16)
    grad_w_query = matmul(normed.T, grad_q_low)
    grad_w_key = matmul(normed.T, grad_k_low)
    grad_w_value = matmul(normed.T, grad_v_low)
    grad_normed = (
        matmul(grad_q_low, wq_back.T)
        + matmul(grad_k_low, wk_back.T)
        + matmul(grad_v_low, wv_back.T)
    )
    gain_one_f = gain_one_back.astype(jnp.float32)
    grad_attn_gain = jnp.sum(grad_normed * x_rows * scale_one, axis=0)
    grad_tokens = (grad_hidden + norm_back(grad_normed, x_rows, scale_one, gain_one_f)).astype(
        jnp.bfloat16
    )
    grad_tokens = grad_tokens.reshape(tokens.shape)
    part_gain_two, part_gate, part_up, part_down = (
        lax.psum_scatter(
            grad_mlp_gain.astype(jnp.bfloat16), "shard", scatter_dimension=0, tiled=True
        ).astype(jnp.float32),
        lax.psum_scatter(
            grad_w_gate.astype(jnp.bfloat16), "shard", scatter_dimension=0, tiled=True
        ).astype(jnp.float32),
        lax.psum_scatter(
            grad_w_up.astype(jnp.bfloat16), "shard", scatter_dimension=0, tiled=True
        ).astype(jnp.float32),
        lax.psum_scatter(
            grad_w_down.astype(jnp.bfloat16), "shard", scatter_dimension=0, tiled=True
        ).astype(jnp.float32),
    )
    part_gain_one, part_query, part_key, part_value, part_out = (
        lax.psum_scatter(
            grad_attn_gain.astype(jnp.bfloat16), "shard", scatter_dimension=0, tiled=True
        ).astype(jnp.float32),
        lax.psum_scatter(
            grad_w_query.astype(jnp.bfloat16), "shard", scatter_dimension=0, tiled=True
        ).astype(jnp.float32),
        lax.psum_scatter(
            grad_w_key.astype(jnp.bfloat16), "shard", scatter_dimension=0, tiled=True
        ).astype(jnp.float32),
        lax.psum_scatter(
            grad_w_value.astype(jnp.bfloat16), "shard", scatter_dimension=0, tiled=True
        ).astype(jnp.float32),
        lax.psum_scatter(
            grad_w_out.astype(jnp.bfloat16), "shard", scatter_dimension=0, tiled=True
        ).astype(jnp.float32),
    )
    summed = (
        lax.psum(part_gain_one.astype(jnp.bfloat16), ("ctx", "batch")).astype(jnp.float32),
        lax.psum(part_query.astype(jnp.bfloat16), ("ctx", "batch")).astype(jnp.float32),
        lax.psum(part_key.astype(jnp.bfloat16), ("ctx", "batch")).astype(jnp.float32),
        lax.psum(part_value.astype(jnp.bfloat16), ("ctx", "batch")).astype(jnp.float32),
        lax.psum(part_out.astype(jnp.bfloat16), ("ctx", "batch")).astype(jnp.float32),
        lax.psum(part_gain_two.astype(jnp.bfloat16), ("ctx", "batch")).astype(jnp.float32),
        lax.psum(part_gate.astype(jnp.bfloat16), ("ctx", "batch")).astype(jnp.float32),
        lax.psum(part_up.astype(jnp.bfloat16), ("ctx", "batch")).astype(jnp.float32),
        lax.psum(part_down.astype(jnp.bfloat16), ("ctx", "batch")).astype(jnp.float32),
    )
    return (
        layer_out,
        grad_tokens,
        summed[0],
        summed[1],
        summed[2],
        summed[3],
        summed[4],
        summed[5],
        summed[6],
        summed[7],
        summed[8],
    )


def fits(mesh):
    split = mesh.shape["ctx"] // 2
    return split == 2 and mesh.shape["batch"] == 2 and mesh.shape["shard"] * split == KV_HEADS and mesh.shape["shard"] == 4


def solution(mesh):
    in_specs = (
        P(("shard", "batch"), "ctx", None),
        P(("shard", "batch"), None),
        P(("shard", "batch"), "ctx"),
        P("shard"),
        P("shard", None),
        P("shard", None),
        P("shard", None),
        P("shard", None),
        P("shard"),
        P("shard", None),
        P("shard", None),
        P("shard", None),
        P(("shard", "batch"), "ctx", None),
    )
    out_specs = (
        P(("shard", "batch"), "ctx", None),
        P(("shard", "batch"), "ctx", None),
        P("shard"),
        P("shard", None),
        P("shard", None),
        P("shard", None),
        P("shard", None),
        P("shard"),
        P("shard", None),
        P("shard", None),
        P("shard", None),
    )
    layer = chip_layer if fits(mesh) else general_layer
    return jax.shard_map(layer, mesh=mesh, in_specs=in_specs, out_specs=out_specs, check_vma=False)
```

```python
import functools

import jax
import jax.numpy as jnp
import numpy as np
from jax import lax
from jax.experimental import pallas as pl
from jax.experimental.pallas import tpu as pltpu
from jax.sharding import PartitionSpec as P

HEADS = 16
KV_HEADS = 8
HEAD_DIM = 96
SPAN = 128
GROUPS = HEADS // KV_HEADS
HALF = HEAD_DIM // 2
LANES = 128
SLOT = LANES // 2
GROUP_COLS = (GROUPS + 2) * HEAD_DIM
Q_COLS = GROUPS * HEAD_DIM
Q_LANES = GROUPS * LANES
PAD_ROWS = 16

norm_eps = 1e-05
rope_base = 100000.0
masked_value = -1e30
score_scale = HEAD_DIM ** (-0.5)
exp2_scale = score_scale * 1.4426950408889634

bf16 = jnp.bfloat16
f32 = jnp.float32
MIB = 1 << 20
NT = (((1,), (1,)), ((), ()))
TN = (((0,), (0,)), ((), ()))


def rms_scale(values):
    return lax.rsqrt(jnp.mean(values * values, axis=-1, keepdims=True) + norm_eps)


def matmul(left, right):
    return jnp.dot(left, right, preferred_element_type=f32)


def dot_nt(left, right):
    return lax.dot_general(left, right, NT, preferred_element_type=f32)


def dot_tn(left, right):
    return lax.dot_general(left, right, TN, preferred_element_type=f32)


def params(limit):
    return pltpu.CompilerParams(vmem_limit_bytes=limit * MIB)


def short():
    return pl.CostEstimate(flops=1000, bytes_accessed=1000, transcendentals=0)


def whole(shape):
    return pl.BlockSpec(shape, lambda *_: (0,) * len(shape))


def part(block, index):
    return pl.BlockSpec(block, lambda *_: index, pipeline_mode=pl.Buffered(1))


def fixed(shape):
    return part(shape, (0,) * len(shape))


def call(kernel, grid, in_specs, out_specs, out_shape, operands, name, prefetch=(), scratch=(), limit=60):
    return pl.pallas_call(
        kernel,
        grid_spec=pltpu.PrefetchScalarGridSpec(
            num_scalar_prefetch=len(prefetch), grid=grid, in_specs=in_specs, out_specs=out_specs, scratch_shapes=list(scratch)
        ),
        out_shape=[jax.ShapeDtypeStruct(shape, dtype) for shape, dtype in out_shape],
        compiler_params=params(limit),
        cost_estimate=short(),
        name=name,
    )(*prefetch, *operands)


def spread_matrix():
    spread = np.zeros((GROUP_COLS, (GROUPS + 2) * LANES), np.float32)
    for row in range(spread.shape[0]):
        head, feature = divmod(row, HEAD_DIM)
        half, place = divmod(feature, HALF)
        spread[row, head * LANES + half * SLOT + place] = 1.0
    return spread


def front_kernel(near_ref, far_ref, flag_ref, *refs):
    spans = 4
    near, far, refs = refs[:spans], refs[spans : 2 * spans], refs[2 * spans :]
    cos_ref, sin_ref, gain_ref, spread_ref, w0, w1, w2, w3a, w3b, x_out, n_out, nt_out, q_out, k_out, v_out, w_out = refs
    q_width, k_width = q_out.shape[1], k_out.shape[1]
    step_at = pl.program_id(0)

    @pl.when(step_at == 0)
    def _():
        depth = w0.shape[1]
        halves = w3a.shape[0]
        for at, piece in enumerate((w0, w1, w2, None)):
            for z in range(w0.shape[0]):
                block = piece[z] if piece is not None else (w3a[z] if z < halves else w3b[z - halves])
                spread = matmul(block, spread_ref[...]).astype(bf16)
                rows = slice(z * depth, (z + 1) * depth)
                w_out[rows, Q_LANES * at : Q_LANES * (at + 1)] = spread[:, :Q_LANES]
                w_out[rows, q_width + LANES * at : q_width + LANES * (at + 1)] = spread[:, Q_LANES : Q_LANES + LANES]
                at_v = q_width + k_width + LANES * at
                w_out[rows, at_v : at_v + LANES] = spread[:, Q_LANES + LANES :]

    for k in range(spans):
        rows = slice(k * SPAN, (k + 1) * SPAN)

        @pl.when(flag_ref[spans * step_at + k] == 0)
        def _():
            x_out[rows, :] = near[k][0]

        @pl.when(flag_ref[spans * step_at + k] != 0)
        def _():
            x_out[rows, :] = far[k][0]

    x = x_out[...].astype(f32)
    normed = (x * rms_scale(x) * gain_ref[...]).astype(bf16)
    n_out[...] = normed
    nt_out[...] = normed.T
    cosine, sine = cos_ref[...], sin_ref[...]
    lane = lax.broadcasted_iota(jnp.int32, (1, LANES), 1)
    ones = jnp.where((lane >= HALF) & (lane < HALF + 3), 1.0, 0.0)
    step = 4 * LANES
    for start in range(0, w_out.shape[1], step):
        raw = matmul(normed, w_out[:, start : start + step])
        for piece in range(0, step, LANES):
            at = start + piece
            head = raw[:, piece : piece + LANES]
            if at < q_width + k_width:
                head = head * cosine + pltpu.roll(head, SLOT, 1) * sine
            if at < q_width:
                q_out[:, at : at + LANES] = head.astype(bf16)
            elif at < q_width + k_width:
                k_out[:, at - q_width : at - q_width + LANES] = (head + ones).astype(bf16)
            else:
                v_out[:, at - q_width - k_width : at - q_width - k_width + LANES] = (head + ones).astype(bf16)


def span_specs(width, count):
    def near(k):
        return pl.BlockSpec((1, SPAN, width), lambda i, near, far, flag: (near[count * i + k], 0, 0))

    def far(k):
        return pl.BlockSpec((1, SPAN, width), lambda i, near, far, flag: (far[count * i + k], 0, 0))

    return [near(k) for k in range(count)] + [far(k) for k in range(count)]


def as_spans(array):
    return array.reshape(array.shape[0] // SPAN, SPAN, array.shape[1])


def front(places, near, far, cosine, sine, gain, pieces):
    rows, width = 2 * near.shape[0], near.shape[1]
    groups = len(pieces) - 1
    n_shard = pieces[0].shape[0]
    depth = width // n_shard
    spread = jnp.asarray(spread_matrix(), bf16)
    spans = 4
    tile = spans * SPAN
    q_width, k_width = groups * Q_LANES, groups * LANES
    total = q_width + 2 * k_width

    def rows_spec(cols):
        return pl.BlockSpec((tile, cols), lambda i, *_: (i, 0))

    near, far = as_spans(near), as_spans(far)
    return call(
        front_kernel,
        (rows // tile,),
        span_specs(width, spans)
        + [rows_spec(LANES), rows_spec(LANES), fixed(gain.shape), fixed(spread.shape)]
        + [part((p.shape[0], depth, p.shape[2]), (0, 0, 0)) for p in pieces],
        [rows_spec(width), rows_spec(width), pl.BlockSpec((width, tile), lambda i, *_: (0, i))]
        + [rows_spec(q_width), rows_spec(k_width), rows_spec(k_width), whole((n_shard * depth, total))],
        [
            ((rows, width), bf16),
            ((rows, width), bf16),
            ((width, rows), bf16),
            ((rows, q_width), bf16),
            ((rows, k_width), bf16),
            ((rows, k_width), bf16),
            ((n_shard * depth, total), bf16),
        ],
        [near] * spans + [far] * spans + [cosine, sine, gain, spread, *pieces],
        "front",
        places,
    )


def span_copy(places, source):
    width = source.shape[1]
    count = places.shape[0]
    step = 2

    def kernel(place_ref, *refs):
        for k in range(step):
            refs[step][k] = refs[k][0]

    spans = as_spans(source)
    (out,) = call(
        kernel,
        (count // step,),
        [pl.BlockSpec((1, SPAN, width), lambda i, place, k=k: (place[step * i + k], 0, 0)) for k in range(step)],
        [pl.BlockSpec((step, SPAN, width), lambda i, place: (i, 0, 0))],
        [((count, SPAN, width), source.dtype)],
        [spans] * step,
        "span_copy",
        [places],
    )
    return out.reshape(count * SPAN, width)


def span_join(places, near, far):
    width = near.shape[1]
    count = 2 * near.shape[0] // SPAN
    step = 4

    def kernel(near_ref, far_ref, flag_ref, *refs):
        out_ref = refs[-1]
        for k in range(step):
            is_far = flag_ref[step * pl.program_id(0) + k] != 0

            @pl.when(jnp.logical_not(is_far))
            def _():
                out_ref[k] = refs[k][0]

            @pl.when(is_far)
            def _():
                out_ref[k] = refs[step + k][0]

    (out,) = call(
        kernel,
        (count // step,),
        span_specs(width, step),
        [pl.BlockSpec((step, SPAN, width), lambda i, *_: (i, 0, 0))],
        [((count, SPAN, width), near.dtype)],
        [as_spans(near)] * step + [as_spans(far)] * step,
        "span_join",
        places,
    )
    return out.reshape(count * SPAN, width)


def three_parts(values):
    first = values.astype(bf16).astype(f32)
    second = (values - first).astype(bf16).astype(f32)
    third = values - first - second
    return first, second, third


def with_lanes(block, column):
    lane = lax.broadcasted_iota(jnp.int32, block.shape, 1)
    first, second, third = three_parts(column)
    wide = block.astype(f32)
    wide = jnp.where(lane == HALF, first, wide)
    wide = jnp.where(lane == HALF + 1, second, wide)
    wide = jnp.where(lane == HALF + 2, third, wide)
    return wide.astype(bf16)


Q_TILE = 256
K_CHUNK = 512


def heads_down(block):
    return jnp.concatenate([block[:, LANES * h : LANES * (h + 1)] for h in range(GROUPS)], axis=0)


def attend_kernel(q_ref, k_ref, v_ref, mixed_ref, q_aug_ref):
    rows = q_ref.shape[0]
    for tile in range(rows // Q_TILE):
        first_row = tile * Q_TILE
        query = heads_down(q_ref[first_row : first_row + Q_TILE, :])
        end = first_row + Q_TILE
        top = acc = None
        for start in range(0, end, K_CHUNK):
            size = min(K_CHUNK, end - start)
            key = k_ref[start : start + size, :]
            value = v_ref[start : start + size, :]
            scores = dot_nt(query, key)
            if start + size > first_row:
                row = lax.broadcasted_iota(jnp.int32, (Q_TILE, size), 0) + first_row
                column = lax.broadcasted_iota(jnp.int32, (Q_TILE, size), 1) + start
                allowed = row >= column
                scores = jnp.where(jnp.concatenate([allowed] * GROUPS, axis=0), scores, masked_value)
            chunk_top = jnp.max(scores, axis=-1, keepdims=True)
            new_top = chunk_top if top is None else jnp.maximum(top, chunk_top)
            weights = jnp.exp2((scores - new_top) * exp2_scale).astype(bf16)
            part = matmul(weights, value)
            acc = part if top is None else acc * jnp.exp2((top - new_top) * exp2_scale) + part
            top = new_top
        total = acc[:, HALF : HALF + 1]
        mixed = (acc * (1.0 / total)).astype(bf16)
        log_total = top + jnp.log2(total) * (1.0 / exp2_scale)
        marked = with_lanes(query, -log_total)
        for h in range(GROUPS):
            mixed_ref[first_row : first_row + Q_TILE, LANES * h : LANES * (h + 1)] = mixed[Q_TILE * h : Q_TILE * (h + 1)]
            q_aug_ref[first_row : first_row + Q_TILE, LANES * h : LANES * (h + 1)] = marked[Q_TILE * h : Q_TILE * (h + 1)]


def attend(queries, keys, values):
    rows, k_width = keys.shape
    groups = k_width // LANES
    pair = pl.BlockSpec((rows, Q_LANES), lambda g: (0, g))
    single = pl.BlockSpec((rows, LANES), lambda g: (0, g))
    return call(
        attend_kernel, (groups,), [pair, single, single], [pair, pair], [(queries.shape, bf16)] * 2, [queries, keys, values], "attend"
    )


def attend_back_kernel(q_ref, k_ref, v_ref, do_ref, o_ref, cos_ref, sin_ref, dq_ref, dk_ref, dv_ref, q_s, do_s, dq_s, dk_s, dv_s):
    rows = q_ref.shape[0]
    tiles = rows // Q_TILE
    for tile in range(tiles):
        at = slice(tile * Q_TILE, (tile + 1) * Q_TILE)
        q_s[tile] = heads_down(q_ref[at, :])
        grad = heads_down(do_ref[at, :])
        inner = jnp.sum(grad.astype(f32) * heads_down(o_ref[at, :]).astype(f32), axis=-1, keepdims=True)
        do_s[tile] = with_lanes(grad, -inner)
        dq_s[tile] = jnp.zeros(dq_s.shape[1:], f32)

    def unit(tile, key_start, size, mask_from):
        key = k_ref[key_start : key_start + size, :]
        value = v_ref[key_start : key_start + size, :]
        query, grad = q_s[tile], do_s[tile]
        probs = jnp.exp2(dot_nt(key, query) * exp2_scale)
        if mask_from is not None:
            row = lax.broadcasted_iota(jnp.int32, (size, Q_TILE), 0)
            column = lax.broadcasted_iota(jnp.int32, (size, Q_TILE), 1) + mask_from
            allowed = jnp.concatenate([row <= column] * GROUPS, axis=1)
            probs = jnp.where(allowed, probs, 0.0)
        d_scores = (probs * dot_nt(value, grad)).astype(bf16)
        dv_s[:size] += matmul(probs.astype(bf16), grad)
        dk_s[:size] += matmul(d_scores, query)
        dq_s[tile] += dot_tn(d_scores, key)

    for key_start in range(0, rows, K_CHUNK):
        dk_s[...] = jnp.zeros(dk_s.shape, f32)
        dv_s[...] = jnp.zeros(dv_s.shape, f32)
        tile = key_start // Q_TILE
        unit(tile, key_start, Q_TILE, 0)
        unit(tile + 1, key_start, K_CHUNK, Q_TILE)
        if tile + 2 < tiles:

            @pl.loop(tile + 2, tiles)
            def _(later):
                unit(later, key_start, K_CHUNK, None)

        at = slice(key_start, key_start + K_CHUNK)
        turned = dk_s[...] * score_scale
        turned = turned * cos_ref[at, :] - pltpu.roll(turned, SLOT, 1) * sin_ref[at, :]
        dk_ref[at, :] = turned.astype(bf16)
        dv_ref[at, :] = dv_s[...].astype(bf16)
    for tile in range(tiles):
        at = slice(tile * Q_TILE, (tile + 1) * Q_TILE)
        cosine, sine = cos_ref[at, :], sin_ref[at, :]
        for h in range(GROUPS):
            turned = dq_s[tile, Q_TILE * h : Q_TILE * (h + 1), :] * score_scale
            turned = turned * cosine - pltpu.roll(turned, SLOT, 1) * sine
            dq_ref[at, LANES * h : LANES * (h + 1)] = turned.astype(bf16)


def attend_back(first, groups, q_aug, keys, values, grad, mixed, cosine, sine):
    rows = keys.shape[0]
    tiles = rows // Q_TILE
    pair = pl.BlockSpec((rows, Q_LANES), lambda g: (0, g + first))
    single = pl.BlockSpec((rows, LANES), lambda g: (0, g + first))
    pair_out = pl.BlockSpec((rows, Q_LANES), lambda g: (0, g))
    single_out = pl.BlockSpec((rows, LANES), lambda g: (0, g))
    stacked = (tiles, GROUPS * Q_TILE, LANES)
    table = fixed((rows, LANES))
    return call(
        attend_back_kernel,
        (groups,),
        [pair, single, single, pair, pair, table, table],
        [pair_out, single_out, single_out],
        [((rows, groups * Q_LANES), bf16), ((rows, groups * LANES), bf16), ((rows, groups * LANES), bf16)],
        [q_aug, keys, values, grad, mixed, cosine, sine],
        "attend_back",
        scratch=[
            pltpu.VMEM(stacked, bf16),
            pltpu.VMEM(stacked, bf16),
            pltpu.VMEM(stacked, f32),
            pltpu.VMEM((K_CHUNK, LANES), f32),
            pltpu.VMEM((K_CHUNK, LANES), f32),
        ],
    )


def flat(block):
    return block.reshape(block.shape[0] * block.shape[1], block.shape[2])


def down_columns(down_ref, j, zs):
    rows = down_ref.shape[1] // 3
    return jnp.concatenate([down_ref[z, rows * j : rows * (j + 1), :] for z in zs], axis=0)


def hidden_kernel(n_ref, cot_ref, gate_ref, up_ref, down_ref, product_ref, dboth_ref):
    n_shard, units = gate_ref.shape[0], gate_ref.shape[2]
    third = cot_ref.shape[1] // 3
    step = 256
    for start in range(0, units, step):
        at = slice(start, start + step)
        zs = range(start * n_shard // units, (start + step) * n_shard // units)
        gate = matmul(n_ref[...], flat(gate_ref[:, :, at]))
        up = matmul(n_ref[...], flat(up_ref[:, :, at]))
        d_product = sum(dot_nt(cot_ref[:, third * j : third * (j + 1)], down_columns(down_ref, j, zs)) for j in range(3))
        sigmoid = 1.0 / (1.0 + jnp.exp(-gate))
        silu = gate * sigmoid
        product_ref[:, at] = (silu * up).astype(bf16)
        dboth_ref[:, at] = (d_product * up * sigmoid * (1.0 + gate * (1.0 - sigmoid))).astype(bf16)
        dboth_ref[:, units + start : units + start + step] = (d_product * silu).astype(bf16)


def feed_grads(normed_t, cot, product, d_both):
    width, rows = normed_t.shape
    units = product.shape[1]
    steps = width // units

    def kernel(n_ref, cot_ref, product_ref, both_ref, gate_ref, up_ref, down_ref, turned_ref):
        step = pl.program_id(0)

        @pl.when(step < steps)
        def _():
            gate_ref[...] = matmul(n_ref[...], both_ref[:, :units]).astype(bf16)
            up_ref[...] = matmul(n_ref[...], both_ref[:, units:]).astype(bf16)

        @pl.when(step == steps)
        def _():
            turned_ref[...] = product_ref[...].T

        @pl.when(step >= steps)
        def _():
            down_ref[...] = matmul(turned_ref[...], cot_ref[...]).astype(bf16)

    early = lambda i: (jnp.minimum(i, steps - 1), 0)
    late = lambda i: (0, jnp.maximum(i - steps, 0))
    return call(
        kernel,
        (2 * steps,),
        [pl.BlockSpec((units, rows), early), pl.BlockSpec((rows, units), late), fixed(product.shape), fixed(d_both.shape)],
        [pl.BlockSpec((units, units), early), pl.BlockSpec((units, units), early), pl.BlockSpec((units, units), late)],
        [((width, units), bf16), ((width, units), bf16), ((units, width), bf16)],
        [normed_t, cot, product, d_both],
        "feed_grads",
        scratch=[pltpu.VMEM((units, rows), bf16)],
    )


def whole_of(array):
    return array, array.shape, (0,) * array.ndim


def third_of(array, index):
    rows = 384
    return array, (array.shape[0], rows, array.shape[2]), (0, index, 0)


def hidden_units(normed, cot, weights):
    rows, width = normed.shape
    units = weights[0][0].shape[2]
    tile = 512
    wide = pl.BlockSpec((tile, width), lambda i: (i, 0))
    thin = pl.BlockSpec((tile, units), lambda i: (i, 0))
    return call(
        hidden_kernel,
        (rows // tile,),
        [wide, wide] + [part(block, index) for _, block, index in weights],
        [thin, pl.BlockSpec((tile, 2 * units), lambda i: (i, 0))],
        [((rows, units), bf16), ((rows, 2 * units), bf16)],
        [normed, cot] + [a for a, _, _ in weights],
        "hidden_units",
    )


def sum_rows_call(body, base, lhs, rhs, others, outs, tile, name):
    rows = outs[0][0][0]

    def shifted(cols):
        return pl.BlockSpec((tile, cols), lambda i, base: (base[0] + i, 0))

    def plain(cols):
        return pl.BlockSpec((tile, cols), lambda i, base: (i, 0))

    in_specs = [shifted(a.shape[1]) for a in lhs] + [part(block, index) for _, block, index in rhs]
    for a, kind in others:
        in_specs.append(fixed(a.shape) if kind == "whole" else {"shifted": shifted, "plain": plain}[kind](a.shape[1]))
    out_specs = [plain(shape[1]) if shape[0] == rows else whole(shape) for shape, _ in outs]
    n_lhs, n_rhs, n_other = len(lhs), len(rhs), len(others)

    def kernel(base_ref, *refs):
        left, refs = refs[:n_lhs], refs[n_lhs:]
        right, refs = refs[:n_rhs], refs[n_rhs:]
        body(left, right, refs[:n_other], refs[n_other:])

    return call(
        kernel,
        (rows // tile,),
        in_specs,
        out_specs,
        outs,
        [*lhs, *[a for a, _, _ in rhs], *[a for a, _ in others]],
        name,
        [base],
    )


def norm_back(grad_normed, values, scale_rows, gain):
    scaled = grad_normed * gain
    return scale_rows * scaled - values * (scale_rows * scale_rows * scale_rows) * jnp.mean(scaled * values, axis=-1, keepdims=True)


def column_sums(values):
    return jnp.sum(values.reshape(-1, 8, values.shape[-1]), axis=0)


def half_specs(tile, tiles, width):
    own = pl.BlockSpec((tile, width), lambda i, core: (jnp.clip(i - tiles * core[0], 0, tiles - 1), 0))
    far = pl.BlockSpec((tile, width), lambda i, core: (jnp.clip(i - tiles * (1 - core[0]), 0, tiles - 1), 0))
    return [own, far]


def place_half(core_ref, tiles, own_refs, far_refs, out_ref):
    is_own = pl.program_id(0) // tiles == core_ref[0]

    def place(refs):
        start = 0
        for ref in refs:
            out_ref[:, start : start + ref.shape[1]] = ref[...]
            start += ref.shape[1]

    @pl.when(is_own)
    def _():
        place(own_refs)

    @pl.when(jnp.logical_not(is_own))
    def _():
        place(far_refs)


def join_halves(core, own, far):
    rows, cols = own[0].shape
    count = len(own)
    width = count * cols
    tile = 256
    tiles = rows // tile

    def kernel(core_ref, *refs):
        out_ref, turned_ref = refs[2 * count :]
        place_half(core_ref, tiles, refs[:count], refs[count : 2 * count], out_ref)
        turned_ref[...] = out_ref[...].T

    own_spec, far_spec = half_specs(tile, tiles, cols)
    return call(
        kernel,
        (2 * tiles,),
        [own_spec] * count + [far_spec] * count,
        [pl.BlockSpec((tile, width), lambda i, _: (i, 0)), pl.BlockSpec((width, tile), lambda i, _: (0, i))],
        [((2 * rows, width), bf16), ((width, 2 * rows), bf16)],
        [*own, *far],
        "join_halves",
        [core],
    )


def mixed_back(core, own, far, w_out_rows):
    rows, cols = own[0].shape
    count = len(own)
    width = count * cols
    heads = w_out_rows.shape[0]
    tile = 512
    tiles = rows // tile

    own_spec, far_spec = half_specs(tile, tiles, cols)

    def kernel(core_ref, *refs):
        w_ref, out_ref, grad_ref = refs[2 * count :]
        place_half(core_ref, tiles, refs[:count], refs[count : 2 * count], out_ref)
        grad_ref[...] = dot_nt(out_ref[...], w_ref[...]).astype(bf16)

    return call(
        kernel,
        (2 * tiles,),
        [own_spec] * count + [far_spec] * count + [fixed(w_out_rows.shape)],
        [pl.BlockSpec((tile, width), lambda i, _: (i, 0)), pl.BlockSpec((tile, heads), lambda i, _: (i, 0))],
        [((2 * rows, width), bf16), ((2 * rows, heads), bf16)],
        [*own, *far, w_out_rows],
        "mixed_back",
        [core],
    )


def out_rows(place, blocks):
    n_shard, rows_in, cols = blocks[0].shape
    chunks = rows_in // HALF
    quarters = len(blocks)
    shape = (quarters * quarters * SLOT, chunks * cols)

    def kernel(place_ref, *refs):
        out_ref = refs[-1]
        out_ref[...] = jnp.zeros(shape, bf16)
        for group in range(quarters):
            for at in range(quarters):
                row = pl.multiple_of(Q_LANES * group + SLOT * (at ^ place_ref[0]), SLOT)
                for j in range(chunks):
                    out_ref[pl.ds(row, HALF), cols * j : cols * (j + 1)] = refs[at][group ^ place_ref[0], HALF * j : HALF * (j + 1), :]

    (out,) = call(
        kernel,
        (1,),
        [fixed((n_shard, rows_in, cols))] * quarters,
        [whole(shape)],
        [(shape, bf16)],
        blocks,
        "out_rows",
        [place],
    )
    return out


def out_grad_blocks(place, mixed, grad):
    rows, heads = mixed.shape
    width = grad.shape[1]
    quarters = heads // Q_LANES
    tile = 512

    def kernel(place_ref, mixed_ref, grad_ref, *refs):
        outs = refs[:quarters]
        group = pl.program_id(0)
        sums = dot_tn(mixed_ref[...], grad_ref[...]).astype(bf16)
        refs[quarters][...] = sums
        shard = group ^ place_ref[0]
        for at in range(quarters):
            row = pl.multiple_of(SLOT * (at ^ place_ref[0]), SLOT)
            outs[at][shard] = refs[quarters][pl.ds(row, HALF), :]

    return call(
        kernel,
        (quarters,),
        [pl.BlockSpec((rows, Q_LANES), lambda g, _: (0, g)), fixed((rows, width))],
        [whole((quarters, HALF, width))] * quarters,
        [((quarters, HALF, width), bf16)] * quarters,
        [mixed, grad],
        "out_grads",
        [place],
        [pltpu.VMEM((Q_LANES, width), bf16)],
    )


def qkv_grad(normed_t, d_query, d_key, d_value):
    width, rows = normed_t.shape
    spread = jnp.asarray(spread_matrix(), bf16)
    tile = 512

    def kernel(n_ref, q_ref, k_ref, v_ref, spread_ref, out_ref):
        query = matmul(n_ref[...], q_ref[...]).astype(bf16)
        both = matmul(n_ref[...], jnp.concatenate([k_ref[...], v_ref[...]], axis=1)).astype(bf16)
        out_ref[...] = dot_nt(jnp.concatenate([query, both], axis=1), spread_ref[...]).astype(bf16)

    (out,) = call(
        kernel,
        (width // tile,),
        [
            pl.BlockSpec((tile, rows), lambda i: (i, 0)),
            fixed(d_query.shape),
            fixed(d_key.shape),
            fixed(d_value.shape),
            fixed(spread.shape),
        ],
        [pl.BlockSpec((tile, GROUP_COLS), lambda i: (i, 0))],
        [((width, GROUP_COLS), bf16)],
        [normed_t, d_query, d_key, d_value, spread],
        "qkv_grad",
    )
    return out


def unit_columns(where, pieces, n_shard, index):
    depth, cols = pieces[0].shape[0] // 2, pieces[0].shape[1]
    tile = 96
    count = len(pieces)
    quarters = count // 2
    unit_cols = cols // n_shard

    def kernel(where_ref, *refs):
        out_ref = refs[-1]
        for k in range(count):
            unit = quarters * (where_ref[1] ^ (k // quarters)) + (where_ref[0] ^ (k % quarters))
            for z in range(n_shard):
                at = pl.multiple_of((count * z + unit) * unit_cols, unit_cols)
                out_ref[:, pl.ds(at, unit_cols)] = refs[k][:, unit_cols * z : unit_cols * (z + 1)].astype(f32)

    steps = depth // tile
    (out,) = call(
        kernel,
        (depth // tile,),
        [pl.BlockSpec((tile, cols), lambda i, _: (index * steps + i, 0))] * count,
        [pl.BlockSpec((tile, cols * count), lambda i, _: (i, 0))],
        [((depth, cols * count), f32)],
        pieces,
        "unit_columns",
        [where],
    )
    return out


def unit_rows(where, pieces, down_depth):
    depth, width = pieces[0].shape
    count = len(pieces)
    quarters = count // 2
    out_depth = depth - down_depth

    def unit_at(i, where_ref):
        return quarters * (where_ref[1] ^ (i // quarters)) + (where_ref[0] ^ (i % quarters))

    def kernel(where_ref, *refs):
        for k in range(count):

            @pl.when(pl.program_id(0) == k)
            def _():
                refs[count][...] = refs[k][:down_depth, :].astype(f32)
                refs[count + 1][...] = refs[k][down_depth:, :].astype(f32)

    return call(
        kernel,
        (count,),
        [fixed((depth, width))] * count,
        [
            pl.BlockSpec((down_depth, width), lambda i, where: (unit_at(i, where), 0)),
            pl.BlockSpec((out_depth, width), lambda i, where: (unit_at(i, where), 0)),
        ],
        [((down_depth * count, width), f32), ((out_depth * count, width), f32)],
        pieces,
        "unit_rows",
        [where],
    )


def head_columns(where, pieces):
    depth, cols = pieces[0].shape
    count = len(pieces)
    quarters = count // 2
    split = 2

    def kernel(where_ref, *refs):
        q_out, k_out, v_out = refs[count:]
        place, core = where_ref[0], where_ref[1]
        row = lax.broadcasted_iota(jnp.int32, (cols, cols), 0)
        column = lax.broadcasted_iota(jnp.int32, (cols, cols), 1)

        def moved(piece, start, size, to):
            chosen = (row >= start) & (row < start + size) & (row - start == column - to)
            return matmul(piece, jnp.where(chosen, 1.0, 0.0).astype(bf16))

        for at in range(quarters):
            total = 0.0
            for other in range(split):
                total += moved(refs[quarters * other + at][...], 0, Q_COLS, Q_COLS * (core ^ other))
            q_out[:, pl.ds(pl.multiple_of(cols * (place ^ at), LANES), cols)] = total
        for pair in range(quarters // 2):
            keys = values = 0.0
            for low in range(2):
                for other in range(split):
                    piece = refs[quarters * other + 2 * pair + low][...]
                    to = HEAD_DIM * (2 * ((place & 1) ^ low) + (core ^ other))
                    keys += moved(piece, Q_COLS, HEAD_DIM, to)
                    values += moved(piece, Q_COLS + HEAD_DIM, HEAD_DIM, to)
            start = pl.multiple_of(cols * ((place >> 1) ^ pair), LANES)
            k_out[:, pl.ds(start, cols)] = keys
            v_out[:, pl.ds(start, cols)] = values

    shapes = [(depth, quarters * split * w) for w in (Q_COLS, HEAD_DIM, HEAD_DIM)]
    return call(
        kernel, (1,), [fixed((depth, cols))] * count, [whole(s) for s in shapes], [(s, f32) for s in shapes], pieces, "head_columns", [where]
    )


def chip_layer(
    tokens, span_order, token_positions, attn_gain, w_query, w_key, w_value, w_out, mlp_gain, w_gate, w_up, w_down, cotangent
):
    seq_dev, local_len, width = tokens.shape
    n_ctx, n_shard = lax.axis_size("ctx"), lax.axis_size("shard")
    split = n_ctx // seq_dev
    full_len = local_len * n_ctx
    half_rows = full_len // split
    spans_dev = local_len // SPAN
    quarters = 4
    units = w_gate.shape[1] // (split * quarters)
    unit_cols = units // n_shard
    gain_width = attn_gain.shape[0]
    ctx, batch, shard = lax.axis_index("ctx"), lax.axis_index("batch"), lax.axis_index("shard")
    seq, core = ctx // split, ctx % split
    place = 2 * seq + batch

    perm_x = [(c, c ^ split) for c in range(n_ctx)]
    perm_core = [(c, c ^ 1) for c in range(n_ctx)]
    perm_both = [(c, c ^ (split | 1)) for c in range(n_ctx)]
    perm_diagonal = [(2 * c + b, 2 * (c ^ split) + (b ^ 1)) for c in range(n_ctx) for b in range(2)]
    over_x = lambda a: lax.ppermute(a, "ctx", perm_x)
    over_core = lambda a: lax.ppermute(a, "ctx", perm_core)
    over_both = lambda a: lax.ppermute(a, "ctx", perm_both)
    over_y = lambda a: lax.ppermute(a, "batch", [(0, 1), (1, 0)])
    over_diagonal = lambda a: lax.ppermute(a, ("ctx", "batch"), perm_diagonal)

    def over_z(piece):
        gathered = lax.all_gather(piece, "shard", axis=0, tiled=True)
        return gathered.reshape(n_shard, piece.shape[0], piece.shape[1])

    def pick(array, index, axis):
        return lax.dynamic_index_in_dim(array, index, axis, keepdims=False)

    def scatter(block):
        return lax.psum_scatter(block, "shard", scatter_dimension=0, tiled=True)

    def add(*terms):
        return functools.reduce(lambda a, b: a + b, [t.astype(f32) for t in terms]).astype(bf16)

    def fence(*arrays):
        return lax.optimization_barrier(arrays)

    column = split * place + core
    unit_at = quarters * core + place

    def columns_of(array, width_of):
        return lax.dynamic_slice_in_dim(array, column * width_of, width_of, 1)

    def units_of(array, at):
        blocks = [lax.dynamic_slice_in_dim(array, (split * quarters * z + at) * unit_cols, unit_cols, 1) for z in range(n_shard)]
        return jnp.concatenate(blocks, axis=1)

    def stacked(rows, cols):
        return jnp.concatenate([rows[:, cols * j : cols * (j + 1)] for j in range(rows.shape[1] // cols)], axis=0)

    head_piece = jnp.concatenate(
        [columns_of(w_query, Q_COLS), columns_of(w_key, HEAD_DIM), columns_of(w_value, HEAD_DIM)], axis=1
    )
    gains = jnp.pad(jnp.stack([attn_gain, mlp_gain]), ((0, PAD_ROWS - 2), (0, 0)))
    head_piece = jnp.concatenate([head_piece, gains], axis=0)

    def second_piece(at):
        return jnp.concatenate([units_of(w_up, at), stacked(lax.dynamic_slice_in_dim(w_down, at * unit_cols, unit_cols, 0), units)], axis=0)

    own_tokens, sent_tokens = pick(tokens, seq, 0), pick(tokens, 1 - seq, 0)
    positions = pick(token_positions, seq, 0)
    sent_positions = pick(token_positions, 1 - seq, 0)
    head_piece, own_tokens, sent_tokens, positions, sent_positions, w_out, w_gate, w_up, w_down = fence(
        head_piece, own_tokens, sent_tokens, positions, sent_positions, w_out, w_gate, w_up, w_down
    )
    head_own = over_z(head_piece)
    positions = jnp.stack([positions, over_x(sent_positions)])
    x_near = jnp.concatenate([own_tokens, over_x(sent_tokens)], axis=0)
    out_piece = stacked(lax.dynamic_slice_in_dim(w_out, unit_at * HALF, HALF, 0), GROUP_COLS)
    gate_piece, second_own, second_last = units_of(w_gate, unit_at), second_piece(unit_at), second_piece(unit_at ^ 3)
    head_own, out_piece, x_near, positions, gate_piece, second_own, second_last, cotangent = fence(
        head_own, out_piece, x_near, positions, gate_piece, second_own, second_last, cotangent
    )

    out_own, gate_own = over_z(out_piece), over_z(gate_piece)
    head_x, head_y, x_far = over_x(head_own), over_y(head_own), over_core(x_near)
    positions = jnp.concatenate([positions, over_core(positions)], axis=0).reshape(-1, SPAN)
    cot_own, cot_sent = pick(cotangent, seq, 0), pick(cotangent, 1 - seq, 0)
    order = pick(span_order, seq, 0)
    n_spans = order.shape[0]
    span_ids = jnp.arange(n_spans, dtype=jnp.int32)
    slot_of = jnp.sum(jnp.where(order[None, :] == span_ids[:, None], span_ids[None, :], 0), axis=1)
    owner = slot_of // spans_dev
    from_far = (owner % split) ^ core
    side_place = ((owner // split) ^ seq) * spans_dev + slot_of % spans_dev
    places = [
        jnp.where(from_far == 0, side_place, 0).astype(jnp.int32),
        jnp.where(from_far == 0, 0, side_place).astype(jnp.int32),
        from_far.astype(jnp.int32),
    ]
    head_x, head_y, x_far, positions, cot_own, cot_sent = fence(head_x, head_y, x_far, positions, cot_own, cot_sent)

    middle = n_shard // 2
    head_last = [over_x(head_y[:middle]), over_y(head_x[middle:])]
    choice = (from_far * seq_dev * spans_dev + side_place)[:, None] == span_ids[None, :]
    positions = jnp.sum(jnp.where(choice[:, :, None], positions[None], 0), axis=1).reshape(full_len)
    frequency = rope_base ** (-2.0 * jnp.arange(HALF, dtype=f32) / HEAD_DIM)
    angles = positions.astype(f32)[:, None] * frequency
    blank = jnp.zeros((full_len, SLOT - HALF), f32)
    cos_half, sin_half = jnp.cos(angles), jnp.sin(angles)
    cosine = jnp.concatenate([cos_half, blank, cos_half, blank], axis=1)
    sine = jnp.concatenate([-sin_half, blank, sin_half, blank], axis=1)
    gain_one = head_own[:, gain_width, :].reshape(1, width).astype(f32)
    gain_two = head_own[:, gain_width + 1, :].reshape(1, width).astype(f32)
    *head_last, cosine, sine, cot_sent, gate_own, second_own, out_own = fence(
        *head_last, cosine, sine, cot_sent, gate_own, second_own, out_own
    )

    out_blocks = [out_own, over_y(out_own), over_x(out_own), over_diagonal(out_own)]
    head_blocks = [head_own, head_y, head_x, *head_last]
    x, normed, normed_t, queries, keys, values, w_qkv = front(places, x_near, x_far, cosine, sine, gain_one, head_blocks)
    x, normed_t, queries, keys, values, w_qkv = fence(x, normed_t, queries, keys, values, w_qkv)

    second_own = over_z(second_own)
    cot_received, gate_y = over_x(cot_sent), over_y(gate_own)
    mixed, q_aug = attend(queries, keys, values)
    cot_near = jnp.concatenate([cot_own, cot_received], axis=0)
    up_own = second_own[:, :gain_width]
    mixed, q_aug, cot_near, gate_y, up_own, second_own, second_last, gate_sent, *out_blocks = fence(
        mixed, q_aug, cot_near, gate_y, up_own, second_own, second_last, gate_own, *out_blocks
    )

    second_last = over_z(second_last)
    gate_x, cot_far = over_x(gate_sent), over_core(cot_near)
    up_y = over_y(up_own)
    place_at = place.astype(jnp.int32)[None]
    w_out_rows = out_rows(place_at, out_blocks)
    mine = core.astype(jnp.int32)[None]
    other = 1 - mine
    row_tile = 256
    tiles_half = half_rows // row_tile
    full_out = (w_out_rows, w_out_rows.shape, (0, 0))

    def out_dot(left, right, store):
        store(slice(None), matmul(left[0][...], right[0][...]))

    def back_dot(left, right, store):
        total = 0.0
        for k, both in enumerate(left):
            for which in range(2):
                total += dot_nt(both[:, units * which : units * (which + 1)], flat(right[2 * k + which][...]))
        store(slice(None), total)

    def down_dot(left, right, store):
        for j in range(width // units):
            total = sum(matmul(a[...], down_columns(b, j, range(n_shard))) for a, b in zip(left, right))
            store(slice(units * j, units * (j + 1)), total)

    def in_dot(left, right, store):
        total = 0.0
        for which, weights in enumerate(right):
            total += dot_nt(jnp.concatenate([a[...] for a in left[which::3]], axis=1), weights[...])
        store(slice(None), total)

    def kept(dots, left, right):
        found = []
        dots(left, right, lambda at, total: found.append(total))
        return found[0]

    thirds = [slice(units * j, units * (j + 1)) for j in range(width // units)]

    def sent_parts(lhs, rhs, dots, name):
        def body(left, right, _, outs):
            def store(at, total):
                start = at.start or 0
                for out, place_of in zip(outs, thirds):
                    if start <= place_of.start < start + total.shape[1]:
                        out[...] = total[:, place_of.start - start : place_of.stop - start].astype(bf16)

            dots(left, right, store)

        tile = half_rows // 2
        return sum_rows_call(body, other * 2, lhs, rhs, [], [((half_rows, units), bf16)] * len(thirds), tile, name)

    def joined(refs):
        return jnp.concatenate([r[...] for r in refs], axis=1).astype(f32)

    received = [over_core(a) for a in sent_parts([mixed], [full_out], out_dot, "out_other")]

    def hidden_body(left, right, others, outs):
        x_ref, *received_refs, gain_ref = others
        hidden = x_ref[...].astype(f32) + kept(out_dot, left, right) + joined(received_refs)
        outs[0][...] = hidden
        normed_rows = (hidden * rms_scale(hidden) * gain_ref[...]).astype(bf16)
        for out, at in zip(outs[1:], thirds):
            out[...] = normed_rows[:, at]

    hidden, *normed_two_own = sum_rows_call(
        hidden_body,
        mine * tiles_half,
        [mixed],
        [full_out],
        [(x, "shifted"), *[(r, "plain") for r in received], (gain_two, "whole")],
        [((half_rows, width), f32)] + [((half_rows, units), bf16)] * len(thirds),
        row_tile,
        "out_own",
    )
    normed_two_far = [over_core(a) for a in normed_two_own]
    cot = span_join(places, cot_near, cot_far)
    down_own = second_own[:, gain_width:]
    normed_two_own, normed_two_far, cot, gate_x, up_y, up_own, down_own = fence(
        normed_two_own, normed_two_far, cot, gate_x, up_y, up_own, down_own
    )
    up_x, down_y = over_x(up_own), over_y(down_own)
    normed_two, normed_two_t = join_halves(mine, normed_two_own, normed_two_far)
    normed_two, normed_two_t, cot, down_own = fence(normed_two, normed_two_t, cot, down_own)

    def feed(normed_two, cot, weights, with_grads=True):
        product, d_both = hidden_units(normed_two, cot, weights)
        if not with_grads:
            return weights, product, d_both
        return weights, product, d_both, feed_grads(normed_two_t, cot, product, d_both)

    def apart(*arrays):
        return [whole_of(a) for a in arrays]

    fed = [feed(normed_two, cot, apart(gate_own, up_own, down_own))]
    own_grads, normed_two, up_x, down_y, gate_x, down_own = fence(fed[0][3], normed_two, up_x, down_y, gate_x, down_own)
    gate_last, down_x = over_y(gate_x), over_x(down_own)
    fed.append(feed(normed_two, cot, apart(gate_y, up_y, down_y)))
    (gate_gy, up_gy, down_gy), normed_two, gate_last, down_x, second_last = fence(fed[1][3], normed_two, gate_last, down_x, second_last)
    down_gy = over_y(down_gy)
    fed.append(feed(normed_two, cot, [whole_of(gate_last), third_of(second_last, 0), third_of(second_last, 1)]))
    (gate_gl, up_gl, down_gl), normed_two, gate_gy, up_gy, down_gy = fence(fed[2][3], normed_two, gate_gy, up_gy, down_gy)
    gate_gy, gate_gl = over_y(gate_gy), scatter(gate_gl)
    fed.append(feed(normed_two, cot, apart(gate_x, up_x, down_x)))
    products, d_boths = [f[1] for f in fed], [f[2] for f in fed]
    (gate_gx, up_gx, down_gx), d_boths, products, gate_gy, up_gy, gate_gl, up_gl, down_gl = fence(
        fed[3][3], d_boths, products, gate_gy, up_gy, gate_gl, up_gl, down_gl
    )

    back_rhs = [f[0][k] for f in fed for k in range(2)]
    downs = [f[0][2] for f in fed]
    up_gy, gate_gx, up_gl = over_y(up_gy), over_x(gate_gx), scatter(up_gl)

    received_two = [over_core(a) for a in sent_parts(d_boths, back_rhs, back_dot, "back_other")]
    out_sent = sent_parts(products, downs, down_dot, "down_other")
    received_two, out_sent, up_gy, gate_gx, up_gl, up_gx, down_gx, down_gl = fence(
        received_two, out_sent, up_gy, gate_gx, up_gl, up_gx, down_gx, down_gl
    )

    def back_body(left, right, others, outs):
        *received_refs, hidden_ref, cot_ref, gain_ref = others
        grad_normed = kept(back_dot, left, right) + joined(received_refs)
        values_ = hidden_ref[...]
        scale_rows = rms_scale(values_)
        grad_hidden = cot_ref[...].astype(f32) + norm_back(grad_normed, values_, scale_rows, gain_ref[...])
        outs[0][...] = grad_hidden
        for out, at in zip(outs[2:], thirds):
            out[...] = grad_hidden[:, at].astype(bf16)

        @pl.when(pl.program_id(0) == 0)
        def _():
            outs[1][...] = jnp.zeros(outs[1].shape, f32)

        outs[1][...] += column_sums(grad_normed * values_ * scale_rows)

    up_gx, down_gl = over_x(up_gx), over_y(down_gl)
    received_out = [over_core(a) for a in out_sent]
    grad_hidden, gain_two_sums, *grad_attended_own = sum_rows_call(
        back_body,
        mine * tiles_half,
        d_boths,
        back_rhs,
        [*[(r, "plain") for r in received_two], (hidden, "plain"), (cot, "shifted"), (gain_two, "whole")],
        [((half_rows, width), f32), ((8, width), f32)] + [((half_rows, units), bf16)] * len(thirds),
        row_tile,
        "back_own",
    )
    gate_sum = scatter(add(own_grads[0], gate_gy, gate_gx))
    grad_attended_far = [over_core(a) for a in grad_attended_own]

    def down_body(left, right, others, outs):
        hidden_ref, *received_refs = others

        def store(at, total):
            received_rows = received_refs[at.start // units][...].astype(f32)
            outs[0][:, at] = (hidden_ref[:, at] + total + received_rows).astype(bf16)

        down_dot(left, right, store)

    (layer_rows,) = sum_rows_call(
        down_body,
        mine * tiles_half,
        products,
        downs,
        [(hidden, "plain"), *[(r, "plain") for r in received_out]],
        [((half_rows, width), bf16)],
        row_tile,
        "down_own",
    )
    grad_attended_own, grad_attended_far, layer_rows, up_gx, down_gl, gate_sum, gate_gl, up_gl = fence(
        grad_attended_own, grad_attended_far, layer_rows, up_gx, down_gl, gate_sum, gate_gl, up_gl
    )
    down_gx = add(down_gx, down_gl)

    pair_order = order.reshape(n_ctx, spans_dev // 2, 2)
    in_half = jnp.where(pair_order[..., 0] // (n_spans // 2) == core, pair_order[..., 0], pair_order[..., 1]) - core * (n_spans // 2)
    steps = jnp.arange(n_ctx, dtype=jnp.int32) ^ ctx
    send_places = in_half[steps].reshape(-1).astype(jnp.int32)
    my_order = lax.dynamic_slice_in_dim(span_order, ctx * spans_dev, spans_dev, 1)
    from_mine = (my_order // (n_spans // 2) == core).reshape(seq_dev, spans_dev // 2, 2, 1, 1)

    def to_slots(arranged):
        return [arranged[0], over_core(arranged[1]), over_x(arranged[2]), over_both(arranged[3])]

    def arrange(rows):
        arranged = span_copy(send_places, rows).reshape(n_ctx, -1, width)
        return [arranged[k] for k in range(n_ctx)]

    def from_slots(parts):
        parts = [p.reshape(spans_dev // 2, 1, SPAN, width) for p in parts]
        near = jnp.where(from_mine[seq], parts[0], parts[1])
        far = jnp.where(from_mine[1 - seq], parts[2], parts[3])
        near, far = near.reshape(local_len, width), far.reshape(local_len, width)
        return jnp.where(seq == 0, jnp.stack([near, far]), jnp.stack([far, near]))

    def both_cores(side):
        return side + [over_core(a) for a in side]

    up_sum = scatter(add(own_grads[1], up_gy, up_gx))
    down_gx = over_x(down_gx)
    both_gl = over_y(jnp.concatenate([gate_gl, up_gl], axis=0))
    grad_attended, grad_mixed = mixed_back(mine, grad_attended_own, grad_attended_far, w_out_rows)
    out_grads = [b.reshape(-1, width) for b in out_grad_blocks(place_at, mixed, grad_attended)]
    layer_parts = arrange(layer_rows)
    grad_mixed, out_grads, down_gx, layer_parts, up_sum, both_gl = fence(grad_mixed, out_grads, down_gx, layer_parts, up_sum, both_gl)

    def back_of(group, q_aug):
        return attend_back(group, 1, q_aug, keys, values, grad_mixed, mixed, cosine, sine)

    down_sum = scatter(add(own_grads[2], down_gy, down_gx))
    layer_parts = [layer_parts[0], over_core(layer_parts[1]), over_x(layer_parts[2]), layer_parts[3]]
    both_gl, out_y, out_last = over_x(both_gl), over_y(out_grads[1]), over_y(out_grads[3])
    back_last = back_of(3, q_aug)
    back_last, q_aug, both_gl, out_last = fence(back_last, q_aug, both_gl, out_last)
    both_sum = add(jnp.concatenate([gate_sum, up_sum], axis=0), both_gl)
    qkv_last = qkv_grad(normed_t, *back_last)
    out_x = add(out_grads[2], out_last)
    qkv_last, q_aug, out_x, both_sum, layer_parts, out_y = fence(qkv_last, q_aug, out_x, both_sum, layer_parts, out_y)

    qkv_last, out_x, both_x = over_y(qkv_last), over_x(out_x), over_x(both_sum)
    back_x = back_of(2, q_aug)
    back_x, q_aug, qkv_last, out_x, down_sum = fence(back_x, q_aug, qkv_last, out_x, down_sum)
    qkv_x = add(qkv_grad(normed_t, *back_x), qkv_last)
    out_sum = add(out_grads[0], out_y, out_x)
    qkv_x, out_sum, q_aug, both_sum, both_x = fence(qkv_x, out_sum, q_aug, both_sum, both_x)

    out_sum = scatter(out_sum)
    qkv_x, both_last, both_y = over_x(qkv_x), over_y(both_x), over_y(both_sum)
    both_far = [over_core(a) for a in (both_sum, both_x)]
    back_y = back_of(1, q_aug)
    back_y, q_aug, both_far, out_sum = fence(back_y, q_aug, both_far, out_sum)
    qkv_y = qkv_grad(normed_t, *back_y)
    row_sum = jnp.concatenate([down_sum, out_sum], axis=0)
    qkv_y, q_aug, row_sum, qkv_x, both_y, both_last, layer_parts = fence(qkv_y, q_aug, row_sum, qkv_x, both_y, both_last, layer_parts)

    layer_parts[3] = over_both(layer_parts[3])
    qkv_y, row_x, row_y = over_y(qkv_y), over_x(row_sum), over_y(row_sum)
    both_far = [both_far[0], over_core(both_y), both_far[1], over_core(both_last)]
    back_own = back_of(0, q_aug)
    back_own, both_far = fence(back_own, both_far)

    depth = w_qkv.shape[0]
    q_width, k_width = queries.shape[1], keys.shape[1]
    in_rhs = [(w_qkv, (depth, q_width), (0, 0))]
    in_rhs += [(w_qkv, (depth, k_width), (0, q_width // k_width + which)) for which in range(2)]
    qkv_sum = add(qkv_grad(normed_t, *back_own), qkv_y, qkv_x)
    qkv_sum, back_own, row_x, row_y, layer_parts = fence(qkv_sum, back_own, row_x, row_y, layer_parts)
    in_lhs = [*back_own, *back_y, *back_x, *back_last]
    qkv_sum = scatter(qkv_sum)
    row_last = over_y(row_x)
    received_in = [over_core(a) for a in sent_parts(in_lhs, in_rhs, in_dot, "in_other")]
    row_far = [over_core(a) for a in (row_sum, row_y, row_x)]

    def in_body(left, right, others, outs):
        *received_refs, x_ref, grad_ref, gain_ref = others
        grad_normed = kept(in_dot, left, right) + joined(received_refs)
        values_ = x_ref[...].astype(f32)
        scale_rows = rms_scale(values_)
        outs[0][...] = (grad_ref[...] + norm_back(grad_normed, values_, scale_rows, gain_ref[...])).astype(bf16)

        @pl.when(pl.program_id(0) == 0)
        def _():
            outs[1][...] = jnp.zeros(outs[1].shape, f32)

        outs[1][...] += column_sums(grad_normed * values_ * scale_rows)

    grad_rows, gain_one_sums = sum_rows_call(
        in_body,
        mine * tiles_half,
        in_lhs,
        in_rhs,
        [*[(r, "plain") for r in received_in], (x, "shifted"), (grad_hidden, "plain"), (gain_one, "whole")],
        [((half_rows, width), bf16), ((8, width), f32)],
        row_tile,
        "in_own",
    )
    sums = jnp.stack([gain_one_sums.sum(0), gain_two_sums.sum(0)])
    sums = sums + over_x(sums)
    sums = sums + over_core(sums)
    token_parts, sums, qkv_sum, row_far, row_last = fence(arrange(grad_rows), sums, qkv_sum, row_far, row_last)

    qkv_x, qkv_y = over_x(qkv_sum), over_y(qkv_sum)
    row_far.append(over_core(row_last))
    sums = sums + over_y(sums)
    layer_out = from_slots(layer_parts)
    token_parts, sums, qkv_x, qkv_y, layer_out, row_far = fence(token_parts, sums, qkv_x, qkv_y, layer_out, row_far)

    token_parts = to_slots(token_parts)
    qkv_last = over_y(qkv_x)
    where = jnp.stack([place, core]).astype(jnp.int32)
    both_pieces = [both_sum, both_y, both_x, both_last] + both_far
    grad_w_gate = unit_columns(where, both_pieces, n_shard, 0)
    grad_w_up = unit_columns(where, both_pieces, n_shard, 1)
    grad_w_down, grad_w_out = unit_rows(where, [row_sum, row_y, row_x, row_last] + row_far, unit_cols)
    head_grads = head_columns(where, both_cores([qkv_sum, qkv_y, qkv_x, qkv_last]))
    token_parts, grad_w_gate, grad_w_up, grad_w_down, grad_w_out, head_grads, sums = fence(
        token_parts, grad_w_gate, grad_w_up, grad_w_down, grad_w_out, head_grads, sums
    )
    total = lax.dynamic_slice_in_dim(sums, shard * gain_width, gain_width, 1)
    for step in range(1, n_shard):
        to = lax.dynamic_slice_in_dim(sums, (shard + step) % n_shard * gain_width, gain_width, 1)
        total = total + lax.ppermute(to, "shard", [(z, (z + step) % n_shard) for z in range(n_shard)])
    grad_w_query, grad_w_key, grad_w_value = head_grads
    grad_tokens = from_slots(token_parts)

    return (
        layer_out,
        grad_tokens,
        total[0],
        grad_w_query,
        grad_w_key,
        grad_w_value,
        grad_w_out,
        total[1],
        grad_w_gate,
        grad_w_up,
        grad_w_down,
    )


def rope_tables(positions):
    half_dim = HEAD_DIM // 2
    frequency = rope_base ** (-2.0 * jnp.arange(half_dim, dtype=jnp.float32) / HEAD_DIM)
    angles = positions.astype(jnp.float32)[..., None] * frequency
    return (jnp.cos(angles), jnp.sin(angles))


def rotate(values, cosine, sine_table):
    half_dim = values.shape[-1] // 2
    first_half = values[..., :half_dim]
    second_half = values[..., half_dim:]
    cosine = cosine[..., None, :]
    sine_table = sine_table[..., None, :]
    return jnp.concatenate(
        [
            first_half * cosine - second_half * sine_table,
            second_half * cosine + first_half * sine_table,
        ],
        axis=-1,
    )


def general_layer(
    tokens,
    span_order,
    token_positions,
    attn_gain,
    w_query,
    w_key,
    w_value,
    w_out,
    mlp_gain,
    w_gate,
    w_up,
    w_down,
    cotangent,
):
    seq_dev, local_len, model_width = tokens.shape
    row_count = seq_dev * local_len
    groups = HEADS // KV_HEADS
    kv_width = KV_HEADS * HEAD_DIM
    score_scale = HEAD_DIM ** (-0.5)
    full_len = local_len * lax.axis_size("ctx")
    ctx_index = lax.axis_index("ctx")
    slot_index = jnp.arange(full_len, dtype=jnp.int32)
    key_index = span_order[:, slot_index // SPAN] * SPAN + slot_index[None, :] % SPAN
    query_index = lax.dynamic_slice_in_dim(key_index, ctx_index * local_len, local_len, 1)
    allowed = query_index[:, :, None] >= key_index[:, None, :]
    cosine, sine_table = rope_tables(token_positions)
    gain_one, wq_full, wk_full, wv_full, wo_full = (
        lax.all_gather(attn_gain, "shard", axis=0, tiled=True),
        lax.all_gather(w_query, "shard", axis=0, tiled=True),
        lax.all_gather(w_key, "shard", axis=0, tiled=True),
        lax.all_gather(w_value, "shard", axis=0, tiled=True),
        lax.all_gather(w_out, "shard", axis=0, tiled=True),
    )
    x_rows = tokens.reshape(row_count, model_width).astype(jnp.float32)
    scale_one = rms_scale(x_rows)
    normed = (x_rows * scale_one * gain_one).astype(jnp.bfloat16)
    queries = rotate(
        matmul(normed, wq_full).reshape(seq_dev, local_len, HEADS, HEAD_DIM), cosine, sine_table
    ).astype(jnp.bfloat16)
    keys_local = rotate(
        matmul(normed, wk_full).reshape(seq_dev, local_len, KV_HEADS, HEAD_DIM), cosine, sine_table
    ).astype(jnp.bfloat16)
    values_local = matmul(normed, wv_full).astype(jnp.bfloat16)
    keys_all, values_all = (
        lax.all_gather(keys_local.reshape(seq_dev, local_len, kv_width), "ctx", axis=1, tiled=True),
        lax.all_gather(
            values_local.reshape(seq_dev, local_len, kv_width), "ctx", axis=1, tiled=True
        ),
    )
    query_heads = queries.reshape(seq_dev, local_len, KV_HEADS, groups, HEAD_DIM).transpose(
        2, 0, 1, 3, 4
    )
    key_heads = keys_all.reshape(seq_dev, full_len, KV_HEADS, HEAD_DIM).transpose(2, 0, 1, 3)
    value_heads = values_all.reshape(seq_dev, full_len, KV_HEADS, HEAD_DIM).transpose(2, 0, 1, 3)

    def scores_of(query_head, key_head):
        raw_scores = (
            jnp.einsum("sqjd,skd->sjqk", query_head, key_head, preferred_element_type=jnp.float32)
            * score_scale
        )
        return jnp.where(allowed[:, None], raw_scores, masked_value)

    def attend_head(pieces):
        query_head, key_head, value_head = pieces
        scores = scores_of(query_head, key_head)
        row_max = jnp.max(scores, axis=-1, keepdims=True)
        exponent = jnp.exp(scores - row_max)
        row_total = jnp.sum(exponent, axis=-1, keepdims=True)
        probabilities = (exponent / row_total).astype(jnp.bfloat16)
        mixed_head = jnp.einsum(
            "sjqk,skd->sqjd", probabilities, value_head, preferred_element_type=jnp.float32
        )
        return (mixed_head, row_max[..., 0] + jnp.log(row_total[..., 0]))

    mixed_heads, log_totals = lax.map(attend_head, (query_heads, key_heads, value_heads))
    mixed_low = (
        mixed_heads.transpose(1, 2, 0, 3, 4).reshape(row_count, model_width).astype(jnp.bfloat16)
    )
    hidden = x_rows + matmul(mixed_low, wo_full)
    scale_two = rms_scale(hidden)
    gain_two, wg_full, wu_full, wd_full = (
        lax.all_gather(mlp_gain, "shard", axis=0, tiled=True),
        lax.all_gather(w_gate, "shard", axis=0, tiled=True),
        lax.all_gather(w_up, "shard", axis=0, tiled=True),
        lax.all_gather(w_down, "shard", axis=0, tiled=True),
    )
    normed_two = (hidden * scale_two * gain_two).astype(jnp.bfloat16)
    gate_pre = matmul(normed_two, wg_full)
    up_pre = matmul(normed_two, wu_full)
    sigmoid_gate = jax.nn.sigmoid(gate_pre)
    activated = gate_pre * sigmoid_gate
    product = (activated * up_pre).astype(jnp.bfloat16)
    layer_out = (hidden + matmul(product, wd_full)).astype(jnp.bfloat16).reshape(tokens.shape)
    grad_out = cotangent.reshape(row_count, model_width)
    gain_two_back, wg_back, wu_back, wd_back = (
        lax.all_gather(mlp_gain, "shard", axis=0, tiled=True),
        lax.all_gather(w_gate, "shard", axis=0, tiled=True),
        lax.all_gather(w_up, "shard", axis=0, tiled=True),
        lax.all_gather(w_down, "shard", axis=0, tiled=True),
    )
    grad_product = matmul(grad_out, wd_back.T)
    grad_w_down = matmul(product.T, grad_out)
    grad_gate = (
        grad_product * up_pre * sigmoid_gate * (1.0 + gate_pre * (1.0 - sigmoid_gate))
    ).astype(jnp.bfloat16)
    grad_up = (grad_product * activated).astype(jnp.bfloat16)
    grad_w_gate = matmul(normed_two.T, grad_gate)
    grad_w_up = matmul(normed_two.T, grad_up)
    grad_normed_two = matmul(grad_gate, wg_back.T) + matmul(grad_up, wu_back.T)
    gain_two_f = gain_two_back.astype(jnp.float32)
    grad_mlp_gain = jnp.sum(grad_normed_two * hidden * scale_two, axis=0)
    grad_hidden = grad_out.astype(jnp.float32) + norm_back(
        grad_normed_two, hidden, scale_two, gain_two_f
    )
    gain_one_back, wq_back, wk_back, wv_back, wo_back = (
        lax.all_gather(attn_gain, "shard", axis=0, tiled=True),
        lax.all_gather(w_query, "shard", axis=0, tiled=True),
        lax.all_gather(w_key, "shard", axis=0, tiled=True),
        lax.all_gather(w_value, "shard", axis=0, tiled=True),
        lax.all_gather(w_out, "shard", axis=0, tiled=True),
    )
    grad_attended = grad_hidden.astype(jnp.bfloat16)
    grad_w_out = matmul(mixed_low.T, grad_attended)
    grad_mixed = matmul(grad_attended, wo_back.T).astype(jnp.bfloat16)
    grad_heads = grad_mixed.reshape(seq_dev, local_len, KV_HEADS, groups, HEAD_DIM).transpose(
        2, 0, 1, 3, 4
    )

    def attend_back(pieces):
        query_head, key_head, value_head, grad_head, log_total = pieces
        scores = scores_of(query_head, key_head)
        probabilities = jnp.exp(scores - log_total[..., None])
        grad_probs = jnp.einsum(
            "sqjd,skd->sjqk", grad_head, value_head, preferred_element_type=jnp.float32
        )
        inner_sum = jnp.sum(probabilities * grad_probs, axis=-1, keepdims=True)
        grad_scores = (probabilities * (grad_probs - inner_sum)).astype(jnp.bfloat16)
        grad_query = (
            jnp.einsum("sjqk,skd->sqjd", grad_scores, key_head, preferred_element_type=jnp.float32)
            * score_scale
        )
        grad_key = (
            jnp.einsum(
                "sjqk,sqjd->skd", grad_scores, query_head, preferred_element_type=jnp.float32
            )
            * score_scale
        )
        grad_value = jnp.einsum(
            "sjqk,sqjd->skd",
            probabilities.astype(jnp.bfloat16),
            grad_head,
            preferred_element_type=jnp.float32,
        )
        return (grad_query, grad_key, grad_value)

    grad_queries, key_terms, value_terms = lax.map(
        attend_back, (query_heads, key_heads, value_heads, grad_heads, log_totals)
    )
    key_terms = key_terms.transpose(1, 2, 0, 3).reshape(seq_dev, full_len, kv_width)
    value_terms = value_terms.transpose(1, 2, 0, 3).reshape(seq_dev, full_len, kv_width)
    grad_keys, grad_values = (
        lax.psum_scatter(
            key_terms.astype(jnp.bfloat16), "ctx", scatter_dimension=1, tiled=True
        ).astype(jnp.float32),
        lax.psum_scatter(
            value_terms.astype(jnp.bfloat16), "ctx", scatter_dimension=1, tiled=True
        ).astype(jnp.float32),
    )
    grad_queries = grad_queries.transpose(1, 2, 0, 3, 4).reshape(
        seq_dev, local_len, HEADS, HEAD_DIM
    )
    grad_q_low = (
        rotate(grad_queries, cosine, -sine_table)
        .reshape(row_count, model_width)
        .astype(jnp.bfloat16)
    )
    grad_k_low = (
        rotate(grad_keys.reshape(seq_dev, local_len, KV_HEADS, HEAD_DIM), cosine, -sine_table)
        .reshape(row_count, kv_width)
        .astype(jnp.bfloat16)
    )
    grad_v_low = grad_values.reshape(row_count, kv_width).astype(jnp.bfloat16)
    grad_w_query = matmul(normed.T, grad_q_low)
    grad_w_key = matmul(normed.T, grad_k_low)
    grad_w_value = matmul(normed.T, grad_v_low)
    grad_normed = (
        matmul(grad_q_low, wq_back.T)
        + matmul(grad_k_low, wk_back.T)
        + matmul(grad_v_low, wv_back.T)
    )
    gain_one_f = gain_one_back.astype(jnp.float32)
    grad_attn_gain = jnp.sum(grad_normed * x_rows * scale_one, axis=0)
    grad_tokens = (grad_hidden + norm_back(grad_normed, x_rows, scale_one, gain_one_f)).astype(
        jnp.bfloat16
    )
    grad_tokens = grad_tokens.reshape(tokens.shape)
    part_gain_two, part_gate, part_up, part_down = (
        lax.psum_scatter(
            grad_mlp_gain.astype(jnp.bfloat16), "shard", scatter_dimension=0, tiled=True
        ).astype(jnp.float32),
        lax.psum_scatter(
            grad_w_gate.astype(jnp.bfloat16), "shard", scatter_dimension=0, tiled=True
        ).astype(jnp.float32),
        lax.psum_scatter(
            grad_w_up.astype(jnp.bfloat16), "shard", scatter_dimension=0, tiled=True
        ).astype(jnp.float32),
        lax.psum_scatter(
            grad_w_down.astype(jnp.bfloat16), "shard", scatter_dimension=0, tiled=True
        ).astype(jnp.float32),
    )
    part_gain_one, part_query, part_key, part_value, part_out = (
        lax.psum_scatter(
            grad_attn_gain.astype(jnp.bfloat16), "shard", scatter_dimension=0, tiled=True
        ).astype(jnp.float32),
        lax.psum_scatter(
            grad_w_query.astype(jnp.bfloat16), "shard", scatter_dimension=0, tiled=True
        ).astype(jnp.float32),
        lax.psum_scatter(
            grad_w_key.astype(jnp.bfloat16), "shard", scatter_dimension=0, tiled=True
        ).astype(jnp.float32),
        lax.psum_scatter(
            grad_w_value.astype(jnp.bfloat16), "shard", scatter_dimension=0, tiled=True
        ).astype(jnp.float32),
        lax.psum_scatter(
            grad_w_out.astype(jnp.bfloat16), "shard", scatter_dimension=0, tiled=True
        ).astype(jnp.float32),
    )
    summed = (
        lax.psum(part_gain_one.astype(jnp.bfloat16), ("ctx", "batch")).astype(jnp.float32),
        lax.psum(part_query.astype(jnp.bfloat16), ("ctx", "batch")).astype(jnp.float32),
        lax.psum(part_key.astype(jnp.bfloat16), ("ctx", "batch")).astype(jnp.float32),
        lax.psum(part_value.astype(jnp.bfloat16), ("ctx", "batch")).astype(jnp.float32),
        lax.psum(part_out.astype(jnp.bfloat16), ("ctx", "batch")).astype(jnp.float32),
        lax.psum(part_gain_two.astype(jnp.bfloat16), ("ctx", "batch")).astype(jnp.float32),
        lax.psum(part_gate.astype(jnp.bfloat16), ("ctx", "batch")).astype(jnp.float32),
        lax.psum(part_up.astype(jnp.bfloat16), ("ctx", "batch")).astype(jnp.float32),
        lax.psum(part_down.astype(jnp.bfloat16), ("ctx", "batch")).astype(jnp.float32),
    )
    return (
        layer_out,
        grad_tokens,
        summed[0],
        summed[1],
        summed[2],
        summed[3],
        summed[4],
        summed[5],
        summed[6],
        summed[7],
        summed[8],
    )


def fits(mesh):
    split = mesh.shape["ctx"] // 2
    return split == 2 and mesh.shape["batch"] == 2 and mesh.shape["shard"] * split == KV_HEADS and mesh.shape["shard"] == 4


def solution(mesh):
    in_specs = (
        P(("shard", "batch"), "ctx", None),
        P(("shard", "batch"), None),
        P(("shard", "batch"), "ctx"),
        P("shard"),
        P("shard", None),
        P("shard", None),
        P("shard", None),
        P("shard", None),
        P("shard"),
        P("shard", None),
        P("shard", None),
        P("shard", None),
        P(("shard", "batch"), "ctx", None),
    )
    out_specs = (
        P(("shard", "batch"), "ctx", None),
        P(("shard", "batch"), "ctx", None),
        P("shard"),
        P("shard", None),
        P("shard", None),
        P("shard", None),
        P("shard", None),
        P("shard"),
        P("shard", None),
        P("shard", None),
        P("shard", None),
    )
    layer = chip_layer if fits(mesh) else general_layer
    return jax.shard_map(layer, mesh=mesh, in_specs=in_specs, out_specs=out_specs, check_vma=False)
```
